32 devices in a mesh: rows: 32 (over z, y, x, core).
Axes of the slice: x: 2, y: 2, z: 4, core: 2. Of those that a mesh axis runs over, the one named last changes fastest.
Arguments:
- covariates: float32 [65536, 128], P('rows'), may hold values from -6 to 6
- outcome: float32 [65536], P('rows'), may hold values from 0 to 3
- predictor: float32 [65536], P('rows'), may hold values from -1.5 to 1.5
- firm_id: int32 [65536], P('rows'), may hold values from 0 to 127
- dy_id: int32 [65536], P('rows'), may hold values from 0 to 2047
- pd_owner: int32 [65536, 1], P('rows'), may hold values from 0 to 31; in each aligned block of 2048 rows (0 to 2047, 2048 to 4095, ...) at most 128 rows name the same one
- pd_local: int32 [65536], P('rows'), may hold values from 0 to 15
Outputs:
- x_tilde: float32 [65536, 128], P('rows')
- z_tilde: float32 [65536], P('rows')
- gram: float32 [128, 128], P('rows')
- rhs: float32 [128], P('rows')
The draws below stay inside these ranges and needn't reach their ends.
Inputs may be any that keep to these rules, and one draw needn't show every extreme that they name: `pd_owner`: among the rows of one device no owner is named more than 128 times, a bound that some block reaches.
All inputs are finite; a program needn't handle non-finite values.
Results may differ from the reference program's by a relative error of at most 0.0003.
Values sent between devices are 32-bit elements; how exact they have to be, the bound alone decides.
No kernel may reach another device: no remote copies, remote signals or barrier semaphores. Data moves between devices by JAX's collectives and lax.ppermute only.
A program may use at most 64 MiB of HBM per device.

```python
import math
import jax
import jax.numpy as jnp
import numpy as np
from jax import lax

K = 128
DY = 2048
ROWS_DEV = 2048
FIRM_DEV = 128
PD_DEV = 16
CAP = 128
ROWS = 65536
N_ROWS = 32


def place_ends(values, own_key, smallest, top_value):
    longest = values.shape.index(max(values.shape))
    spots = []
    for shift in (0, 1):
        where = [jax.random.randint(jax.random.fold_in(own_key, axis), (), 0, length) for axis, length in enumerate(values.shape)]
        where[longest] = (where[longest] + shift) % values.shape[longest]
        spots.append(tuple(where))
    return values.at[spots[0]].set(smallest).at[spots[1]].set(top_value)


def strengthened(drawn, own_key, source, target, shards_of, factor):
    def block_of(axis_at):
        return (jnp.arange(drawn.shape[axis_at]) // (drawn.shape[axis_at] // shards_of)).reshape((-1,) + (1,) * (drawn.ndim - 1 - axis_at))

    near = jax.random.permutation(own_key, shards_of)[block_of(target)]
    other_side = (block_of(target) + shards_of // 2) % shards_of
    return jnp.where((block_of(source) == near) | (block_of(source) == other_side), factor * drawn, drawn)


def levels(rng, shape, cuts, least, top_value):
    level = 1.0
    for dim, parts in cuts:
        heights = jax.random.uniform(jax.random.fold_in(jax.random.fold_in(rng, 6), dim), (parts,), jnp.float32, least / len(cuts), top_value / len(cuts))
        level = level * jnp.repeat(jnp.exp(heights), shape[dim] // parts).reshape((-1,) + (1,) * (len(shape) - 1 - dim))
    return level


def rank_table(count, slope):
    portions = [(1 << 20) // math.isqrt(rank ** slope) + 1 for rank in range(1, count + 1)]
    deviation = 1 + sum(portions) // (1 << 30)
    return np.cumsum(np.array([max(1, weight // deviation) for weight in portions]))


def ranked_ids(stream_key, shape, amount, lean):
    listing = rank_table(amount, lean)
    lot = jax.random.randint(jax.random.fold_in(stream_key, 1), shape, 0, int(listing[amount - 1]))
    standing = jnp.searchsorted(jnp.asarray(listing, jnp.int32), lot, side="right")
    return jax.random.permutation(jax.random.fold_in(stream_key, 2), amount)[standing].astype(jnp.int32)


def assign_block(rng, own, number, rows, number_of, top, most, slope):
    order = jax.random.permutation(rng, number_of)
    heavy_load, common = portions_of(number_of, rows * top, most, slope, True), portions_of(number_of, rows * top, most, slope, False)
    places = jnp.arange(number_of)

    def named(sizes, turn):
        used = int((sizes > 0).sum())
        fixed = max(1, used // 4)
        shifted = fixed + (places - fixed + turn * (used - fixed)) % max(1, number_of - fixed)
        return jnp.zeros((number_of,), jnp.int32).at[order[jnp.where(places < fixed, places, shifted)]].set(jnp.asarray(sizes, jnp.int32))

    sizes = jnp.where(number % 4 == 0, named(heavy_load, number // 4), named(common, number - number // 4 - 1))
    mixed = jax.random.permutation(jax.random.fold_in(own, 3), number_of)
    giver, sink = mixed[0:number_of // 2 * 2:2], mixed[1:number_of // 2 * 2:2]
    room = jnp.minimum(sizes[giver] - 1, most - sizes[sink]) // 2
    room = jnp.where((giver == order[0]) | (sink == order[0]) | (sizes[sink] == 0), 0, jnp.maximum(room, 0))
    shifted = jax.random.randint(jax.random.fold_in(own, 4), (number_of // 2,), 0, 1 << 20) % (room + 1)
    sizes = sizes.at[giver].add(-shifted).at[sink].add(shifted)
    items = jnp.searchsorted(jnp.cumsum(sizes), jnp.arange(rows * top), side="right").astype(jnp.int32)
    listing = items.reshape(top, rows).T
    listing = listing[jax.random.permutation(jax.random.fold_in(own, 1), rows)]
    turn = jax.random.randint(jax.random.fold_in(own, 2), (rows, 1), 0, top)
    return jnp.take_along_axis(listing, (jnp.arange(top)[None, :] + turn) % top, axis=1)


def portions_of(amount, total, bound, lean, full):
    weights = [(1 << 20) // math.isqrt(rank ** lean) + 1 for rank in range(1, amount + 1)]
    largest = bound if full else min(bound, max(-(-total // amount), total * weights[0] // sum(weights)))
    least = 1 if total - largest >= amount - 1 else 0
    given, rest = [largest] + [least] * (amount - 1), total - largest - least * (amount - 1)
    while rest > 0:
        candidates = [i for i in range(1, amount) if given[i] < largest] or [i for i in range(1, amount) if given[i] < bound]
        pool, left = sum([weights[i] for i in candidates]), rest
        for i in candidates:
            addition = min(bound - given[i], max(1, left * weights[i] // pool), rest)
            given[i] = given[i] + addition
            rest = rest - addition
    return np.array(given)


def heavy_noise(rng, shape, deviation, reach, pieces, heavy, held_as=jnp.bfloat16):
    result = deviation * jax.random.normal(rng, shape, jnp.float32)
    if pieces:
        result = result * levels(rng, shape, pieces, -0.22, 0.18)
    return jnp.clip(strengthened(result, jax.random.fold_in(rng, 3), *heavy), -reach, reach).astype(held_as)


def setup_inputs(seed: int = 0) -> dict:
    key_of = jax.random.split(jax.random.key(seed), 8)
    covariates = heavy_noise(key_of[0], (ROWS, K), 1.0, 6.0, ((0, 32),), (0, 1, 32, 2.75), jnp.float32)
    outcome = jnp.clip(3.0 * jax.random.uniform(key_of[1], (ROWS,), jnp.float32) ** levels(key_of[1], (ROWS,), ((0, 32),), -0.2, 0.2), 0.0, 3.0)
    predictor = jnp.clip(jax.random.uniform(key_of[2], (ROWS,), jnp.float32, -1.5, 1.5) * levels(key_of[2], (ROWS,), ((0, 32),), -0.4, 0.0), -1.5, 1.5)
    firm_id = place_ends(jax.random.randint(key_of[3], (ROWS,), 0, FIRM_DEV), jax.random.fold_in(key_of[3], 1), 0, FIRM_DEV - 1).astype(jnp.int32)
    dy_id = place_ends(ranked_ids(key_of[4], (ROWS,), DY, 1), jax.random.fold_in(key_of[4], 3), 0, DY - 1).astype(jnp.int32)
    pd_owner_keys = jax.random.split(jax.random.fold_in(key_of[5], 1), ROWS // ROWS_DEV)
    pd_owner_turns = jax.random.permutation(jax.random.fold_in(key_of[5], 3), ROWS // ROWS_DEV)
    pd_owner = jax.vmap(lambda own, number: assign_block(jax.random.fold_in(key_of[5], 2), own, number, ROWS_DEV, N_ROWS, 1, CAP, 2))(pd_owner_keys, pd_owner_turns).reshape((ROWS, 1))
    pd_local = place_ends(ranked_ids(key_of[6], (ROWS,), PD_DEV, 2), jax.random.fold_in(key_of[6], 3), 0, PD_DEV - 1).astype(jnp.int32)
    return dict(covariates=covariates, outcome=outcome, predictor=predictor, firm_id=firm_id, dy_id=dy_id, pd_owner=pd_owner, pd_local=pd_local)


def center(values, weight, groups, segments):
    sum_w = jax.ops.segment_sum(weight, groups, num_segments=segments)
    sum_v = jax.ops.segment_sum(weight[:, None] * values, groups, num_segments=segments)
    denominator = jnp.where(sum_w > 0.0, sum_w, jnp.float32(1.0))
    mean_v = sum_v / denominator[:, None]
    return values - mean_v[groups]


def reference(covariates, outcome, predictor, firm_id, dy_id, pd_owner, pd_local):
    weight = jnp.exp(predictor)
    working = predictor + outcome / weight - 1.0
    shard_of = (jnp.arange(ROWS, dtype=jnp.int32) // ROWS_DEV).astype(jnp.int32)
    firm = (shard_of * FIRM_DEV + firm_id).astype(jnp.int32)
    effect = (pd_owner[:, 0] * PD_DEV + pd_local).astype(jnp.int32)
    values = jnp.concatenate([covariates, working[:, None]], axis=1)
    values = center(values, weight, firm, N_ROWS * FIRM_DEV)
    values = center(values, weight, dy_id, DY)
    values = center(values, weight, effect, N_ROWS * PD_DEV)
    x_tilde = values[:, :K]
    z_tilde = values[:, K]
    scaled = weight[:, None] * x_tilde
    gram = jnp.dot(scaled.T, x_tilde, precision=lax.Precision.HIGHEST) / ROWS
    rhs = jnp.dot(scaled.T, z_tilde, precision=lax.Precision.HIGHEST) / ROWS
    return x_tilde, z_tilde, gram, rhs
```

```python
import functools
import math

import jax
import jax.numpy as jnp
from jax import lax
from jax.experimental import pallas as pl
from jax.experimental.pallas import tpu as pltpu
from jax.sharding import PartitionSpec as P

DY = 2048
FIRM_DEV = 128
PD_DEV = 16
LANES = 128
TILE = 8
VMEM_LIMIT = 48 * 1024 * 1024

BF16 = jnp.bfloat16
F32 = jnp.float32
I32 = jnp.int32


def iota(shape, dim):
    return lax.broadcasted_iota(I32, shape, dim)


def dot(a, b):
    return jnp.dot(a, b, preferred_element_type=F32)


def dot_exact(a, b):
    return jnp.dot(a, b, precision=lax.Precision.HIGHEST, preferred_element_type=F32)


def onehot(mask):
    return jnp.where(mask, 1.0, 0.0).astype(BF16)


def pieces(value, count):
    parts = []
    for _ in range(count):
        part = value.astype(BF16)
        parts.append(part)
        value = value - part.astype(F32)
    return parts


def pair(value):
    return jnp.concatenate(pieces(value, 2), axis=1)


def unpair(value):
    return value[:, :LANES] + value[:, LANES:]


def row_block(a):
    return slice(a * LANES, (a + 1) * LANES)


def weights_of(predictor, outcome):
    weight = jnp.exp(predictor)
    return weight, predictor + outcome / weight - 1.0


def scatter_half(ids, ids_t, weight, working, pairs_ref, base, blocks, width, out_ref, sums_ref):
    rows = ids.shape[0] * LANES
    count = blocks * width
    step = math.gcd(count, 256)
    for first in range(0, count, step):
        labels = iota((step, LANES), 0) + (base + first)
        table = jnp.concatenate(
            [onehot(labels == ids[a : a + 1, :]) for a in range(rows // LANES)], axis=1
        )
        sums = unpair(dot(table, pairs_ref[...]))
        out_ref[first // width : (first + step) // width, :width, :] = sums.reshape(
            step // width, width, LANES
        )
    block = lax.div(ids, I32(width))
    place = lax.rem(ids_t, I32(width))
    labels = iota((blocks, LANES), 0) + lax.div(base, I32(width))
    parts = pieces(weight, 3) + pieces(weight * working, 3)
    left = []
    for a in range(rows // LANES):
        mask = labels == block[a : a + 1, :]
        left.append(
            jnp.concatenate(
                [jnp.where(mask, part[a : a + 1, :].astype(F32), 0.0) for part in parts], axis=0
            ).astype(BF16)
        )
    right = jnp.concatenate(
        [onehot(iota((LANES, LANES), 1) == place[:, a : a + 1]) for a in range(rows // LANES)], axis=0
    )
    sums = dot(jnp.concatenate(left, axis=1), right)
    sums = [sums[i * blocks : (i + 1) * blocks, :] for i in range(6)]
    sum_w = sums[0] + sums[1] + sums[2]
    sum_z = sums[3] + sums[4] + sums[5]
    sum_z = pltpu.roll(sum_z, width, 1)
    out_ref[:, width, :] = jnp.where(iota((blocks, LANES), 1) < width, sum_w, sum_z)


def gather_half(ids, ids_t, means_ref, base, blocks, width, x_of, z, step=256):
    rows = ids.shape[0] * LANES
    count = blocks * width
    table = pair(means_ref[:, :width, :].reshape(count, LANES))
    x_new = []
    for a in range(rows // LANES):
        labels = iota((LANES, count), 1) + base
        picked = unpair(dot(onehot(labels == ids_t[:, a : a + 1]), table))
        x_new.append(x_of(a) - picked)
    mean_z = pltpu.roll(means_ref[:, width, :], LANES - width, 1)
    parts = jnp.concatenate([part.astype(F32) for part in pieces(mean_z, 3)], axis=0)
    left = jnp.transpose(parts)[:width, :].astype(BF16)
    block = lax.div(ids, I32(width)) - lax.div(base, I32(width))
    place = lax.rem(ids, I32(width))
    z_new = []
    for a in range(rows // LANES):
        mask = onehot(iota((blocks, LANES), 0) == block[a : a + 1, :])
        candidates = dot(left, jnp.concatenate([mask, mask, mask], axis=0))
        chosen = jnp.where(iota((width, LANES), 0) == place[a : a + 1, :], candidates, 0.0)
        z_new.append(z[a : a + 1, :] - jnp.sum(chosen, axis=0, keepdims=True))
    return x_new, jnp.concatenate(z_new, axis=0)


def firm_kernel(
    blocks, width, base_ref, x_ref, outcome_ref, predictor_ref, firm_ref, dy_ref,
    x1_ref, z1_ref, pairs_ref, out_ref,
):
    count = firm_ref.shape[0]
    firm = firm_ref[...]
    weight, working = weights_of(predictor_ref[...], outcome_ref[...])
    weight_t = jnp.transpose(weight)
    firm_t = jnp.transpose(firm)
    for a in range(count):
        pairs_ref[row_block(a), :] = pair(x_ref[row_block(a), :] * weight_t[:, a : a + 1])
    masks = [iota((FIRM_DEV, LANES), 0) == firm[a : a + 1, :] for a in range(count)]
    table = jnp.concatenate([onehot(mask) for mask in masks], axis=1)
    sum_x = unpair(dot(table, pairs_ref[...]))
    spread_w = jnp.zeros((FIRM_DEV, LANES), F32)
    spread_z = jnp.zeros((FIRM_DEV, LANES), F32)
    weighted = weight * working
    for a in range(count):
        spread_w += jnp.where(masks[a], weight[a : a + 1, :], 0.0)
        spread_z += jnp.where(masks[a], weighted[a : a + 1, :], 0.0)
    sum_w = jnp.sum(spread_w, axis=1, keepdims=True)
    sum_z = jnp.sum(spread_z, axis=1, keepdims=True)
    denominator = jnp.where(sum_w > 0.0, sum_w, 1.0)
    mean_x = pair(sum_x / denominator)
    mean_z = sum_z / denominator
    z1 = []
    for a in range(count):
        selector = onehot(iota((LANES, FIRM_DEV), 1) == firm_t[:, a : a + 1])
        x1 = x_ref[row_block(a), :] - unpair(dot(selector, mean_x))
        x1_ref[row_block(a), :] = x1
        pairs_ref[row_block(a), :] = pair(x1 * weight_t[:, a : a + 1])
        picked = jnp.sum(jnp.where(masks[a], mean_z, 0.0), axis=0, keepdims=True)
        z1.append(working[a : a + 1, :] - picked)
    z1 = jnp.concatenate(z1, axis=0)
    z1_ref[...] = z1
    dy = dy_ref[...]
    scatter_half(dy, jnp.transpose(dy), weight, z1, pairs_ref, base_ref[0], blocks, width, out_ref, None)


def sums_kernel(blocks, width, base_ref, pairs_ref, z1_ref, predictor_ref, dy_ref, out_ref):
    dy = dy_ref[...]
    weight = jnp.exp(predictor_ref[...])
    scatter_half(dy, jnp.transpose(dy), weight, z1_ref[...], pairs_ref, base_ref[0], blocks, width, out_ref, None)


def means_of(total, width):
    line = total[width : width + 1, :]
    diagonal = iota((width, LANES), 0) == iota((width, LANES), 1)
    sum_w = jnp.sum(jnp.where(diagonal, line, 0.0), axis=1, keepdims=True)
    mean_x = total[:width, :] / jnp.where(sum_w > 0.0, sum_w, 1.0)
    lane = iota((1, LANES), 1)
    divisor = pltpu.roll(jnp.where(lane < width, line, 1.0), width, 1)
    divisor = jnp.where(divisor > 0.0, divisor, 1.0)
    in_z = (lane >= width) & (lane < 2 * width)
    return mean_x, jnp.where(in_z, line / divisor, line)


def means_kernel(width, in_ref, out_ref):
    blocks, height = in_ref.shape[0], in_ref.shape[1]
    total = in_ref[0]
    for j in range(1, blocks):
        total = total + in_ref[j]
    mean_x, line = means_of(total, width)
    rest = jnp.zeros((height - width - 1, LANES), F32)
    result = jnp.concatenate([mean_x, line, rest], axis=0)
    for j in range(blocks):
        out_ref[j] = result


def gather_kernel(blocks, width, base_ref, x_ref, z_ref, means_ref, dy_ref, x_out, z_out):
    dy = dy_ref[...]
    x_new, z_new = gather_half(
        dy, jnp.transpose(dy), means_ref, base_ref[0], blocks, width, lambda a: x_ref[row_block(a), :], z_ref[...]
    )
    for a, value in enumerate(x_new):
        x_out[row_block(a), :] = value
    z_out[...] = z_new


def effect_kernel(
    blocks, width, pd_width, share, base_ref, x_ref, z_ref, means_ref, dy_ref, predictor_ref, owner_ref, local_ref,
    x2_ref, z2_ref, keep_ref, send_ref, weighted_ref, plain_ref,
):
    dy = dy_ref[...]
    weight = jnp.exp(predictor_ref[...])
    weight_t = jnp.transpose(weight)
    x_new, z2 = gather_half(
        dy, jnp.transpose(dy), means_ref, base_ref[0], blocks, width, lambda a: x_ref[row_block(a), :], z_ref[...]
    )
    for a, value in enumerate(x_new):
        x2_ref[row_block(a), :] = value
        plain_ref[row_block(a), :] = pair(value)
        weighted_ref[row_block(a), :] = pair(value * weight_t[:, a : a + 1])
    z2_ref[...] = z2
    effect = owner_ref[...] * PD_DEV + local_ref[...]
    effect_t = jnp.transpose(effect)
    for index, out_ref in ((1, keep_ref), (2, send_ref)):
        scatter_half(effect, effect_t, weight, z2, weighted_ref, base_ref[index], blocks, pd_width, out_ref, None)
    gram = lax.dot_general(
        weighted_ref[...], plain_ref[...], (((0,), (0,)), ((), ())), preferred_element_type=F32
    )
    gram = unpair(gram[:LANES, :] + gram[LANES:, :])
    left = [part.astype(F32) for part in pieces(weight * z2, 3)]
    rhs = jnp.zeros((TILE, 2 * LANES), F32)
    for a in range(dy.shape[0]):
        rows = jnp.concatenate([part[a : a + 1, :] for part in left] + [jnp.zeros((TILE - 3, LANES), F32)], axis=0)
        rhs += dot(rows.astype(BF16), plain_ref[row_block(a), :])
    rhs = unpair(jnp.sum(rhs, axis=0, keepdims=True))
    core = base_ref[3]
    spare = jnp.zeros((keep_ref.shape[1] - pd_width - 2 - share, LANES), F32)
    for j in range(blocks):
        even = gram[2 * j * share : (2 * j + 1) * share, :]
        odd = gram[(2 * j + 1) * share : (2 * j + 2) * share, :]
        keep_ref[j, pd_width + 1 :, :] = jnp.concatenate([jnp.where(core == 0, even, odd), rhs, spare], axis=0)
        send_ref[j, pd_width + 1 :, :] = jnp.concatenate([jnp.where(core == 0, odd, even), rhs, spare], axis=0)


def final_means_kernel(width, in_ref, out_ref, total_ref):
    blocks, height = in_ref.shape[0], in_ref.shape[1]
    total = in_ref[0]
    for j in range(1, blocks):
        total = total + in_ref[j]
    mean_x, line = means_of(total, width)
    rest = jnp.zeros((height - width - 1, LANES), F32)
    result = jnp.concatenate([mean_x, line, rest], axis=0)
    for j in range(blocks):
        out_ref[j] = result
    total_ref[...] = total


def last_kernel(
    blocks, width, share, total_rows, base_ref, x_ref, z_ref, own_ref, other_ref, total_ref, owner_ref, local_ref,
    x_out, z_out, gram_out, rhs_out,
):
    effect = owner_ref[...] * PD_DEV + local_ref[...]
    effect_t = jnp.transpose(effect)
    x_new, z_new = gather_half(
        effect, effect_t, own_ref, base_ref[1], blocks, width, lambda a: x_ref[row_block(a), :], z_ref[...]
    )
    x_new, z_new = gather_half(
        effect, effect_t, other_ref, base_ref[2], blocks, width, lambda a: x_new[a], z_new
    )
    for a, value in enumerate(x_new):
        x_out[row_block(a), :] = value
    z_out[...] = z_new
    first = base_ref[4]
    pick = jnp.where(iota((TILE, LANES), 1) == iota((TILE, LANES), 0) + first, 1.0, 0.0)
    gram_less = jnp.zeros((TILE, LANES), F32)
    rhs_less = jnp.zeros((1, LANES), F32)
    for ref in (own_ref, other_ref):
        mean_x = ref[:, :width, :]
        line = ref[:, width, :][:, None, :]
        lane = iota((blocks, width, LANES), 2)
        place = iota((blocks, width, LANES), 1)
        sum_w = jnp.sum(jnp.where(lane == place, line, 0.0), axis=2, keepdims=True)
        mean_z = jnp.sum(jnp.where(lane == place + width, line, 0.0), axis=2, keepdims=True)
        sum_x = (sum_w * mean_x).reshape(blocks * width, LANES)
        mean_x = mean_x.reshape(blocks * width, LANES)
        mean_z = mean_z.reshape(blocks * width, 1)
        columns = lax.dot_general(
            pick, sum_x, (((1,), (1,)), ((), ())), precision=lax.Precision.HIGHEST, preferred_element_type=F32
        )
        gram_less += dot_exact(columns, mean_x)
        rhs_less += jnp.sum(sum_x * mean_z, axis=0, keepdims=True)
    total = total_ref[...]
    scale = 1.0 / total_rows
    gram_out[...] = (total[width + 1 : width + 1 + share, :] - gram_less[:share, :]) * scale
    rhs = (total[width + 1 + share : width + 2 + share, :] - rhs_less) * scale
    rhs_out[...] = pltpu.roll(rhs, LANES - first, 1)[:, :share]


def call(kernel, outs, args, scratch=(), flops=0):
    size = sum(math.prod(v.shape) * v.dtype.itemsize for v in list(args) + list(outs))
    specs = [pl.BlockSpec(memory_space=pltpu.VMEM)] * len(args)
    if args[0].ndim == 1:
        specs[0] = pl.BlockSpec(memory_space=pltpu.SMEM)
    return pl.pallas_call(
        kernel,
        out_shape=tuple(outs),
        in_specs=specs,
        out_specs=tuple(pl.BlockSpec(memory_space=pltpu.VMEM) for _ in outs),
        scratch_shapes=scratch,
        cost_estimate=pl.CostEstimate(flops=flops, bytes_accessed=size, transcendentals=0),
        compiler_params=pltpu.CompilerParams(vmem_limit_bytes=VMEM_LIMIT),
    )(*args)


def shaped(*shape, dtype=F32):
    return jax.ShapeDtypeStruct(shape, dtype)


def shards(covariates, outcome, predictor, firm_id, dy_id, pd_owner, pd_local):
    rows, width = covariates.shape
    devices = lax.axis_size("rows")
    blocks = devices // 2
    share = width // devices
    total_rows = rows * devices
    dy_width, pd_width = DY // devices, PD_DEV
    dy_high, pd_high = dy_width + TILE, pd_width + TILE
    lines = rows // LANES
    me = lax.axis_index("rows")
    core = lax.rem(me, 2)
    groups = [[core_of + 2 * chip for chip in range(blocks)] for core_of in range(2)]
    partner = [(i, i ^ 1) for i in range(devices)]
    outcome, predictor, firm, dy, owner, local = (
        v.reshape(lines, LANES) for v in (outcome, predictor, firm_id, dy_id, pd_owner, pd_local)
    )
    dy_half, pd_half = blocks * dy_width, blocks * pd_width
    zero = jnp.zeros((), I32)

    def table(*values):
        return jnp.stack([jnp.asarray(v, I32) for v in values])

    keep_base = table(core * dy_half)
    send_base = table((1 - core) * dy_half)
    pd_base = table((1 - core) * dy_half, core * pd_half, (1 - core) * pd_half, core, me * share)

    def exchange(v):
        return lax.ppermute(v, "rows", partner)

    def across(v):
        return lax.all_to_all(v, "rows", 0, 0, axis_index_groups=groups)

    wide = 4 * rows * LANES
    x1, z1, pairs, send = call(
        functools.partial(firm_kernel, blocks, dy_width),
        (
            shaped(rows, width),
            shaped(lines, LANES),
            shaped(rows, 2 * LANES, dtype=BF16),
            shaped(blocks, dy_high, LANES),
        ),
        (send_base, covariates, outcome, predictor, firm, dy),
        flops=wide * (dy_half + 2 * FIRM_DEV),
    )
    got = exchange(send)
    (keep,) = call(
        functools.partial(sums_kernel, blocks, dy_width),
        (shaped(blocks, dy_high, LANES),),
        (keep_base, pairs, z1, predictor, dy),
        flops=wide * dy_half,
    )
    sums = across(keep + got)
    (means,) = call(
        functools.partial(means_kernel, dy_width),
        (shaped(blocks, dy_high, LANES),),
        (sums,),
    )
    means = across(means)
    other = exchange(means)
    x1, z1 = call(
        functools.partial(gather_kernel, blocks, dy_width),
        (shaped(rows, width), shaped(lines, LANES)),
        (keep_base, x1, z1, means, dy),
        flops=wide * dy_half,
    )
    x2, z2, keep, send = call(
        functools.partial(effect_kernel, blocks, dy_width, pd_width, share),
        (
            shaped(rows, width),
            shaped(lines, LANES),
            shaped(blocks, pd_high, LANES),
            shaped(blocks, pd_high, LANES),
        ),
        (pd_base, x1, z1, other, dy, predictor, owner, local),
        scratch=(pltpu.VMEM((rows, 2 * LANES), BF16), pltpu.VMEM((rows, 2 * LANES), BF16)),
        flops=wide * (dy_half + 2 * pd_half + 2 * LANES),
    )
    sums = across(keep + exchange(send))
    means, total = call(
        functools.partial(final_means_kernel, pd_width),
        (shaped(blocks, pd_high, LANES), shaped(pd_high, LANES)),
        (sums,),
    )
    means = across(means)
    other = exchange(means)
    x3, z3, gram, rhs = call(
        functools.partial(last_kernel, blocks, pd_width, share, total_rows),
        (shaped(rows, width), shaped(lines, LANES), shaped(share, LANES), shaped(1, share)),
        (pd_base, x2, z2, means, other, total, owner, local),
        flops=wide * 2 * pd_half,
    )
    return x3, z3.reshape(rows), gram, rhs.reshape(share)


def solution(mesh):
    in_specs = (
        P("rows", None),
        P("rows"),
        P("rows"),
        P("rows"),
        P("rows"),
        P("rows", None),
        P("rows"),
    )
    out_specs = (P("rows", None), P("rows"), P("rows", None), P("rows"))
    return jax.shard_map(shards, mesh=mesh, in_specs=in_specs, out_specs=out_specs, check_vma=False)
```

```python
import functools
import math

import jax
import jax.numpy as jnp
from jax import lax
from jax.experimental import pallas as pl
from jax.experimental.pallas import tpu as pltpu
from jax.sharding import PartitionSpec as P

DY = 2048
FIRM_DEV = 128
PD_DEV = 16
LANES = 128
TILE = 8
VMEM_LIMIT = 48 * 1024 * 1024

BF16 = jnp.bfloat16
F32 = jnp.float32
I32 = jnp.int32


def iota(shape, dim):
    return lax.broadcasted_iota(I32, shape, dim)


def dot(a, b):
    return jnp.dot(a, b, preferred_element_type=F32)


def dot_exact(a, b):
    return jnp.dot(a, b, precision=lax.Precision.HIGHEST, preferred_element_type=F32)


def onehot(mask):
    return jnp.where(mask, 1.0, 0.0).astype(BF16)


def pieces(value, count):
    parts = []
    for _ in range(count):
        part = value.astype(BF16)
        parts.append(part)
        value = value - part.astype(F32)
    return parts


def pair(value):
    return jnp.concatenate(pieces(value, 2), axis=1)


def unpair(value):
    return value[:, :LANES] + value[:, LANES:]


def row_block(a):
    return slice(a * LANES, (a + 1) * LANES)


def weights_of(predictor, outcome):
    weight = jnp.exp(predictor)
    return weight, predictor + outcome / weight - 1.0


def scatter_half(ids, ids_t, weight, working, pairs_ref, base, blocks, width, out_ref):
    lines = ids.shape[0]
    count = blocks * width
    step = math.gcd(count, 256)
    for first in range(0, count, step):
        labels = iota((step, LANES), 0) + (base + first)
        table = jnp.concatenate([onehot(labels == ids[a : a + 1, :]) for a in range(lines)], axis=1)
        sums = unpair(dot(table, pairs_ref[...]))
        out_ref[first // width : (first + step) // width, :width, :] = sums.reshape(
            step // width, width, LANES
        )
    block = lax.div(ids, I32(width))
    place = lax.rem(ids_t, I32(width))
    labels = iota((blocks, LANES), 0) + lax.div(base, I32(width))
    parts = [part.astype(F32) for part in pieces(weight, 3) + pieces(weight * working, 3)]
    left = []
    for a in range(lines):
        mask = labels == block[a : a + 1, :]
        left.append(jnp.concatenate([jnp.where(mask, part[a : a + 1, :], 0.0) for part in parts], axis=0))
    left = jnp.concatenate(left, axis=1).astype(BF16)
    right = jnp.concatenate(
        [onehot(iota((LANES, LANES), 1) == place[:, a : a + 1]) for a in range(lines)], axis=0
    )
    sums = dot(left, right)
    sums = [sums[i * blocks : (i + 1) * blocks, :] for i in range(6)]
    out_ref[:, width, :] = sums[0] + sums[1] + sums[2]
    out_ref[:, width + 1, :] = sums[3] + sums[4] + sums[5]
    spare = out_ref.shape[1] - width - 2
    if spare:
        out_ref[:, width + 2 :, :] = jnp.zeros((blocks, spare, LANES), F32)


def gather_half(ids, ids_t, means_ref, base, blocks, width, x_of, z):
    lines = ids.shape[0]
    count = blocks * width
    table = pair(means_ref[:, :width, :].reshape(count, LANES))
    x_new = []
    for a in range(lines):
        labels = iota((LANES, count), 1) + base
        picked = unpair(dot(onehot(labels == ids_t[:, a : a + 1]), table))
        x_new.append(x_of(a) - picked)
    parts = jnp.concatenate([part.astype(F32) for part in pieces(means_ref[:, width + 1, :], 3)], axis=0)
    left = jnp.transpose(parts)[:width, :].astype(BF16)
    block = lax.div(ids, I32(width)) - lax.div(base, I32(width))
    place = lax.rem(ids, I32(width))
    z_new = []
    for a in range(lines):
        mask = onehot(iota((blocks, LANES), 0) == block[a : a + 1, :])
        candidates = dot(left, jnp.concatenate([mask, mask, mask], axis=0))
        chosen = jnp.where(iota((width, LANES), 0) == place[a : a + 1, :], candidates, 0.0)
        z_new.append(z[a : a + 1, :] - jnp.sum(chosen, axis=0, keepdims=True))
    return x_new, jnp.concatenate(z_new, axis=0)


def firm_kernel(
    blocks, width, base_ref, x_hbm, outcome_hbm, predictor_hbm, firm_hbm, dy_hbm,
    x1_ref, z1_ref, pairs_ref, out_ref, x_ref, outcome_ref, predictor_ref, firm_ref, dy_ref, sems,
):
    small = [(firm_hbm, firm_ref), (predictor_hbm, predictor_ref), (outcome_hbm, outcome_ref), (dy_hbm, dy_ref)]
    copies = [pltpu.make_async_copy(src, dst, sems.at[i]) for i, (src, dst) in enumerate(small)]
    count = firm_ref.shape[0]
    chunk = max(1, count // 4)
    starts = list(range(0, count, chunk))
    for i, a in enumerate(starts):
        span = slice(a * LANES, (a + chunk) * LANES)
        copies.append(pltpu.make_async_copy(x_hbm.at[span, :], x_ref.at[span, :], sems.at[len(small) + i]))
    for copy in copies:
        copy.start()
    for copy in copies[: len(small)]:
        copy.wait()
    firm = firm_ref[...]
    weight, working = weights_of(predictor_ref[...], outcome_ref[...])
    weight_t = jnp.transpose(weight)
    firm_t = jnp.transpose(firm)
    masks = [iota((FIRM_DEV, LANES), 0) == firm[a : a + 1, :] for a in range(count)]
    spread_w = jnp.zeros((FIRM_DEV, LANES), F32)
    spread_z = jnp.zeros((FIRM_DEV, LANES), F32)
    weighted = weight * working
    for a in range(count):
        spread_w += jnp.where(masks[a], weight[a : a + 1, :], 0.0)
        spread_z += jnp.where(masks[a], weighted[a : a + 1, :], 0.0)
    sum_w = jnp.sum(spread_w, axis=1, keepdims=True)
    sum_z = jnp.sum(spread_z, axis=1, keepdims=True)
    denominator = jnp.where(sum_w > 0.0, sum_w, 1.0)
    mean_z = sum_z / denominator
    table = jnp.concatenate([onehot(mask) for mask in masks], axis=1)
    for i, a in enumerate(starts):
        copies[len(small) + i].wait()
        for b in range(a, a + chunk):
            pairs_ref[row_block(b), :] = pair(x_ref[row_block(b), :] * weight_t[:, b : b + 1])
    mean_x = pair(unpair(dot(table, pairs_ref[...])) / denominator)
    z1 = []
    for a in range(count):
        selector = onehot(iota((LANES, FIRM_DEV), 1) == firm_t[:, a : a + 1])
        x1 = x_ref[row_block(a), :] - unpair(dot(selector, mean_x))
        x1_ref[row_block(a), :] = x1
        pairs_ref[row_block(a), :] = pair(x1 * weight_t[:, a : a + 1])
        picked = jnp.sum(jnp.where(masks[a], mean_z, 0.0), axis=0, keepdims=True)
        z1.append(working[a : a + 1, :] - picked)
    z1 = jnp.concatenate(z1, axis=0)
    z1_ref[...] = z1
    dy = dy_ref[...]
    scatter_half(dy, jnp.transpose(dy), weight, z1, pairs_ref, base_ref[0], blocks, width, out_ref)


def sums_kernel(blocks, width, base_ref, pairs_ref, z1_ref, predictor_ref, dy_ref, out_ref):
    dy = dy_ref[...]
    weight = jnp.exp(predictor_ref[...])
    scatter_half(dy, jnp.transpose(dy), weight, z1_ref[...], pairs_ref, base_ref[0], blocks, width, out_ref)


def total_kernel(in_ref, out_ref):
    total = in_ref[0]
    for j in range(1, in_ref.shape[0]):
        total = total + in_ref[j]
    out_ref[...] = total


def means_kernel(width, mine_ref, got_ref, out_ref, *rest_ref):
    total = mine_ref[...] + got_ref[...]
    line_w = total[width : width + 1, :]
    line_z = total[width + 1 : width + 2, :]
    diagonal = iota((width, LANES), 0) == iota((width, LANES), 1)
    sum_w = jnp.sum(jnp.where(diagonal, line_w, 0.0), axis=1, keepdims=True)
    mean_x = total[:width, :] / jnp.where(sum_w > 0.0, sum_w, 1.0)
    mean_z = line_z / jnp.where(line_w > 0.0, line_w, 1.0)
    height = out_ref.shape[1]
    rest = jnp.zeros((height - width - 2, LANES), F32)
    result = jnp.concatenate([mean_x, line_w, mean_z, rest], axis=0)
    for j in range(out_ref.shape[0]):
        out_ref[j] = result
    if rest_ref:
        rest_ref[0][...] = total[height:, :]


def gather_kernel(blocks, width, base_ref, x_ref, z_ref, means_ref, dy_ref, x_out, z_out):
    dy = dy_ref[...]
    x_new, z_new = gather_half(
        dy, jnp.transpose(dy), means_ref, base_ref[0], blocks, width, lambda a: x_ref[row_block(a), :], z_ref[...]
    )
    for a, value in enumerate(x_new):
        x_out[row_block(a), :] = value
    z_out[...] = z_new


def effect_kernel(
    blocks, width, pd_width, base_ref, x_ref, z_ref, means_ref, dy_ref, predictor_ref, owner_ref, local_ref,
    x2_ref, z2_ref, weighted_ref, send_ref,
):
    dy = dy_ref[...]
    weight = jnp.exp(predictor_ref[...])
    weight_t = jnp.transpose(weight)
    x_new, z2 = gather_half(
        dy, jnp.transpose(dy), means_ref, base_ref[0], blocks, width, lambda a: x_ref[row_block(a), :], z_ref[...]
    )
    for a, value in enumerate(x_new):
        x2_ref[row_block(a), :] = value
        weighted_ref[row_block(a), :] = pair(value * weight_t[:, a : a + 1])
    z2_ref[...] = z2
    effect = owner_ref[...] * PD_DEV + local_ref[...]
    scatter_half(
        effect, jnp.transpose(effect), weight, z2, weighted_ref, base_ref[2], blocks, pd_width, send_ref
    )


def gram_kernel(
    blocks, pd_width, share, base_ref, x2_ref, z2_ref, weighted_ref, predictor_ref, owner_ref, local_ref,
    keep_ref, gram_ref, plain_ref,
):
    weight = jnp.exp(predictor_ref[...])
    z2 = z2_ref[...]
    lines = z2.shape[0]
    effect = owner_ref[...] * PD_DEV + local_ref[...]
    scatter_half(
        effect, jnp.transpose(effect), weight, z2, weighted_ref, base_ref[1], blocks, pd_width, keep_ref
    )
    for a in range(lines):
        plain_ref[row_block(a), :] = pair(x2_ref[row_block(a), :])
    gram = lax.dot_general(
        weighted_ref[...], plain_ref[...], (((0,), (0,)), ((), ())), preferred_element_type=F32
    )
    gram = unpair(gram[:LANES, :] + gram[LANES:, :])
    left = [part.astype(F32) for part in pieces(weight * z2, 3)]
    none = jnp.zeros((TILE - 3, LANES), F32)
    left = jnp.concatenate(
        [jnp.concatenate([part[a : a + 1, :] for part in left] + [none], axis=0) for a in range(lines)], axis=1
    )
    rhs = unpair(jnp.sum(dot(left.astype(BF16), plain_ref[...]), axis=0, keepdims=True))
    spare = jnp.zeros((gram_ref.shape[1] - 4 * share - 1, LANES), F32)
    half = blocks * 2 * share
    for j in range(blocks):
        low = gram[2 * j * share : 2 * (j + 1) * share, :]
        high = gram[half + 2 * j * share : half + 2 * (j + 1) * share, :]
        gram_ref[j] = jnp.concatenate([low, high, rhs, spare], axis=0)


def last_kernel(
    blocks, width, share, total_rows, base_ref, x_ref, z_ref, own_ref, other_ref, mine_ref, got_ref, owner_ref,
    local_ref, x_hbm, z_out, gram_out, rhs_out, x_out, sems,
):
    effect = owner_ref[...] * PD_DEV + local_ref[...]
    effect_t = jnp.transpose(effect)
    x_new, z_new = gather_half(
        effect, effect_t, own_ref, base_ref[1], blocks, width, lambda a: x_ref[row_block(a), :], z_ref[...]
    )
    x_new, z_new = gather_half(
        effect, effect_t, other_ref, base_ref[2], blocks, width, lambda a: x_new[a], z_new
    )
    copies = []
    count = len(x_new)
    chunk = max(1, count // 4)
    for a, value in enumerate(x_new):
        x_out[row_block(a), :] = value
        if a % chunk == chunk - 1:
            span = slice((a + 1 - chunk) * LANES, (a + 1) * LANES)
            copies.append(pltpu.make_async_copy(x_out.at[span, :], x_hbm.at[span, :], sems.at[a // chunk]))
            copies[-1].start()
    z_out[...] = z_new
    me, core, high = base_ref[4], base_ref[3], base_ref[5]
    first = me * share
    pick = jnp.where(iota((TILE, LANES), 1) == iota((TILE, LANES), 0) + first, 1.0, 0.0)
    gram_less = jnp.zeros((TILE, LANES), F32)
    rhs_less = jnp.zeros((1, LANES), F32)
    for ref in (own_ref, other_ref):
        mean_x = ref[:, :width, :]
        diagonal = iota((blocks, width, LANES), 2) == iota((blocks, width, LANES), 1)
        sum_w = jnp.sum(jnp.where(diagonal, ref[:, width, :][:, None, :], 0.0), axis=2, keepdims=True)
        mean_z = jnp.sum(jnp.where(diagonal, ref[:, width + 1, :][:, None, :], 0.0), axis=2, keepdims=True)
        sum_x = (sum_w * mean_x).reshape(blocks * width, LANES)
        mean_x = mean_x.reshape(blocks * width, LANES)
        mean_z = mean_z.reshape(blocks * width, 1)
        columns = lax.dot_general(
            pick, sum_x, (((1,), (1,)), ((), ())), precision=lax.Precision.HIGHEST, preferred_element_type=F32
        )
        gram_less += dot_exact(columns, mean_x)
        rhs_less += jnp.sum(sum_x * mean_z, axis=0, keepdims=True)
    total = mine_ref[...] + got_ref[...]
    gram = jnp.zeros((share, LANES), F32)
    for place in range(4):
        here = (high == place // 2) & (core == place % 2)
        gram = jnp.where(here, total[place * share : (place + 1) * share, :], gram)
    scale = 1.0 / total_rows
    gram_out[...] = (gram - gram_less[:share, :]) * scale
    rhs = (total[4 * share : 4 * share + 1, :] - rhs_less) * scale
    rhs_out[...] = pltpu.roll(rhs, LANES - first, 1)[:, :share]
    for copy in copies:
        copy.wait()


VMEM = pl.BlockSpec(memory_space=pltpu.VMEM)
SMEM = pl.BlockSpec(memory_space=pltpu.SMEM)
HBM = pl.BlockSpec(memory_space=pltpu.HBM)


def call(kernel, outs, args, scratch=(), flops=0, in_specs=None, out_specs=None):
    size = sum(math.prod(v.shape) * v.dtype.itemsize for v in list(args) + list(outs))
    return pl.pallas_call(
        kernel,
        out_shape=tuple(outs),
        in_specs=in_specs or [SMEM if v.ndim == 1 else VMEM for v in args],
        out_specs=tuple(out_specs or [VMEM] * len(outs)),
        scratch_shapes=scratch,
        cost_estimate=pl.CostEstimate(flops=flops, bytes_accessed=size, transcendentals=0),
        compiler_params=pltpu.CompilerParams(vmem_limit_bytes=VMEM_LIMIT),
    )(*args)


def shaped(*shape, dtype=F32):
    return jax.ShapeDtypeStruct(shape, dtype)


def rounded(rows):
    return -(-rows // TILE) * TILE


def shards(covariates, outcome, predictor, firm_id, dy_id, pd_owner, pd_local):
    rows, width = covariates.shape
    devices = lax.axis_size("rows")
    blocks = devices // 4
    share = width // devices
    total_rows = rows * devices
    dy_width, pd_width = DY // (2 * blocks), devices * PD_DEV // (2 * blocks)
    dy_high, pd_high = rounded(dy_width + 2), rounded(pd_width + 2)
    gram_high = rounded(4 * share + 1)
    lines = rows // LANES
    me = lax.axis_index("rows")
    core = lax.rem(me, 2)
    high = lax.div(me, devices // 2)
    groups = [
        [half * (devices // 2) + core_of + 2 * chip for chip in range(blocks)]
        for half in range(2)
        for core_of in range(2)
    ]
    partner = [(i, i ^ 1) for i in range(devices)]
    opposite = [(i, (i + devices // 2) % devices) for i in range(devices)]
    outcome, predictor, firm, dy, owner, local = (
        v.reshape(lines, LANES) for v in (outcome, predictor, firm_id, dy_id, pd_owner, pd_local)
    )
    dy_half, pd_half = blocks * dy_width, blocks * pd_width

    def table(*values):
        return jnp.stack([jnp.asarray(v, I32) for v in values])

    keep_base = table(core * dy_half)
    send_base = table((1 - core) * dy_half)
    pd_base = table((1 - core) * dy_half, core * pd_half, (1 - core) * pd_half, core, me, high)

    def to_core(v):
        return lax.ppermute(v, "rows", partner)

    def to_half(v):
        return lax.ppermute(v, "rows", opposite)

    def across(v):
        return lax.all_to_all(v, "rows", 0, 0, axis_index_groups=groups)

    def total_of(v):
        return call(total_kernel, (shaped(*v.shape[1:]),), (v,))[0]

    wide = 4 * rows * LANES
    count = min(4, lines)
    x1, z1, pairs, send = call(
        functools.partial(firm_kernel, blocks, dy_width),
        (
            shaped(rows, width),
            shaped(lines, LANES),
            shaped(rows, 2 * LANES, dtype=BF16),
            shaped(blocks, dy_high, LANES),
        ),
        (send_base, covariates, outcome, predictor, firm, dy),
        scratch=(
            pltpu.VMEM((rows, width), F32),
            pltpu.VMEM((lines, LANES), F32),
            pltpu.VMEM((lines, LANES), F32),
            pltpu.VMEM((lines, LANES), I32),
            pltpu.VMEM((lines, LANES), I32),
            pltpu.SemaphoreType.DMA((4 + count,)),
        ),
        flops=wide * (dy_half + 2 * FIRM_DEV),
        in_specs=[SMEM] + [HBM] * 5,
    )
    got = to_core(send)
    (keep,) = call(
        functools.partial(sums_kernel, blocks, dy_width),
        (shaped(blocks, dy_high, LANES),),
        (keep_base, pairs, z1, predictor, dy),
        flops=wide * dy_half,
    )
    mine = total_of(across(keep + got))
    (means,) = call(
        functools.partial(means_kernel, dy_width), (shaped(blocks, dy_high, LANES),), (mine, to_half(mine))
    )
    means = across(means)
    other = to_core(means)
    x1, z1 = call(
        functools.partial(gather_kernel, blocks, dy_width),
        (shaped(rows, width), shaped(lines, LANES)),
        (keep_base, x1, z1, means, dy),
        flops=wide * dy_half,
    )
    x2, z2, pairs, send = call(
        functools.partial(effect_kernel, blocks, dy_width, pd_width),
        (
            shaped(rows, width),
            shaped(lines, LANES),
            shaped(rows, 2 * LANES, dtype=BF16),
            shaped(blocks, pd_high, LANES),
        ),
        (pd_base, x1, z1, other, dy, predictor, owner, local),
        flops=wide * (dy_half + pd_half),
    )
    got = to_core(send)
    keep, gram = call(
        functools.partial(gram_kernel, blocks, pd_width, share),
        (shaped(blocks, pd_high, LANES), shaped(blocks, gram_high, LANES)),
        (pd_base, x2, z2, pairs, predictor, owner, local),
        scratch=(pltpu.VMEM((rows, 2 * LANES), BF16),),
        flops=wide * (pd_half + 2 * LANES),
    )
    mine = total_of(across(jnp.concatenate([keep + got, gram], axis=1)))
    means, gram = call(
        functools.partial(means_kernel, pd_width),
        (shaped(blocks, pd_high, LANES), shaped(gram_high, LANES)),
        (mine, to_half(mine)),
    )
    got = to_core(gram)
    means = across(means)
    other = to_core(means)
    x3, z3, gram, rhs = call(
        functools.partial(last_kernel, blocks, pd_width, share, total_rows),
        (shaped(rows, width), shaped(lines, LANES), shaped(share, LANES), shaped(1, share)),
        (pd_base, x2, z2, means, other, gram, got, owner, local),
        scratch=(pltpu.VMEM((rows, width), F32), pltpu.SemaphoreType.DMA((count,))),
        flops=wide * 2 * pd_half,
        out_specs=[HBM, VMEM, VMEM, VMEM],
    )
    return x3, z3.reshape(rows), gram, rhs.reshape(share)


def solution(mesh):
    in_specs = (
        P("rows", None),
        P("rows"),
        P("rows"),
        P("rows"),
        P("rows"),
        P("rows", None),
        P("rows"),
    )
    out_specs = (P("rows", None), P("rows"), P("rows", None), P("rows"))
    return jax.shard_map(shards, mesh=mesh, in_specs=in_specs, out_specs=out_specs, check_vma=False)
```

```python
import functools
import math

import jax
import jax.numpy as jnp
from jax import lax
from jax.experimental import pallas as pl
from jax.experimental.pallas import tpu as pltpu
from jax.sharding import PartitionSpec as P

DY = 2048
FIRM_DEV = 128
PD_DEV = 16
LANES = 128
TILE = 8
AXIS = "rows"
VMEM_LIMIT = 32 * 1024 * 1024

BF16 = jnp.bfloat16
F32 = jnp.float32
I32 = jnp.int32


def core_index():
    return lax.rem(lax.axis_index(AXIS), 2)


def iota(shape, dim):
    return lax.broadcasted_iota(I32, shape, dim)


def dot(a, b):
    return jnp.dot(a, b, preferred_element_type=F32)


def dot_exact(a, b):
    return jnp.dot(a, b, precision=lax.Precision.HIGHEST, preferred_element_type=F32)


def onehot(mask):
    return jnp.where(mask, 1.0, 0.0).astype(BF16)


def pieces(value, count):
    parts = []
    for _ in range(count):
        part = value.astype(BF16)
        parts.append(part)
        value = value - part.astype(F32)
    return parts


def pair(value):
    return jnp.concatenate(pieces(value, 2), axis=1)


def unpair(value):
    return value[:, :LANES] + value[:, LANES:]


def row_block(a):
    return slice(a * LANES, (a + 1) * LANES)


def weights_of(predictor, outcome):
    weight = jnp.exp(predictor)
    return weight, predictor + outcome / weight - 1.0


def scatter_half(ids, ids_t, weight, working, pairs_ref, base, blocks, width, out_ref):
    lines = ids.shape[0]
    count = blocks * width
    step = math.gcd(count, 256)
    for first in range(0, count, step):
        labels = iota((step, LANES), 0) + (base + first)
        table = jnp.concatenate([onehot(labels == ids[a : a + 1, :]) for a in range(lines)], axis=1)
        sums = unpair(dot(table, pairs_ref[...]))
        out_ref[first // width : (first + step) // width, :width, :] = sums.reshape(
            step // width, width, LANES
        )
    block = lax.div(ids, I32(width))
    place = lax.rem(ids_t, I32(width))
    labels = iota((blocks, LANES), 0) + lax.div(base, I32(width))
    parts = [part.astype(F32) for part in pieces(weight, 3) + pieces(weight * working, 3)]
    left = []
    for a in range(lines):
        mask = labels == block[a : a + 1, :]
        left.append(jnp.concatenate([jnp.where(mask, part[a : a + 1, :], 0.0) for part in parts], axis=0))
    left = jnp.concatenate(left, axis=1).astype(BF16)
    right = jnp.concatenate(
        [onehot(iota((LANES, LANES), 1) == place[:, a : a + 1]) for a in range(lines)], axis=0
    )
    sums = dot(left, right)
    sums = [sums[i * blocks : (i + 1) * blocks, :] for i in range(6)]
    out_ref[:, width, :] = sums[0] + sums[1] + sums[2]
    out_ref[:, width + 1, :] = sums[3] + sums[4] + sums[5]
    spare = out_ref.shape[1] - width - 2
    if spare:
        out_ref[:, width + 2 :, :] = jnp.zeros((blocks, spare, LANES), F32)


def gather_half(ids, ids_t, means_ref, base, blocks, width, x_of, z):
    lines = ids.shape[0]
    count = blocks * width
    table = pair(means_ref[:, :width, :].reshape(count, LANES))
    x_new = []
    for a in range(lines):
        labels = iota((LANES, count), 1) + base
        picked = unpair(dot(onehot(labels == ids_t[:, a : a + 1]), table))
        x_new.append(x_of(a) - picked)
    parts = jnp.concatenate([part.astype(F32) for part in pieces(means_ref[:, width + 1, :], 3)], axis=0)
    left = jnp.transpose(parts)[:width, :].astype(BF16)
    block = lax.div(ids, I32(width)) - lax.div(base, I32(width))
    place = lax.rem(ids, I32(width))
    z_new = []
    for a in range(lines):
        mask = onehot(iota((blocks, LANES), 0) == block[a : a + 1, :])
        candidates = dot(left, jnp.concatenate([mask, mask, mask], axis=0))
        chosen = jnp.where(iota((width, LANES), 0) == place[a : a + 1, :], candidates, 0.0)
        z_new.append(z[a : a + 1, :] - jnp.sum(chosen, axis=0, keepdims=True))
    return x_new, jnp.concatenate(z_new, axis=0)


def firm_kernel(
    blocks, width, x_hbm, outcome_hbm, predictor_hbm, firm_hbm, dy_hbm,
    x1_ref, z1_ref, weight_ref, dy_ref, pairs_ref, out_ref, x_ref, outcome_ref, predictor_ref, firm_ref, sems,
):
    small = [(firm_hbm, firm_ref), (predictor_hbm, predictor_ref), (outcome_hbm, outcome_ref), (dy_hbm, dy_ref)]
    copies = [pltpu.make_async_copy(src, dst, sems.at[i]) for i, (src, dst) in enumerate(small)]
    count = firm_ref.shape[0]
    chunk = max(1, count // 4)
    starts = list(range(0, count, chunk))
    for i, a in enumerate(starts):
        span = slice(a * LANES, (a + chunk) * LANES)
        copies.append(pltpu.make_async_copy(x_hbm.at[span, :], x_ref.at[span, :], sems.at[len(small) + i]))
    for copy in copies:
        copy.start()
    for copy in copies[: len(small)]:
        copy.wait()
    firm = firm_ref[...]
    weight, working = weights_of(predictor_ref[...], outcome_ref[...])
    weight_ref[...] = weight
    weight_t = jnp.transpose(weight)
    firm_t = jnp.transpose(firm)
    masks = [iota((FIRM_DEV, LANES), 0) == firm[a : a + 1, :] for a in range(count)]
    spread_w = jnp.zeros((FIRM_DEV, LANES), F32)
    spread_z = jnp.zeros((FIRM_DEV, LANES), F32)
    weighted = weight * working
    for a in range(count):
        spread_w += jnp.where(masks[a], weight[a : a + 1, :], 0.0)
        spread_z += jnp.where(masks[a], weighted[a : a + 1, :], 0.0)
    sum_w = jnp.sum(spread_w, axis=1, keepdims=True)
    sum_z = jnp.sum(spread_z, axis=1, keepdims=True)
    denominator = jnp.where(sum_w > 0.0, sum_w, 1.0)
    mean_z = sum_z / denominator
    table = jnp.concatenate([onehot(mask) for mask in masks], axis=1)
    for i, a in enumerate(starts):
        copies[len(small) + i].wait()
        for b in range(a, a + chunk):
            pairs_ref[row_block(b), :] = pair(x_ref[row_block(b), :] * weight_t[:, b : b + 1])
    mean_x = pair(unpair(dot(table, pairs_ref[...])) / denominator)
    z1 = []
    for a in range(count):
        selector = onehot(iota((LANES, FIRM_DEV), 1) == firm_t[:, a : a + 1])
        x1 = x_ref[row_block(a), :] - unpair(dot(selector, mean_x))
        x1_ref[row_block(a), :] = x1
        pairs_ref[row_block(a), :] = pair(x1 * weight_t[:, a : a + 1])
        picked = jnp.sum(jnp.where(masks[a], mean_z, 0.0), axis=0, keepdims=True)
        z1.append(working[a : a + 1, :] - picked)
    z1 = jnp.concatenate(z1, axis=0)
    z1_ref[...] = z1
    dy = dy_ref[...]
    scatter_half(dy, jnp.transpose(dy), weight, z1, pairs_ref, (1 - core_index()) * (blocks * width), blocks, width, out_ref)


def sums_kernel(blocks, width, pairs_ref, z1_ref, weight_ref, dy_ref, out_ref):
    dy = dy_ref[...]
    scatter_half(dy, jnp.transpose(dy), weight_ref[...], z1_ref[...], pairs_ref, core_index() * (blocks * width), blocks, width, out_ref)


def total_kernel(in_ref, out_ref):
    total = in_ref[0]
    for j in range(1, in_ref.shape[0]):
        total = total + in_ref[j]
    out_ref[...] = total


def means_kernel(width, mine_ref, got_ref, out_ref, *rest_ref):
    total = mine_ref[...] + got_ref[...]
    line_w = total[width : width + 1, :]
    line_z = total[width + 1 : width + 2, :]
    diagonal = iota((width, LANES), 0) == iota((width, LANES), 1)
    sum_w = jnp.sum(jnp.where(diagonal, line_w, 0.0), axis=1, keepdims=True)
    mean_x = total[:width, :] / jnp.where(sum_w > 0.0, sum_w, 1.0)
    mean_z = line_z / jnp.where(line_w > 0.0, line_w, 1.0)
    height = out_ref.shape[1]
    rest = jnp.zeros((height - width - 2, LANES), F32)
    result = jnp.concatenate([mean_x, line_w, mean_z, rest], axis=0)
    for j in range(out_ref.shape[0]):
        out_ref[j] = result
    if rest_ref:
        rest_ref[0][...] = total[height:, :]


def gather_kernel(blocks, width, x_ref, z_ref, means_ref, dy_ref, x_out, z_out):
    dy = dy_ref[...]
    x_new, z_new = gather_half(
        dy, jnp.transpose(dy), means_ref, core_index() * (blocks * width), blocks, width, lambda a: x_ref[row_block(a), :], z_ref[...]
    )
    for a, value in enumerate(x_new):
        x_out[row_block(a), :] = value
    z_out[...] = z_new


def effect_kernel(
    blocks, width, pd_width, x_ref, z_ref, means_ref, dy_ref, weight_ref, owner_ref, local_ref,
    x2_ref, z2_ref, weighted_ref, send_ref,
):
    dy = dy_ref[...]
    weight = weight_ref[...]
    weight_t = jnp.transpose(weight)
    x_new, z2 = gather_half(
        dy, jnp.transpose(dy), means_ref, (1 - core_index()) * (blocks * width), blocks, width, lambda a: x_ref[row_block(a), :], z_ref[...]
    )
    for a, value in enumerate(x_new):
        x2_ref[row_block(a), :] = value
        weighted_ref[row_block(a), :] = pair(value * weight_t[:, a : a + 1])
    z2_ref[...] = z2
    effect = owner_ref[...] * PD_DEV + local_ref[...]
    scatter_half(
        effect, jnp.transpose(effect), weight, z2, weighted_ref, (1 - core_index()) * (blocks * pd_width), blocks, pd_width, send_ref
    )


def gram_kernel(
    blocks, pd_width, share, x2_ref, z2_ref, weighted_ref, weight_ref, owner_ref, local_ref,
    keep_ref, gram_ref, plain_ref,
):
    weight = weight_ref[...]
    z2 = z2_ref[...]
    lines = z2.shape[0]
    effect = owner_ref[...] * PD_DEV + local_ref[...]
    scatter_half(
        effect, jnp.transpose(effect), weight, z2, weighted_ref, core_index() * (blocks * pd_width), blocks, pd_width, keep_ref
    )
    for a in range(lines):
        plain_ref[row_block(a), :] = pair(x2_ref[row_block(a), :])
    gram = lax.dot_general(
        weighted_ref[...], plain_ref[...], (((0,), (0,)), ((), ())), preferred_element_type=F32
    )
    gram = unpair(gram[:LANES, :] + gram[LANES:, :])
    left = [part.astype(F32) for part in pieces(weight * z2, 3)]
    none = jnp.zeros((TILE - 3, LANES), F32)
    left = jnp.concatenate(
        [jnp.concatenate([part[a : a + 1, :] for part in left] + [none], axis=0) for a in range(lines)], axis=1
    )
    rhs = unpair(jnp.sum(dot(left.astype(BF16), plain_ref[...]), axis=0, keepdims=True))
    spare = jnp.zeros((gram_ref.shape[1] - 4 * share - 1, LANES), F32)
    half = blocks * 2 * share
    for j in range(blocks):
        low = gram[2 * j * share : 2 * (j + 1) * share, :]
        high = gram[half + 2 * j * share : half + 2 * (j + 1) * share, :]
        gram_ref[j] = jnp.concatenate([low, high, rhs, spare], axis=0)


def gram_less(means_ref, blocks, width, first):
    mean_x = means_ref[:, :width, :]
    diagonal = iota((blocks, width, LANES), 2) == iota((blocks, width, LANES), 1)
    sum_w = jnp.sum(jnp.where(diagonal, means_ref[:, width, :][:, None, :], 0.0), axis=2, keepdims=True)
    mean_z = jnp.sum(jnp.where(diagonal, means_ref[:, width + 1, :][:, None, :], 0.0), axis=2, keepdims=True)
    sum_x = (sum_w * mean_x).reshape(blocks * width, LANES)
    pick = jnp.where(iota((TILE, LANES), 1) == iota((TILE, LANES), 0) + first, 1.0, 0.0)
    columns = lax.dot_general(
        pick, sum_x, (((1,), (1,)), ((), ())), precision=lax.Precision.HIGHEST, preferred_element_type=F32
    )
    rhs = jnp.sum(sum_x * mean_z.reshape(blocks * width, 1), axis=0, keepdims=True)
    return dot_exact(columns, mean_x.reshape(blocks * width, LANES)), rhs


def own_kernel(
    blocks, width, share, x_ref, z_ref, means_ref, owner_ref, local_ref, x_out, z_out, less_ref
):
    effect = owner_ref[...] * PD_DEV + local_ref[...]
    x_new, z_new = gather_half(
        effect, jnp.transpose(effect), means_ref, core_index() * (blocks * width), blocks, width, lambda a: x_ref[row_block(a), :],
        z_ref[...],
    )
    for a, value in enumerate(x_new):
        x_out[row_block(a), :] = value
    z_out[...] = z_new
    gram, rhs = gram_less(means_ref, blocks, width, lax.axis_index(AXIS) * share)
    less_ref[...] = jnp.concatenate([gram, rhs, jnp.zeros((TILE - 1, LANES), F32)], axis=0)


def last_kernel(
    blocks, width, share, total_rows, x_ref, z_ref, means_ref, less_ref, mine_ref, got_ref, owner_ref,
    local_ref, x_hbm, z_out, gram_out, rhs_out, x_out, sems,
):
    effect = owner_ref[...] * PD_DEV + local_ref[...]
    x_new, z_new = gather_half(
        effect, jnp.transpose(effect), means_ref, (1 - core_index()) * (blocks * width), blocks, width, lambda a: x_ref[row_block(a), :],
        z_ref[...],
    )
    copies = []
    chunk = max(1, len(x_new) // 4)
    for a, value in enumerate(x_new):
        x_out[row_block(a), :] = value
        if a % chunk == chunk - 1:
            span = slice((a + 1 - chunk) * LANES, (a + 1) * LANES)
            copies.append(pltpu.make_async_copy(x_out.at[span, :], x_hbm.at[span, :], sems.at[a // chunk]))
            copies[-1].start()
    z_out[...] = z_new
    me = lax.axis_index(AXIS)
    core, high = core_index(), lax.div(me, 2 * blocks)
    first = me * share
    gram_part, rhs_part = gram_less(means_ref, blocks, width, first)
    total = mine_ref[...] + got_ref[...]
    gram = jnp.zeros((share, LANES), F32)
    for place in range(4):
        here = (high == place // 2) & (core == place % 2)
        gram = jnp.where(here, total[place * share : (place + 1) * share, :], gram)
    scale = 1.0 / total_rows
    gram_out[...] = (gram - (gram_part[:share, :] + less_ref[:share, :])) * scale
    rhs = (total[4 * share : 4 * share + 1, :] - (rhs_part + less_ref[TILE : TILE + 1, :])) * scale
    rhs_out[...] = pltpu.roll(rhs, LANES - first, 1)[:, :share]
    for copy in copies:
        copy.wait()


VMEM = pl.BlockSpec(memory_space=pltpu.VMEM)
HBM = pl.BlockSpec(memory_space=pltpu.HBM)


def call(kernel, outs, args, scratch=(), flops=0, in_specs=None, out_specs=None):
    size = sum(math.prod(v.shape) * v.dtype.itemsize for v in list(args) + list(outs))
    return pl.pallas_call(
        kernel,
        out_shape=tuple(outs),
        in_specs=in_specs or [VMEM] * len(args),
        out_specs=tuple(out_specs or [VMEM] * len(outs)),
        scratch_shapes=scratch,
        cost_estimate=pl.CostEstimate(flops=flops, bytes_accessed=size, transcendentals=0),
        compiler_params=pltpu.CompilerParams(vmem_limit_bytes=VMEM_LIMIT),
    )(*args)


def in_hbm(v):
    return pltpu.with_memory_space_constraint(v, pltpu.HBM)


def shaped(*shape, dtype=F32):
    return jax.ShapeDtypeStruct(shape, dtype)


def rounded(rows):
    return -(-rows // TILE) * TILE


def shards(covariates, outcome, predictor, firm_id, dy_id, pd_owner, pd_local):
    rows, width = covariates.shape
    devices = lax.axis_size(AXIS)
    blocks = devices // 4
    share = width // devices
    total_rows = rows * devices
    dy_width, pd_width = DY // (2 * blocks), devices * PD_DEV // (2 * blocks)
    dy_high, pd_high = rounded(dy_width + 2), rounded(pd_width + 2)
    gram_high = rounded(4 * share + 1)
    lines = rows // LANES
    groups = [
        [half * (devices // 2) + core_of + 2 * chip for chip in range(blocks)]
        for half in range(2)
        for core_of in range(2)
    ]
    partner = [(i, i ^ 1) for i in range(devices)]
    opposite = [(i, (i + devices // 2) % devices) for i in range(devices)]
    outcome, predictor, firm, dy, owner, local = (
        v.reshape(lines, LANES) for v in (outcome, predictor, firm_id, dy_id, pd_owner, pd_local)
    )
    dy_half, pd_half = blocks * dy_width, blocks * pd_width

    def to_core(v):
        return lax.ppermute(v, AXIS, partner)

    def to_half(v):
        return lax.ppermute(v, AXIS, opposite)

    def across(v):
        return lax.all_to_all(v, AXIS, 0, 0, axis_index_groups=groups)

    def total_of(v):
        return call(total_kernel, (shaped(*v.shape[1:]),), (v,))[0]

    wide = 4 * rows * LANES
    count = min(4, lines)
    x1, z1, weight, dy, pairs, send = call(
        functools.partial(firm_kernel, blocks, dy_width),
        (
            shaped(rows, width),
            shaped(lines, LANES),
            shaped(lines, LANES),
            shaped(lines, LANES, dtype=I32),
            shaped(rows, 2 * LANES, dtype=BF16),
            shaped(blocks, dy_high, LANES),
        ),
        tuple(in_hbm(v) for v in (covariates, outcome, predictor, firm, dy)),
        scratch=(
            pltpu.VMEM((rows, width), F32),
            pltpu.VMEM((lines, LANES), F32),
            pltpu.VMEM((lines, LANES), F32),
            pltpu.VMEM((lines, LANES), I32),
            pltpu.SemaphoreType.DMA((4 + count,)),
        ),
        flops=wide * (dy_half + 2 * FIRM_DEV),
        in_specs=[HBM] * 5,
    )
    got = to_core(send)
    (keep,) = call(
        functools.partial(sums_kernel, blocks, dy_width),
        (shaped(blocks, dy_high, LANES),),
        (pairs, z1, weight, dy),
        flops=wide * dy_half,
    )
    mine = total_of(across(keep + got))
    (means,) = call(
        functools.partial(means_kernel, dy_width), (shaped(blocks, dy_high, LANES),), (mine, to_half(mine))
    )
    means = across(means)
    other = to_core(means)
    x1, z1 = call(
        functools.partial(gather_kernel, blocks, dy_width),
        (shaped(rows, width), shaped(lines, LANES)),
        (x1, z1, means, dy),
        flops=wide * dy_half,
    )
    x2, z2, pairs, send = call(
        functools.partial(effect_kernel, blocks, dy_width, pd_width),
        (
            shaped(rows, width),
            shaped(lines, LANES),
            shaped(rows, 2 * LANES, dtype=BF16),
            shaped(blocks, pd_high, LANES),
        ),
        (x1, z1, other, dy, weight, owner, local),
        flops=wide * (dy_half + pd_half),
    )
    got = to_core(send)
    keep, gram = call(
        functools.partial(gram_kernel, blocks, pd_width, share),
        (shaped(blocks, pd_high, LANES), shaped(blocks, gram_high, LANES)),
        (x2, z2, pairs, weight, owner, local),
        scratch=(pltpu.VMEM((rows, 2 * LANES), BF16),),
        flops=wide * (pd_half + 2 * LANES),
    )
    mine = total_of(across(jnp.concatenate([keep + got, gram], axis=1)))
    means, gram = call(
        functools.partial(means_kernel, pd_width),
        (shaped(blocks, pd_high, LANES), shaped(gram_high, LANES)),
        (mine, to_half(mine)),
    )
    got = to_core(gram)
    means = across(means)
    other = to_core(means)
    x3, z3, less = call(
        functools.partial(own_kernel, blocks, pd_width, share),
        (shaped(rows, width), shaped(lines, LANES), shaped(2 * TILE, LANES)),
        (x2, z2, means, owner, local),
        flops=wide * pd_half,
    )
    x3, z3, gram, rhs = call(
        functools.partial(last_kernel, blocks, pd_width, share, total_rows),
        (shaped(rows, width), shaped(lines, LANES), shaped(share, LANES), shaped(1, share)),
        (x3, z3, other, less, gram, got, owner, local),
        scratch=(pltpu.VMEM((rows, width), F32), pltpu.SemaphoreType.DMA((count,))),
        flops=wide * pd_half,
        out_specs=[HBM, VMEM, VMEM, VMEM],
    )
    return x3, z3.reshape(rows), gram, rhs.reshape(share)


def solution(mesh):
    in_specs = (
        P("rows", None),
        P("rows"),
        P("rows"),
        P("rows"),
        P("rows"),
        P("rows", None),
        P("rows"),
    )
    out_specs = (P("rows", None), P("rows"), P("rows", None), P("rows"))
    return jax.shard_map(shards, mesh=mesh, in_specs=in_specs, out_specs=out_specs, check_vma=False)
```

```python
import functools
import math

import jax
import jax.numpy as jnp
from jax import lax
from jax.experimental import pallas as pl
from jax.experimental.pallas import tpu as pltpu
from jax.sharding import PartitionSpec as P

DY = 2048
FIRM_DEV = 128
PD_DEV = 16
LANES = 128
TILE = 8
AXIS = "rows"
VMEM_LIMIT = 32 * 1024 * 1024

BF16 = jnp.bfloat16
F32 = jnp.float32
I32 = jnp.int32


def core_index():
    return lax.rem(lax.axis_index(AXIS), 2)


def iota(shape, dim):
    return lax.broadcasted_iota(I32, shape, dim)


def dot(a, b):
    return jnp.dot(a, b, preferred_element_type=F32)


def dot_first(a, b):
    return lax.dot_general(a, b, (((0,), (0,)), ((), ())), preferred_element_type=F32)


def onehot(mask):
    return jnp.where(mask, 1.0, 0.0).astype(BF16)


def pieces(value, count):
    parts = []
    for _ in range(count):
        part = value.astype(BF16)
        parts.append(part)
        value = value - part.astype(F32)
    return parts


def pair(value):
    return jnp.concatenate(pieces(value, 2), axis=1)


def unpair(value):
    return value[:, :LANES] + value[:, LANES:]


def row_block(a):
    return slice(a * LANES, (a + 1) * LANES)


def weights_of(predictor, outcome):
    weight = jnp.exp(predictor)
    return weight, predictor + outcome / weight - 1.0


def scatter_half(ids, weight, working, pairs_ref, base, blocks, width, out_ref, group=16):
    lines = ids.shape[0]
    count = blocks * width
    step = math.gcd(count, 256)
    for first in range(0, count, step):
        labels = iota((step, LANES), 0) + (base + first)
        table = jnp.concatenate([onehot(labels == ids[a : a + 1, :]) for a in range(lines)], axis=1)
        sums = unpair(dot(table, pairs_ref[...]))
        out_ref[first // width : (first + step) // width, :width, :] = sums.reshape(
            step // width, width, LANES
        )
    block = lax.div(ids, I32(width))
    place = lax.rem(ids, I32(width))
    labels = iota((blocks, LANES), 0) + lax.div(base, I32(width))
    parts = [part.astype(F32) for part in pieces(weight, 3) + pieces(weight * working, 3)]
    sums = jnp.zeros((6 * blocks, width), F32)
    for a in range(0, lines, group):
        left, right = [], []
        for b in range(a, min(a + group, lines)):
            mask = labels == block[b : b + 1, :]
            left.append(jnp.concatenate([jnp.where(mask, part[b : b + 1, :], 0.0) for part in parts], axis=0))
            right.append(onehot(iota((width, LANES), 0) == place[b : b + 1, :]))
        left = jnp.concatenate(left, axis=1).astype(BF16)
        right = jnp.concatenate(right, axis=1)
        sums += lax.dot_general(left, right, (((1,), (1,)), ((), ())), preferred_element_type=F32)
    sums = [sums[i * blocks : (i + 1) * blocks, :] for i in range(6)]
    out_ref[:, width, :width] = sums[0] + sums[1] + sums[2]
    out_ref[:, width + 1, :width] = sums[3] + sums[4] + sums[5]
    spare = out_ref.shape[1] - width - 2
    if spare:
        out_ref[:, width + 2 :, :] = jnp.zeros((blocks, spare, LANES), F32)


def gather_half(ids, means_ref, base, blocks, width, z, emit):
    lines = ids.shape[0]
    count = blocks * width
    group = math.gcd(lines, 4)
    parts = jnp.concatenate([part.astype(F32) for part in pieces(means_ref[:, width + 1, :], 3)], axis=0)
    left = jnp.transpose(parts)[:width, :].astype(BF16)
    block = lax.div(ids, I32(width)) - lax.div(base, I32(width))
    place = lax.rem(ids, I32(width))
    table = pair(means_ref[:, :width, :].reshape(count, LANES))
    labels = iota((count, LANES), 0) + base
    z_new = []
    for a in range(0, lines, group):
        for b in range(a, a + group):
            mask = onehot(iota((blocks, LANES), 0) == block[b : b + 1, :])
            candidates = dot(left, jnp.concatenate([mask, mask, mask], axis=0))
            chosen = jnp.where(iota((width, LANES), 0) == place[b : b + 1, :], candidates, 0.0)
            z_new.append(z[b : b + 1, :] - jnp.sum(chosen, axis=0, keepdims=True))
        mask = jnp.concatenate([onehot(labels == ids[b : b + 1, :]) for b in range(a, a + group)], axis=1)
        picked = unpair(dot_first(mask, table))
        for b in range(group):
            emit(a + b, picked[row_block(b), :])
    return jnp.concatenate(z_new, axis=0)


def firm_kernel(
    blocks, width, x_hbm, outcome_hbm, predictor_hbm, firm_hbm, dy_hbm,
    x1_ref, z1_ref, weight_ref, dy_ref, pairs_ref, out_ref, x_ref, outcome_ref, predictor_ref, firm_ref, sems,
):
    small = [(firm_hbm, firm_ref), (predictor_hbm, predictor_ref), (outcome_hbm, outcome_ref), (dy_hbm, dy_ref)]
    copies = [pltpu.make_async_copy(src, dst, sems.at[i]) for i, (src, dst) in enumerate(small)]
    count = firm_ref.shape[0]
    chunk = max(1, count // 4)
    starts = list(range(0, count, chunk))
    for i, a in enumerate(starts):
        span = slice(a * LANES, (a + chunk) * LANES)
        copies.append(pltpu.make_async_copy(x_hbm.at[span, :], x_ref.at[span, :], sems.at[len(small) + i]))
    for copy in copies:
        copy.start()
    for copy in copies[: len(small)]:
        copy.wait()
    firm = firm_ref[...]
    weight, working = weights_of(predictor_ref[...], outcome_ref[...])
    weight_ref[...] = weight
    weight_t = jnp.transpose(weight)
    group = math.gcd(count, 4)
    masks = [iota((FIRM_DEV, LANES), 0) == firm[a : a + 1, :] for a in range(count)]
    spread_w = jnp.zeros((FIRM_DEV, LANES), F32)
    spread_z = jnp.zeros((FIRM_DEV, LANES), F32)
    weighted = weight * working
    for a in range(count):
        spread_w += jnp.where(masks[a], weight[a : a + 1, :], 0.0)
        spread_z += jnp.where(masks[a], weighted[a : a + 1, :], 0.0)
    sum_w = jnp.sum(spread_w, axis=1, keepdims=True)
    sum_z = jnp.sum(spread_z, axis=1, keepdims=True)
    denominator = jnp.where(sum_w > 0.0, sum_w, 1.0)
    mean_z = sum_z / denominator
    table = jnp.concatenate([onehot(mask) for mask in masks], axis=1)
    sum_x = jnp.zeros((FIRM_DEV, 2 * LANES), F32)
    for i, a in enumerate(starts):
        copies[len(small) + i].wait()
        span = slice(a * LANES, (a + chunk) * LANES)
        for b in range(a, a + chunk):
            pairs_ref[row_block(b), :] = pair(x_ref[row_block(b), :] * weight_t[:, b : b + 1])
        sum_x += dot(table[:, span], pairs_ref[span, :])
    mean_x = pair(unpair(sum_x) / denominator)
    z1 = []
    for a in range(count):
        if a % group == 0:
            picked = unpair(dot_first(table[:, a * LANES : (a + group) * LANES], mean_x))
        x1 = x_ref[row_block(a), :] - picked[row_block(a % group), :]
        x1_ref[row_block(a), :] = x1
        pairs_ref[row_block(a), :] = pair(x1 * weight_t[:, a : a + 1])
        picked_z = jnp.sum(jnp.where(masks[a], mean_z, 0.0), axis=0, keepdims=True)
        z1.append(working[a : a + 1, :] - picked_z)
    z1 = jnp.concatenate(z1, axis=0)
    z1_ref[...] = z1
    dy = dy_ref[...]
    scatter_half(dy, weight, z1, pairs_ref, (1 - core_index()) * (blocks * width), blocks, width, out_ref)


def sums_kernel(blocks, width, pairs_ref, z1_ref, weight_ref, dy_ref, out_ref):
    dy = dy_ref[...]
    scatter_half(dy, weight_ref[...], z1_ref[...], pairs_ref, core_index() * (blocks * width), blocks, width, out_ref)


def total_kernel(in_ref, out_ref):
    total = in_ref[0]
    for j in range(1, in_ref.shape[0]):
        total = total + in_ref[j]
    out_ref[...] = total


def means_kernel(width, mine_ref, got_ref, out_ref, *rest_ref):
    total = mine_ref[...] + got_ref[...]
    line_w = total[width : width + 1, :]
    line_z = total[width + 1 : width + 2, :]
    diagonal = iota((width, LANES), 0) == iota((width, LANES), 1)
    sum_w = jnp.sum(jnp.where(diagonal, line_w, 0.0), axis=1, keepdims=True)
    mean_x = total[:width, :] / jnp.where(sum_w > 0.0, sum_w, 1.0)
    mean_z = line_z / jnp.where(line_w > 0.0, line_w, 1.0)
    height = out_ref.shape[1]
    rest = jnp.zeros((height - width - 2, LANES), F32)
    result = jnp.concatenate([mean_x, line_w, mean_z, rest], axis=0)
    for j in range(out_ref.shape[0]):
        out_ref[j] = result
    if rest_ref:
        gram = total[height:, :]
        rest_ref[0][: gram.shape[0], :] = gram
        rest_ref[0][gram.shape[0] :, :] = total[width + 2 : width + 2 + TILE, :]


def gather_kernel(blocks, width, x_ref, z_ref, means_ref, dy_ref, x_out, z_out):
    def emit(a, picked):
        x_out[row_block(a), :] = x_ref[row_block(a), :] - picked

    base = core_index() * (blocks * width)
    z_out[...] = gather_half(dy_ref[...], means_ref, base, blocks, width, z_ref[...], emit)


def effect_kernel(
    blocks, width, pd_width, x_ref, z_ref, means_ref, dy_ref, weight_ref, owner_ref, local_ref,
    x2_ref, z2_ref, weighted_ref, send_ref,
):
    dy = dy_ref[...]
    weight = weight_ref[...]
    weight_t = jnp.transpose(weight)

    def emit(a, picked):
        x2 = x_ref[row_block(a), :] - picked
        x2_ref[row_block(a), :] = x2
        weighted_ref[row_block(a), :] = pair(x2 * weight_t[:, a : a + 1])

    z2 = gather_half(dy, means_ref, (1 - core_index()) * (blocks * width), blocks, width, z_ref[...], emit)
    z2_ref[...] = z2
    effect = owner_ref[...] * PD_DEV + local_ref[...]
    scatter_half(
        effect, weight, z2, weighted_ref, (1 - core_index()) * (blocks * pd_width), blocks, pd_width, send_ref
    )


def gram_kernel(
    blocks, pd_width, share, x2_ref, z2_ref, weighted_ref, weight_ref, owner_ref, local_ref,
    keep_ref, gram_ref, plain_ref,
):
    weight = weight_ref[...]
    z2 = z2_ref[...]
    lines = z2.shape[0]
    effect = owner_ref[...] * PD_DEV + local_ref[...]
    scatter_half(
        effect, weight, z2, weighted_ref, core_index() * (blocks * pd_width), blocks, pd_width, keep_ref
    )
    for a in range(lines):
        plain_ref[row_block(a), :] = pair(x2_ref[row_block(a), :])
    gram = dot_first(weighted_ref[...], plain_ref[...])
    gram = unpair(gram[:LANES, :] + gram[LANES:, :])
    left = [part.astype(F32) for part in pieces(weight * z2, 3)]
    none = jnp.zeros((TILE - 3, LANES), F32)
    left = jnp.concatenate(
        [jnp.concatenate([part[a : a + 1, :] for part in left] + [none], axis=0) for a in range(lines)], axis=1
    )
    rhs = unpair(jnp.sum(dot(left.astype(BF16), plain_ref[...]), axis=0, keepdims=True))
    keep_ref[:, pd_width + 2, :] = jnp.broadcast_to(rhs, (blocks, LANES))
    half = blocks * 2 * share
    for j in range(blocks):
        low = gram[2 * j * share : 2 * (j + 1) * share, :]
        high = gram[half + 2 * j * share : half + 2 * (j + 1) * share, :]
        gram_ref[j, : 4 * share, :] = jnp.concatenate([low, high], axis=0)


def gram_less(means_ref, blocks, width, first, share):
    count = blocks * width
    diagonal = iota((blocks, width, LANES), 2) == iota((blocks, width, LANES), 1)
    sum_w = jnp.sum(jnp.where(diagonal, means_ref[:, width, :][:, None, :], 0.0), axis=2, keepdims=True)
    mean_z = jnp.sum(jnp.where(diagonal, means_ref[:, width + 1, :][:, None, :], 0.0), axis=2, keepdims=True)
    mean_x = means_ref[:, :width, :].reshape(count, LANES)
    sum_x = mean_x * sum_w.reshape(count, 1)
    lane = iota((count, LANES), 1)
    rows = []
    for i in range(share):
        column = jnp.sum(jnp.where(lane == first + i, sum_x, 0.0), axis=1, keepdims=True)
        rows.append(jnp.sum(column * mean_x, axis=0, keepdims=True))
    rows.append(jnp.sum(sum_x * mean_z.reshape(count, 1), axis=0, keepdims=True))
    return jnp.concatenate(rows, axis=0)


def own_kernel(blocks, width, share, x_ref, z_ref, means_ref, owner_ref, local_ref, x_out, z_out, less_ref):
    effect = owner_ref[...] * PD_DEV + local_ref[...]

    def emit(a, picked):
        x_out[row_block(a), :] = x_ref[row_block(a), :] - picked

    z_out[...] = gather_half(effect, means_ref, core_index() * (blocks * width), blocks, width, z_ref[...], emit)
    less_ref[: share + 1, :] = gram_less(means_ref, blocks, width, lax.axis_index(AXIS) * share, share)


def last_kernel(
    blocks, width, share, total_rows, x_ref, z_ref, means_ref, less_ref, mine_ref, got_ref, owner_ref, local_ref,
    x_hbm, z_hbm, gram_hbm, rhs_hbm, x_out, z_out, gram_out, rhs_out, sems,
):
    me = lax.axis_index(AXIS)
    core, high = core_index(), lax.div(me, 2 * blocks)
    first = me * share
    copies = []
    effect = owner_ref[...] * PD_DEV + local_ref[...]
    lines = effect.shape[0]
    chunk = max(1, lines // 4)

    def emit(a, picked):
        x_out[row_block(a), :] = x_ref[row_block(a), :] - picked
        if a % chunk == chunk - 1:
            span = slice((a + 1 - chunk) * LANES, (a + 1) * LANES)
            copies.append(pltpu.make_async_copy(x_out.at[span, :], x_hbm.at[span, :], sems.at[3 + a // chunk]))
            copies[-1].start()

    z_out[...] = gather_half(effect, means_ref, (1 - core) * (blocks * width), blocks, width, z_ref[...], emit)
    copies.append(pltpu.make_async_copy(z_out, z_hbm, sems.at[2]))
    copies[-1].start()
    less = gram_less(means_ref, blocks, width, first, share) + less_ref[: share + 1, :]
    total = mine_ref[...] + got_ref[...]
    high_rows = total.shape[0] - TILE
    gram = jnp.zeros((share, LANES), F32)
    for place in range(4):
        here = (high == place // 2) & (core == place % 2)
        gram = jnp.where(here, total[place * share : (place + 1) * share, :], gram)
    scale = 1.0 / total_rows
    gram_out[...] = (gram - less[:share, :]) * scale
    rhs = (total[high_rows : high_rows + 1, :] - less[share:, :]) * scale
    rhs_out[...] = pltpu.roll(rhs, LANES - first, 1)[:, :share]
    copies.append(pltpu.make_async_copy(gram_out, gram_hbm, sems.at[0]))
    copies.append(pltpu.make_async_copy(rhs_out, rhs_hbm, sems.at[1]))
    for copy in copies[-2:]:
        copy.start()
    for copy in copies:
        copy.wait()


VMEM = pl.BlockSpec(memory_space=pltpu.VMEM)
HBM = pl.BlockSpec(memory_space=pltpu.HBM)


def call(kernel, outs, args, scratch=(), flops=0, in_specs=None, out_specs=None):
    size = sum(math.prod(v.shape) * v.dtype.itemsize for v in list(args) + list(outs))
    return pl.pallas_call(
        kernel,
        out_shape=tuple(outs),
        in_specs=in_specs or [VMEM] * len(args),
        out_specs=tuple(out_specs or [VMEM] * len(outs)),
        scratch_shapes=scratch,
        cost_estimate=pl.CostEstimate(flops=flops, bytes_accessed=size, transcendentals=0),
        compiler_params=pltpu.CompilerParams(vmem_limit_bytes=VMEM_LIMIT),
    )(*args)


def in_hbm(v):
    return pltpu.with_memory_space_constraint(v, pltpu.HBM)


def shaped(*shape, dtype=F32):
    return jax.ShapeDtypeStruct(shape, dtype)


def rounded(rows):
    return -(-rows // TILE) * TILE


def shards(covariates, outcome, predictor, firm_id, dy_id, pd_owner, pd_local):
    rows, width = covariates.shape
    devices = lax.axis_size(AXIS)
    blocks = devices // 4
    share = width // devices
    total_rows = rows * devices
    dy_width, pd_width = DY // (2 * blocks), devices * PD_DEV // (2 * blocks)
    dy_high, pd_high = rounded(dy_width + 2), rounded(pd_width + 3)
    gram_high = rounded(4 * share)
    lines = rows // LANES
    groups = [
        [half * (devices // 2) + core_of + 2 * chip for chip in range(blocks)]
        for half in range(2)
        for core_of in range(2)
    ]
    partner = [(i, i ^ 1) for i in range(devices)]
    opposite = [(i, (i + devices // 2) % devices) for i in range(devices)]
    outcome, predictor, firm, dy, owner, local = (
        v.reshape(lines, LANES) for v in (outcome, predictor, firm_id, dy_id, pd_owner, pd_local)
    )
    dy_half, pd_half = blocks * dy_width, blocks * pd_width

    def to_core(v):
        return lax.ppermute(v, AXIS, partner)

    def to_half(v):
        return lax.ppermute(v, AXIS, opposite)

    def across(v):
        return lax.all_to_all(v, AXIS, 0, 0, axis_index_groups=groups)

    def total_of(v):
        return call(total_kernel, (shaped(*v.shape[1:]),), (v,))[0]

    wide = 4 * rows * LANES
    count = min(4, lines)
    x1, z1, weight, dy, pairs, send = call(
        functools.partial(firm_kernel, blocks, dy_width),
        (
            shaped(rows, width),
            shaped(lines, LANES),
            shaped(lines, LANES),
            shaped(lines, LANES, dtype=I32),
            shaped(rows, 2 * LANES, dtype=BF16),
            shaped(blocks, dy_high, LANES),
        ),
        tuple(in_hbm(v) for v in (covariates, outcome, predictor, firm, dy)),
        scratch=(
            pltpu.VMEM((rows, width), F32),
            pltpu.VMEM((lines, LANES), F32),
            pltpu.VMEM((lines, LANES), F32),
            pltpu.VMEM((lines, LANES), I32),
            pltpu.SemaphoreType.DMA((4 + count,)),
        ),
        flops=wide * (dy_half + 2 * FIRM_DEV),
        in_specs=[HBM] * 5,
    )
    got = to_core(send)
    (keep,) = call(
        functools.partial(sums_kernel, blocks, dy_width),
        (shaped(blocks, dy_high, LANES),),
        (pairs, z1, weight, dy),
        flops=wide * dy_half,
    )
    mine = total_of(across(keep + got))
    (means,) = call(
        functools.partial(means_kernel, dy_width), (shaped(blocks, dy_high, LANES),), (mine, to_half(mine))
    )
    means = across(means)
    other = to_core(means)
    x1, z1 = call(
        functools.partial(gather_kernel, blocks, dy_width),
        (shaped(rows, width), shaped(lines, LANES)),
        (x1, z1, means, dy),
        flops=wide * dy_half,
    )
    x2, z2, pairs, send = call(
        functools.partial(effect_kernel, blocks, dy_width, pd_width),
        (
            shaped(rows, width),
            shaped(lines, LANES),
            shaped(rows, 2 * LANES, dtype=BF16),
            shaped(blocks, pd_high, LANES),
        ),
        (x1, z1, other, dy, weight, owner, local),
        flops=wide * (dy_half + pd_half),
    )
    got = to_core(send)
    keep, gram = call(
        functools.partial(gram_kernel, blocks, pd_width, share),
        (shaped(blocks, pd_high, LANES), shaped(blocks, gram_high, LANES)),
        (x2, z2, pairs, weight, owner, local),
        scratch=(pltpu.VMEM((rows, 2 * LANES), BF16),),
        flops=wide * (pd_half + 2 * LANES),
    )
    mine = total_of(across(jnp.concatenate([keep + got, gram], axis=1)))
    means, gram = call(
        functools.partial(means_kernel, pd_width),
        (shaped(blocks, pd_high, LANES), shaped(gram_high + TILE, LANES)),
        (mine, to_half(mine)),
    )
    got = to_core(gram)
    means = across(means)
    other = to_core(means)
    x3, z3, less = call(
        functools.partial(own_kernel, blocks, pd_width, share),
        (shaped(rows, width), shaped(lines, LANES), shaped(rounded(share + 1), LANES)),
        (x2, z2, means, owner, local),
        flops=wide * pd_half,
    )
    x3, z3, gram, rhs = call(
        functools.partial(last_kernel, blocks, pd_width, share, total_rows),
        (shaped(rows, width), shaped(lines, LANES), shaped(share, LANES), shaped(1, share)),
        (x3, z3, other, less, gram, got, owner, local),
        scratch=(
            pltpu.VMEM((rows, width), F32),
            pltpu.VMEM((lines, LANES), F32),
            pltpu.VMEM((share, LANES), F32),
            pltpu.VMEM((1, share), F32),
            pltpu.SemaphoreType.DMA((3 + count,)),
        ),
        flops=wide * pd_half,
        out_specs=[HBM] * 4,
    )
    return x3, z3.reshape(rows), gram, rhs.reshape(share)


def solution(mesh):
    in_specs = (
        P("rows", None),
        P("rows"),
        P("rows"),
        P("rows"),
        P("rows"),
        P("rows", None),
        P("rows"),
    )
    out_specs = (P("rows", None), P("rows"), P("rows", None), P("rows"))
    return jax.shard_map(shards, mesh=mesh, in_specs=in_specs, out_specs=out_specs, check_vma=False)
```

```python
import functools
import math

import jax
import jax.numpy as jnp
from jax import lax
from jax.experimental import pallas as pl
from jax.experimental.pallas import tpu as pltpu
from jax.sharding import PartitionSpec as P

DY = 2048
FIRM_DEV = 128
PD_DEV = 16
LANES = 128
TILE = 8
AXIS = "rows"
VMEM_LIMIT = 32 * 1024 * 1024

BF16 = jnp.bfloat16
F32 = jnp.float32
I32 = jnp.int32


def core_index():
    return lax.rem(lax.axis_index(AXIS), 2)


def iota(shape, dim):
    return lax.broadcasted_iota(I32, shape, dim)


def dot(a, b):
    return jnp.dot(a, b, preferred_element_type=F32)


def dot_first(a, b):
    return lax.dot_general(a, b, (((0,), (0,)), ((), ())), preferred_element_type=F32)


def onehot(mask):
    return jnp.where(mask, 1.0, 0.0).astype(BF16)


def pieces(value, count):
    parts = []
    for _ in range(count):
        part = value.astype(BF16)
        parts.append(part)
        value = value - part.astype(F32)
    return parts


def pair(value):
    return jnp.concatenate(pieces(value, 2), axis=1)


def unpair(value):
    return value[:, :LANES] + value[:, LANES:]


def row_block(a):
    return slice(a * LANES, (a + 1) * LANES)


def weights_of(predictor, outcome):
    weight = jnp.exp(predictor)
    return weight, predictor + outcome / weight - 1.0


def scatter_half(ids, weight, working, pairs_ref, base, blocks, width, out_ref, group=16):
    lines = ids.shape[0]
    count = blocks * width
    step = math.gcd(count, 256)
    for first in range(0, count, step):
        labels = iota((step, LANES), 0) + (base + first)
        table = jnp.concatenate([onehot(labels == ids[a : a + 1, :]) for a in range(lines)], axis=1)
        sums = unpair(dot(table, pairs_ref[...]))
        out_ref[first // width : (first + step) // width, :width, :] = sums.reshape(
            step // width, width, LANES
        )
    block = lax.div(ids, I32(width))
    place = lax.rem(ids, I32(width))
    labels = iota((blocks, LANES), 0) + lax.div(base, I32(width))
    parts = [part.astype(F32) for part in pieces(weight, 3) + pieces(weight * working, 3)]
    sums = jnp.zeros((6 * blocks, width), F32)
    for a in range(0, lines, group):
        left, right = [], []
        for b in range(a, min(a + group, lines)):
            mask = labels == block[b : b + 1, :]
            left.append(jnp.concatenate([jnp.where(mask, part[b : b + 1, :], 0.0) for part in parts], axis=0))
            right.append(onehot(iota((width, LANES), 0) == place[b : b + 1, :]))
        left = jnp.concatenate(left, axis=1).astype(BF16)
        right = jnp.concatenate(right, axis=1)
        sums += lax.dot_general(left, right, (((1,), (1,)), ((), ())), preferred_element_type=F32)
    sums = [sums[i * blocks : (i + 1) * blocks, :] for i in range(6)]
    out_ref[:, width, :width] = sums[0] + sums[1] + sums[2]
    out_ref[:, width + 1, :width] = sums[3] + sums[4] + sums[5]
    spare = out_ref.shape[1] - width - 2
    if spare:
        out_ref[:, width + 2 :, :] = jnp.zeros((blocks, spare, LANES), F32)


def gather_half(ids, means_ref, base, blocks, width, z, emit):
    lines = ids.shape[0]
    count = blocks * width
    group = math.gcd(lines, 4)
    parts = jnp.concatenate([part.astype(F32) for part in pieces(means_ref[:, width + 1, :], 3)], axis=0)
    left = jnp.transpose(parts)[:width, :].astype(BF16)
    block = lax.div(ids, I32(width)) - lax.div(base, I32(width))
    place = lax.rem(ids, I32(width))
    table = pair(means_ref[:, :width, :].reshape(count, LANES))
    labels = iota((count, LANES), 0) + base
    z_new = []
    for a in range(0, lines, group):
        for b in range(a, a + group):
            mask = onehot(iota((blocks, LANES), 0) == block[b : b + 1, :])
            candidates = dot(left, jnp.concatenate([mask, mask, mask], axis=0))
            chosen = jnp.where(iota((width, LANES), 0) == place[b : b + 1, :], candidates, 0.0)
            z_new.append(z[b : b + 1, :] - jnp.sum(chosen, axis=0, keepdims=True))
        mask = jnp.concatenate([onehot(labels == ids[b : b + 1, :]) for b in range(a, a + group)], axis=1)
        picked = unpair(dot_first(mask, table))
        for b in range(group):
            emit(a + b, picked[row_block(b), :])
    return jnp.concatenate(z_new, axis=0)


def firm_kernel(
    blocks, width, x_hbm, outcome_hbm, predictor_hbm, firm_hbm, dy_hbm,
    x1_ref, z1_ref, weight_ref, dy_ref, pairs_ref, out_ref, x_ref, outcome_ref, predictor_ref, firm_ref, sems,
):
    small = [(firm_hbm, firm_ref), (predictor_hbm, predictor_ref), (outcome_hbm, outcome_ref), (dy_hbm, dy_ref)]
    copies = [pltpu.make_async_copy(src, dst, sems.at[i]) for i, (src, dst) in enumerate(small)]
    count = firm_ref.shape[0]
    chunk = max(1, count // 4)
    starts = list(range(0, count, chunk))
    for i, a in enumerate(starts):
        span = slice(a * LANES, (a + chunk) * LANES)
        copies.append(pltpu.make_async_copy(x_hbm.at[span, :], x_ref.at[span, :], sems.at[len(small) + i]))
    for copy in copies:
        copy.start()
    for copy in copies[: len(small)]:
        copy.wait()
    firm = firm_ref[...]
    weight, working = weights_of(predictor_ref[...], outcome_ref[...])
    weight_ref[...] = weight
    weight_t = jnp.transpose(weight)
    group = math.gcd(count, 4)
    masks = [iota((FIRM_DEV, LANES), 0) == firm[a : a + 1, :] for a in range(count)]
    spread_w = jnp.zeros((FIRM_DEV, LANES), F32)
    spread_z = jnp.zeros((FIRM_DEV, LANES), F32)
    weighted = weight * working
    for a in range(count):
        spread_w += jnp.where(masks[a], weight[a : a + 1, :], 0.0)
        spread_z += jnp.where(masks[a], weighted[a : a + 1, :], 0.0)
    sum_w = jnp.sum(spread_w, axis=1, keepdims=True)
    sum_z = jnp.sum(spread_z, axis=1, keepdims=True)
    denominator = jnp.where(sum_w > 0.0, sum_w, 1.0)
    mean_z = sum_z / denominator
    table = jnp.concatenate([onehot(mask) for mask in masks], axis=1)
    sum_x = jnp.zeros((FIRM_DEV, 2 * LANES), F32)
    for i, a in enumerate(starts):
        copies[len(small) + i].wait()
        span = slice(a * LANES, (a + chunk) * LANES)
        if a == 0:
            offset = jnp.sum(x_ref[row_block(0), :], axis=0, keepdims=True) * (1.0 / LANES)
        for b in range(a, a + chunk):
            pairs_ref[row_block(b), :] = pair((x_ref[row_block(b), :] - offset) * weight_t[:, b : b + 1])
        sum_x += dot(table[:, span], pairs_ref[span, :])
    mean_x = pair(unpair(sum_x) / denominator)
    z1 = []
    for a in range(count):
        if a % group == 0:
            picked = unpair(dot_first(table[:, a * LANES : (a + group) * LANES], mean_x))
        x1 = (x_ref[row_block(a), :] - offset) - picked[row_block(a % group), :]
        x1_ref[row_block(a), :] = x1
        pairs_ref[row_block(a), :] = pair(x1 * weight_t[:, a : a + 1])
        picked_z = jnp.sum(jnp.where(masks[a], mean_z, 0.0), axis=0, keepdims=True)
        z1.append(working[a : a + 1, :] - picked_z)
    z1 = jnp.concatenate(z1, axis=0)
    z1_ref[...] = z1
    dy = dy_ref[...]
    scatter_half(dy, weight, z1, pairs_ref, (1 - core_index()) * (blocks * width), blocks, width, out_ref)


def sums_kernel(blocks, width, pairs_ref, z1_ref, weight_ref, dy_ref, out_ref):
    dy = dy_ref[...]
    scatter_half(dy, weight_ref[...], z1_ref[...], pairs_ref, core_index() * (blocks * width), blocks, width, out_ref)


def total_kernel(in_ref, out_ref):
    total = in_ref[0]
    for j in range(1, in_ref.shape[0]):
        total = total + in_ref[j]
    out_ref[...] = total


def means_kernel(width, mine_ref, got_ref, out_ref, *rest_ref):
    total = mine_ref[...] + got_ref[...]
    line_w = total[width : width + 1, :]
    line_z = total[width + 1 : width + 2, :]
    diagonal = iota((width, LANES), 0) == iota((width, LANES), 1)
    sum_w = jnp.sum(jnp.where(diagonal, line_w, 0.0), axis=1, keepdims=True)
    mean_x = total[:width, :] / jnp.where(sum_w > 0.0, sum_w, 1.0)
    mean_z = line_z / jnp.where(line_w > 0.0, line_w, 1.0)
    height = out_ref.shape[1]
    rest = jnp.zeros((height - width - 2, LANES), F32)
    result = jnp.concatenate([mean_x, line_w, mean_z, rest], axis=0)
    for j in range(out_ref.shape[0]):
        out_ref[j] = result
    if rest_ref:
        gram = total[height:, :]
        rest_ref[0][: gram.shape[0], :] = gram
        rest_ref[0][gram.shape[0] :, :] = total[width + 2 : width + 2 + TILE, :]


def gather_kernel(blocks, width, x_ref, z_ref, means_ref, dy_ref, x_out, z_out):
    def emit(a, picked):
        x_out[row_block(a), :] = x_ref[row_block(a), :] - picked

    base = core_index() * (blocks * width)
    z_out[...] = gather_half(dy_ref[...], means_ref, base, blocks, width, z_ref[...], emit)


def effect_kernel(
    blocks, width, pd_width, x_ref, z_ref, means_ref, dy_ref, weight_ref, owner_ref, local_ref,
    x2_ref, z2_ref, weighted_ref, send_ref,
):
    dy = dy_ref[...]
    weight = weight_ref[...]
    weight_t = jnp.transpose(weight)

    def emit(a, picked):
        x2 = x_ref[row_block(a), :] - picked
        x2_ref[row_block(a), :] = x2
        weighted_ref[row_block(a), :] = pair(x2 * weight_t[:, a : a + 1])

    z2 = gather_half(dy, means_ref, (1 - core_index()) * (blocks * width), blocks, width, z_ref[...], emit)
    z2_ref[...] = z2
    effect = owner_ref[...] * PD_DEV + local_ref[...]
    scatter_half(
        effect, weight, z2, weighted_ref, (1 - core_index()) * (blocks * pd_width), blocks, pd_width, send_ref
    )


def gram_kernel(
    blocks, pd_width, share, x2_ref, z2_ref, weighted_ref, weight_ref, owner_ref, local_ref,
    keep_ref, gram_ref, plain_ref,
):
    weight = weight_ref[...]
    z2 = z2_ref[...]
    lines = z2.shape[0]
    effect = owner_ref[...] * PD_DEV + local_ref[...]
    scatter_half(
        effect, weight, z2, weighted_ref, core_index() * (blocks * pd_width), blocks, pd_width, keep_ref
    )
    for a in range(lines):
        plain_ref[row_block(a), :] = pair(x2_ref[row_block(a), :])
    gram = dot_first(weighted_ref[...], plain_ref[...])
    gram = unpair(gram[:LANES, :] + gram[LANES:, :])
    left = [part.astype(F32) for part in pieces(weight * z2, 3)]
    none = jnp.zeros((TILE - 3, LANES), F32)
    left = jnp.concatenate(
        [jnp.concatenate([part[a : a + 1, :] for part in left] + [none], axis=0) for a in range(lines)], axis=1
    )
    rhs = unpair(jnp.sum(dot(left.astype(BF16), plain_ref[...]), axis=0, keepdims=True))
    keep_ref[:, pd_width + 2, :] = jnp.broadcast_to(rhs, (blocks, LANES))
    half = blocks * 2 * share
    for j in range(blocks):
        low = gram[2 * j * share : 2 * (j + 1) * share, :]
        high = gram[half + 2 * j * share : half + 2 * (j + 1) * share, :]
        gram_ref[j, : 4 * share, :] = jnp.concatenate([low, high], axis=0)


def gram_less(means_ref, blocks, width, first, share):
    count = blocks * width
    diagonal = iota((blocks, width, LANES), 2) == iota((blocks, width, LANES), 1)
    sum_w = jnp.sum(jnp.where(diagonal, means_ref[:, width, :][:, None, :], 0.0), axis=2, keepdims=True)
    mean_z = jnp.sum(jnp.where(diagonal, means_ref[:, width + 1, :][:, None, :], 0.0), axis=2, keepdims=True)
    mean_x = means_ref[:, :width, :].reshape(count, LANES)
    sum_x = mean_x * sum_w.reshape(count, 1)
    lane = iota((count, LANES), 1)
    rows = []
    for i in range(share):
        column = jnp.sum(jnp.where(lane == first + i, sum_x, 0.0), axis=1, keepdims=True)
        rows.append(jnp.sum(column * mean_x, axis=0, keepdims=True))
    rows.append(jnp.sum(sum_x * mean_z.reshape(count, 1), axis=0, keepdims=True))
    return jnp.concatenate(rows, axis=0)


def own_kernel(blocks, width, share, x_ref, z_ref, means_ref, owner_ref, local_ref, x_out, z_out, less_ref):
    effect = owner_ref[...] * PD_DEV + local_ref[...]

    def emit(a, picked):
        x_out[row_block(a), :] = x_ref[row_block(a), :] - picked

    z_out[...] = gather_half(effect, means_ref, core_index() * (blocks * width), blocks, width, z_ref[...], emit)
    less_ref[: share + 1, :] = gram_less(means_ref, blocks, width, lax.axis_index(AXIS) * share, share)


def last_kernel(
    blocks, width, share, total_rows, x_ref, z_ref, means_ref, less_ref, mine_ref, got_ref, owner_ref, local_ref,
    x_hbm, z_hbm, gram_hbm, rhs_hbm, x_out, z_out, gram_out, rhs_out, sems,
):
    me = lax.axis_index(AXIS)
    core, high = core_index(), lax.div(me, 2 * blocks)
    first = me * share
    copies = []
    effect = owner_ref[...] * PD_DEV + local_ref[...]
    lines = effect.shape[0]
    chunk = max(1, lines // 4)

    def emit(a, picked):
        x_out[row_block(a), :] = x_ref[row_block(a), :] - picked
        if a % chunk == chunk - 1:
            span = slice((a + 1 - chunk) * LANES, (a + 1) * LANES)
            copies.append(pltpu.make_async_copy(x_out.at[span, :], x_hbm.at[span, :], sems.at[3 + a // chunk]))
            copies[-1].start()

    z_out[...] = gather_half(effect, means_ref, (1 - core) * (blocks * width), blocks, width, z_ref[...], emit)
    copies.append(pltpu.make_async_copy(z_out, z_hbm, sems.at[2]))
    copies[-1].start()
    less = gram_less(means_ref, blocks, width, first, share) + less_ref[: share + 1, :]
    total = mine_ref[...] + got_ref[...]
    high_rows = total.shape[0] - TILE
    gram = jnp.zeros((share, LANES), F32)
    for place in range(4):
        here = (high == place // 2) & (core == place % 2)
        gram = jnp.where(here, total[place * share : (place + 1) * share, :], gram)
    scale = 1.0 / total_rows
    gram_out[...] = (gram - less[:share, :]) * scale
    rhs = (total[high_rows : high_rows + 1, :] - less[share:, :]) * scale
    rhs_out[...] = pltpu.roll(rhs, LANES - first, 1)[:, :share]
    copies.append(pltpu.make_async_copy(gram_out, gram_hbm, sems.at[0]))
    copies.append(pltpu.make_async_copy(rhs_out, rhs_hbm, sems.at[1]))
    for copy in copies[-2:]:
        copy.start()
    for copy in copies:
        copy.wait()


VMEM = pl.BlockSpec(memory_space=pltpu.VMEM)
HBM = pl.BlockSpec(memory_space=pltpu.HBM)


def call(kernel, outs, args, scratch=(), flops=0, in_specs=None, out_specs=None):
    size = sum(math.prod(v.shape) * v.dtype.itemsize for v in list(args) + list(outs))
    return pl.pallas_call(
        kernel,
        out_shape=tuple(outs),
        in_specs=in_specs or [VMEM] * len(args),
        out_specs=tuple(out_specs or [VMEM] * len(outs)),
        scratch_shapes=scratch,
        cost_estimate=pl.CostEstimate(flops=flops, bytes_accessed=size, transcendentals=0),
        compiler_params=pltpu.CompilerParams(vmem_limit_bytes=VMEM_LIMIT),
    )(*args)


def in_hbm(v):
    return pltpu.with_memory_space_constraint(v, pltpu.HBM)


def shaped(*shape, dtype=F32):
    return jax.ShapeDtypeStruct(shape, dtype)


def rounded(rows):
    return -(-rows // TILE) * TILE


def shards(covariates, outcome, predictor, firm_id, dy_id, pd_owner, pd_local):
    rows, width = covariates.shape
    devices = lax.axis_size(AXIS)
    blocks = devices // 4
    share = width // devices
    total_rows = rows * devices
    dy_width, pd_width = DY // (2 * blocks), devices * PD_DEV // (2 * blocks)
    dy_high, pd_high = rounded(dy_width + 2), rounded(pd_width + 3)
    gram_high = rounded(4 * share)
    lines = rows // LANES
    groups = [
        [half * (devices // 2) + core_of + 2 * chip for chip in range(blocks)]
        for half in range(2)
        for core_of in range(2)
    ]
    partner = [(i, i ^ 1) for i in range(devices)]
    opposite = [(i, (i + devices // 2) % devices) for i in range(devices)]
    outcome, predictor, firm, dy, owner, local = (
        v.reshape(lines, LANES) for v in (outcome, predictor, firm_id, dy_id, pd_owner, pd_local)
    )
    dy_half, pd_half = blocks * dy_width, blocks * pd_width

    def to_core(v):
        return lax.ppermute(v, AXIS, partner)

    def to_half(v):
        return lax.ppermute(v, AXIS, opposite)

    def across(v):
        return lax.all_to_all(v, AXIS, 0, 0, axis_index_groups=groups)

    def total_of(v):
        return call(total_kernel, (shaped(*v.shape[1:]),), (v,))[0]

    wide = 4 * rows * LANES
    count = min(4, lines)
    x1, z1, weight, dy, pairs, send = call(
        functools.partial(firm_kernel, blocks, dy_width),
        (
            shaped(rows, width),
            shaped(lines, LANES),
            shaped(lines, LANES),
            shaped(lines, LANES, dtype=I32),
            shaped(rows, 2 * LANES, dtype=BF16),
            shaped(blocks, dy_high, LANES),
        ),
        tuple(in_hbm(v) for v in (covariates, outcome, predictor, firm, dy)),
        scratch=(
            pltpu.VMEM((rows, width), F32),
            pltpu.VMEM((lines, LANES), F32),
            pltpu.VMEM((lines, LANES), F32),
            pltpu.VMEM((lines, LANES), I32),
            pltpu.SemaphoreType.DMA((4 + count,)),
        ),
        flops=wide * (dy_half + 2 * FIRM_DEV),
        in_specs=[HBM] * 5,
    )
    got = to_core(send)
    (keep,) = call(
        functools.partial(sums_kernel, blocks, dy_width),
        (shaped(blocks, dy_high, LANES),),
        (pairs, z1, weight, dy),
        flops=wide * dy_half,
    )
    mine = total_of(across(keep + got))
    (means,) = call(
        functools.partial(means_kernel, dy_width), (shaped(blocks, dy_high, LANES),), (mine, to_half(mine))
    )
    means = across(means)
    other = to_core(means)
    x1, z1 = call(
        functools.partial(gather_kernel, blocks, dy_width),
        (shaped(rows, width), shaped(lines, LANES)),
        (x1, z1, means, dy),
        flops=wide * dy_half,
    )
    x2, z2, pairs, send = call(
        functools.partial(effect_kernel, blocks, dy_width, pd_width),
        (
            shaped(rows, width),
            shaped(lines, LANES),
            shaped(rows, 2 * LANES, dtype=BF16),
            shaped(blocks, pd_high, LANES),
        ),
        (x1, z1, other, dy, weight, owner, local),
        flops=wide * (dy_half + pd_half),
    )
    got = to_core(send)
    keep, gram = call(
        functools.partial(gram_kernel, blocks, pd_width, share),
        (shaped(blocks, pd_high, LANES), shaped(blocks, gram_high, LANES)),
        (x2, z2, pairs, weight, owner, local),
        scratch=(pltpu.VMEM((rows, 2 * LANES), BF16),),
        flops=wide * (pd_half + 2 * LANES),
    )
    mine = total_of(across(jnp.concatenate([keep + got, gram], axis=1)))
    means, gram = call(
        functools.partial(means_kernel, pd_width),
        (shaped(blocks, pd_high, LANES), shaped(gram_high + TILE, LANES)),
        (mine, to_half(mine)),
    )
    got = to_core(gram)
    means = across(means)
    other = to_core(means)
    x3, z3, less = call(
        functools.partial(own_kernel, blocks, pd_width, share),
        (shaped(rows, width), shaped(lines, LANES), shaped(rounded(share + 1), LANES)),
        (x2, z2, means, owner, local),
        flops=wide * pd_half,
    )
    x3, z3, gram, rhs = call(
        functools.partial(last_kernel, blocks, pd_width, share, total_rows),
        (shaped(rows, width), shaped(lines, LANES), shaped(share, LANES), shaped(1, share)),
        (x3, z3, other, less, gram, got, owner, local),
        scratch=(
            pltpu.VMEM((rows, width), F32),
            pltpu.VMEM((lines, LANES), F32),
            pltpu.VMEM((share, LANES), F32),
            pltpu.VMEM((1, share), F32),
            pltpu.SemaphoreType.DMA((3 + count,)),
        ),
        flops=wide * pd_half,
        out_specs=[HBM] * 4,
    )
    return x3, z3.reshape(rows), gram, rhs.reshape(share)


def solution(mesh):
    in_specs = (
        P("rows", None),
        P("rows"),
        P("rows"),
        P("rows"),
        P("rows"),
        P("rows", None),
        P("rows"),
    )
    out_specs = (P("rows", None), P("rows"), P("rows", None), P("rows"))
    return jax.shard_map(shards, mesh=mesh, in_specs=in_specs, out_specs=out_specs, check_vma=False)
```

```python
import functools
import math

import jax
import jax.numpy as jnp
from jax import lax
from jax.experimental import pallas as pl
from jax.experimental.pallas import tpu as pltpu
from jax.sharding import PartitionSpec as P

DY = 2048
FIRM_DEV = 128
PD_DEV = 16
LANES = 128
TILE = 8
AXIS = "rows"
VMEM_LIMIT = 32 * 1024 * 1024

BF16 = jnp.bfloat16
F32 = jnp.float32
I32 = jnp.int32


def core_index():
    return lax.rem(lax.axis_index(AXIS), 2)


def iota(shape, dim):
    return lax.broadcasted_iota(I32, shape, dim)


def dot(a, b):
    return jnp.dot(a, b, preferred_element_type=F32)


def dot_first(a, b):
    return lax.dot_general(a, b, (((0,), (0,)), ((), ())), preferred_element_type=F32)


def onehot(mask):
    return jnp.where(mask, 1.0, 0.0).astype(BF16)


def pieces(value, count):
    parts = []
    for _ in range(count):
        part = value.astype(BF16)
        parts.append(part)
        value = value - part.astype(F32)
    return parts


def pair(value):
    return jnp.concatenate(pieces(value, 2), axis=1)


def unpair(value):
    return value[:, :LANES] + value[:, LANES:]


def row_block(a):
    return slice(a * LANES, (a + 1) * LANES)


def weights_of(predictor, outcome):
    weight = jnp.exp(predictor)
    return weight, predictor + outcome / weight - 1.0


def scatter_half(ids, weight, working, pairs_ref, base, blocks, width, out_ref, group=16):
    lines = ids.shape[0]
    count = blocks * width
    step = math.gcd(count, 256)
    for first in range(0, count, step):
        labels = iota((step, LANES), 0) + (base + first)
        table = jnp.concatenate([onehot(labels == ids[a : a + 1, :]) for a in range(lines)], axis=1)
        sums = unpair(dot(table, pairs_ref[...]))
        out_ref[first // width : (first + step) // width, :width, :] = sums.reshape(
            step // width, width, LANES
        )
    block = lax.div(ids, I32(width))
    place = lax.rem(ids, I32(width))
    labels = iota((blocks, LANES), 0) + lax.div(base, I32(width))
    parts = [part.astype(F32) for part in pieces(weight, 3) + pieces(weight * working, 3)]
    sums = jnp.zeros((6 * blocks, width), F32)
    for a in range(0, lines, group):
        left, right = [], []
        for b in range(a, min(a + group, lines)):
            mask = labels == block[b : b + 1, :]
            left.append(jnp.concatenate([jnp.where(mask, part[b : b + 1, :], 0.0) for part in parts], axis=0))
            right.append(onehot(iota((width, LANES), 0) == place[b : b + 1, :]))
        left = jnp.concatenate(left, axis=1).astype(BF16)
        right = jnp.concatenate(right, axis=1)
        sums += lax.dot_general(left, right, (((1,), (1,)), ((), ())), preferred_element_type=F32)
    sums = [sums[i * blocks : (i + 1) * blocks, :] for i in range(6)]
    out_ref[:, width, :width] = sums[0] + sums[1] + sums[2]
    out_ref[:, width + 1, :width] = sums[3] + sums[4] + sums[5]
    spare = out_ref.shape[1] - width - 2
    if spare:
        out_ref[:, width + 2 :, :] = jnp.zeros((blocks, spare, LANES), F32)


def gather_half(ids, means_ref, base, blocks, width, z, emit):
    lines = ids.shape[0]
    count = blocks * width
    group = math.gcd(lines, 4)
    parts = jnp.concatenate([part.astype(F32) for part in pieces(means_ref[:, width + 1, :], 3)], axis=0)
    left = jnp.transpose(parts)[:width, :].astype(BF16)
    block = lax.div(ids, I32(width)) - lax.div(base, I32(width))
    place = lax.rem(ids, I32(width))
    table = pair(means_ref[:, :width, :].reshape(count, LANES))
    labels = iota((count, LANES), 0) + base
    z_new = []
    for a in range(0, lines, group):
        span = range(a, a + group)
        mask = jnp.concatenate([onehot(iota((blocks, LANES), 0) == block[b : b + 1, :]) for b in span], axis=1)
        candidates = dot(left, jnp.concatenate([mask, mask, mask], axis=0))
        for b in span:
            chosen = jnp.where(iota((width, LANES), 0) == place[b : b + 1, :], candidates[:, row_block(b - a)], 0.0)
            z_new.append(z[b : b + 1, :] - jnp.sum(chosen, axis=0, keepdims=True))
        mask = jnp.concatenate([onehot(labels == ids[b : b + 1, :]) for b in range(a, a + group)], axis=1)
        picked = unpair(dot_first(mask, table))
        for b in range(group):
            emit(a + b, picked[row_block(b), :])
    return jnp.concatenate(z_new, axis=0)


def firm_kernel(
    blocks, width, x_hbm, outcome_hbm, predictor_hbm, firm_hbm, dy_hbm,
    x1_ref, z1_ref, weight_ref, dy_ref, pairs_ref, out_ref, x_ref, outcome_ref, predictor_ref, firm_ref, sems,
):
    small = [(firm_hbm, firm_ref), (predictor_hbm, predictor_ref), (outcome_hbm, outcome_ref), (dy_hbm, dy_ref)]
    copies = [pltpu.make_async_copy(src, dst, sems.at[i]) for i, (src, dst) in enumerate(small)]
    count = firm_ref.shape[0]
    chunk = max(1, count // 4)
    starts = list(range(0, count, chunk))
    for i, a in enumerate(starts):
        span = slice(a * LANES, (a + chunk) * LANES)
        copies.append(pltpu.make_async_copy(x_hbm.at[span, :], x_ref.at[span, :], sems.at[len(small) + i]))
    for copy in copies:
        copy.start()
    for copy in copies[: len(small)]:
        copy.wait()
    firm = firm_ref[...]
    weight, working = weights_of(predictor_ref[...], outcome_ref[...])
    weight_ref[...] = weight
    weight_t = jnp.transpose(weight)
    group = math.gcd(count, 4)
    masks = [iota((FIRM_DEV, LANES), 0) == firm[a : a + 1, :] for a in range(count)]
    spread_w = jnp.zeros((FIRM_DEV, LANES), F32)
    spread_z = jnp.zeros((FIRM_DEV, LANES), F32)
    weighted = weight * working
    for a in range(count):
        spread_w += jnp.where(masks[a], weight[a : a + 1, :], 0.0)
        spread_z += jnp.where(masks[a], weighted[a : a + 1, :], 0.0)
    sum_w = jnp.sum(spread_w, axis=1, keepdims=True)
    sum_z = jnp.sum(spread_z, axis=1, keepdims=True)
    denominator = jnp.where(sum_w > 0.0, sum_w, 1.0)
    mean_z = sum_z / denominator
    table = jnp.concatenate([onehot(mask) for mask in masks], axis=1)
    sum_x = jnp.zeros((FIRM_DEV, 2 * LANES), F32)
    for i, a in enumerate(starts):
        copies[len(small) + i].wait()
        span = slice(a * LANES, (a + chunk) * LANES)
        if a == 0:
            offset = jnp.sum(x_ref[row_block(0), :], axis=0, keepdims=True) * (1.0 / LANES)
        for b in range(a, a + chunk):
            pairs_ref[row_block(b), :] = pair((x_ref[row_block(b), :] - offset) * weight_t[:, b : b + 1])
        sum_x += dot(table[:, span], pairs_ref[span, :])
    mean_x = pair(unpair(sum_x) / denominator)
    z1 = []
    for a in range(count):
        if a % group == 0:
            picked = unpair(dot_first(table[:, a * LANES : (a + group) * LANES], mean_x))
        x1 = (x_ref[row_block(a), :] - offset) - picked[row_block(a % group), :]
        x1_ref[row_block(a), :] = x1
        pairs_ref[row_block(a), :] = pair(x1 * weight_t[:, a : a + 1])
        picked_z = jnp.sum(jnp.where(masks[a], mean_z, 0.0), axis=0, keepdims=True)
        z1.append(working[a : a + 1, :] - picked_z)
    z1 = jnp.concatenate(z1, axis=0)
    z1_ref[...] = z1
    dy = dy_ref[...]
    scatter_half(dy, weight, z1, pairs_ref, (1 - core_index()) * (blocks * width), blocks, width, out_ref)


def sums_kernel(blocks, width, pairs_ref, z1_ref, weight_ref, dy_ref, out_ref):
    dy = dy_ref[...]
    scatter_half(dy, weight_ref[...], z1_ref[...], pairs_ref, core_index() * (blocks * width), blocks, width, out_ref)


def total_kernel(in_ref, out_ref):
    total = in_ref[0]
    for j in range(1, in_ref.shape[0]):
        total = total + in_ref[j]
    out_ref[...] = total


def means_kernel(width, mine_ref, got_ref, out_ref, *rest_ref):
    total = mine_ref[...] + got_ref[...]
    line_w = total[width : width + 1, :]
    line_z = total[width + 1 : width + 2, :]
    diagonal = iota((width, LANES), 0) == iota((width, LANES), 1)
    sum_w = jnp.sum(jnp.where(diagonal, line_w, 0.0), axis=1, keepdims=True)
    mean_x = total[:width, :] / jnp.where(sum_w > 0.0, sum_w, 1.0)
    mean_z = line_z / jnp.where(line_w > 0.0, line_w, 1.0)
    height = out_ref.shape[1]
    rest = jnp.zeros((height - width - 2, LANES), F32)
    result = jnp.concatenate([mean_x, line_w, mean_z, rest], axis=0)
    for j in range(out_ref.shape[0]):
        out_ref[j] = result
    if rest_ref:
        gram = total[height:, :]
        rest_ref[0][: gram.shape[0], :] = gram
        rest_ref[0][gram.shape[0] :, :] = total[width + 2 : width + 2 + TILE, :]


def gather_kernel(blocks, width, x_ref, z_ref, means_ref, dy_ref, x_out, z_out):
    def emit(a, picked):
        x_out[row_block(a), :] = x_ref[row_block(a), :] - picked

    base = core_index() * (blocks * width)
    z_out[...] = gather_half(dy_ref[...], means_ref, base, blocks, width, z_ref[...], emit)


def effect_kernel(
    blocks, width, pd_width, x_ref, z_ref, means_ref, dy_ref, weight_ref, owner_ref, local_ref,
    x2_ref, z2_ref, weighted_ref, send_ref,
):
    dy = dy_ref[...]
    weight = weight_ref[...]
    weight_t = jnp.transpose(weight)

    def emit(a, picked):
        x2 = x_ref[row_block(a), :] - picked
        x2_ref[row_block(a), :] = x2
        weighted_ref[row_block(a), :] = pair(x2 * weight_t[:, a : a + 1])

    z2 = gather_half(dy, means_ref, (1 - core_index()) * (blocks * width), blocks, width, z_ref[...], emit)
    z2_ref[...] = z2
    effect = owner_ref[...] * PD_DEV + local_ref[...]
    scatter_half(
        effect, weight, z2, weighted_ref, (1 - core_index()) * (blocks * pd_width), blocks, pd_width, send_ref
    )


def gram_kernel(
    blocks, pd_width, share, x2_ref, z2_ref, weighted_ref, weight_ref, owner_ref, local_ref,
    keep_ref, gram_ref, plain_ref,
):
    weight = weight_ref[...]
    z2 = z2_ref[...]
    lines = z2.shape[0]
    effect = owner_ref[...] * PD_DEV + local_ref[...]
    scatter_half(
        effect, weight, z2, weighted_ref, core_index() * (blocks * pd_width), blocks, pd_width, keep_ref
    )
    for a in range(lines):
        plain_ref[row_block(a), :] = pair(x2_ref[row_block(a), :])
    gram = dot_first(weighted_ref[...], plain_ref[...])
    gram = unpair(gram[:LANES, :] + gram[LANES:, :])
    left = [part.astype(F32) for part in pieces(weight * z2, 3)]
    none = jnp.zeros((TILE - 3, LANES), F32)
    left = jnp.concatenate(
        [jnp.concatenate([part[a : a + 1, :] for part in left] + [none], axis=0) for a in range(lines)], axis=1
    )
    rhs = unpair(jnp.sum(dot(left.astype(BF16), plain_ref[...]), axis=0, keepdims=True))
    keep_ref[:, pd_width + 2, :] = jnp.broadcast_to(rhs, (blocks, LANES))
    half = blocks * 2 * share
    for j in range(blocks):
        low = gram[2 * j * share : 2 * (j + 1) * share, :]
        high = gram[half + 2 * j * share : half + 2 * (j + 1) * share, :]
        gram_ref[j, : 4 * share, :] = jnp.concatenate([low, high], axis=0)


def gram_less(means_ref, blocks, width, first, share):
    count = blocks * width
    diagonal = iota((blocks, width, LANES), 2) == iota((blocks, width, LANES), 1)
    sum_w = jnp.sum(jnp.where(diagonal, means_ref[:, width, :][:, None, :], 0.0), axis=2, keepdims=True)
    mean_z = jnp.sum(jnp.where(diagonal, means_ref[:, width + 1, :][:, None, :], 0.0), axis=2, keepdims=True)
    mean_x = means_ref[:, :width, :].reshape(count, LANES)
    sum_x = mean_x * sum_w.reshape(count, 1)
    lane = iota((count, LANES), 1)
    rows = []
    for i in range(share):
        column = jnp.sum(jnp.where(lane == first + i, sum_x, 0.0), axis=1, keepdims=True)
        rows.append(jnp.sum(column * mean_x, axis=0, keepdims=True))
    rows.append(jnp.sum(sum_x * mean_z.reshape(count, 1), axis=0, keepdims=True))
    return jnp.concatenate(rows, axis=0)


def own_kernel(blocks, width, share, x_ref, z_ref, means_ref, owner_ref, local_ref, x_out, z_out, less_ref):
    effect = owner_ref[...] * PD_DEV + local_ref[...]

    def emit(a, picked):
        x_out[row_block(a), :] = x_ref[row_block(a), :] - picked

    z_out[...] = gather_half(effect, means_ref, core_index() * (blocks * width), blocks, width, z_ref[...], emit)
    less_ref[: share + 1, :] = gram_less(means_ref, blocks, width, lax.axis_index(AXIS) * share, share)


def last_kernel(
    blocks, width, share, total_rows, x_ref, z_ref, means_ref, less_ref, mine_ref, got_ref, owner_ref, local_ref,
    x_hbm, z_hbm, gram_hbm, rhs_hbm, x_out, z_out, gram_out, rhs_out, sems,
):
    me = lax.axis_index(AXIS)
    core, high = core_index(), lax.div(me, 2 * blocks)
    first = me * share
    copies = []
    effect = owner_ref[...] * PD_DEV + local_ref[...]
    lines = effect.shape[0]
    chunk = max(1, lines // 4)

    def emit(a, picked):
        x_out[row_block(a), :] = x_ref[row_block(a), :] - picked
        if a % chunk == chunk - 1:
            span = slice((a + 1 - chunk) * LANES, (a + 1) * LANES)
            copies.append(pltpu.make_async_copy(x_out.at[span, :], x_hbm.at[span, :], sems.at[3 + a // chunk]))
            copies[-1].start()

    z_out[...] = gather_half(effect, means_ref, (1 - core) * (blocks * width), blocks, width, z_ref[...], emit)
    copies.append(pltpu.make_async_copy(z_out, z_hbm, sems.at[2]))
    copies[-1].start()
    less = gram_less(means_ref, blocks, width, first, share) + less_ref[: share + 1, :]
    total = mine_ref[...] + got_ref[...]
    high_rows = total.shape[0] - TILE
    gram = jnp.zeros((share, LANES), F32)
    for place in range(4):
        here = (high == place // 2) & (core == place % 2)
        gram = jnp.where(here, total[place * share : (place + 1) * share, :], gram)
    scale = 1.0 / total_rows
    gram_out[...] = (gram - less[:share, :]) * scale
    rhs = (total[high_rows : high_rows + 1, :] - less[share:, :]) * scale
    rhs_out[...] = pltpu.roll(rhs, LANES - first, 1)[:, :share]
    copies.append(pltpu.make_async_copy(gram_out, gram_hbm, sems.at[0]))
    copies.append(pltpu.make_async_copy(rhs_out, rhs_hbm, sems.at[1]))
    for copy in copies[-2:]:
        copy.start()
    for copy in copies:
        copy.wait()


VMEM = pl.BlockSpec(memory_space=pltpu.VMEM)
HBM = pl.BlockSpec(memory_space=pltpu.HBM)


def call(kernel, outs, args, scratch=(), flops=0, in_specs=None, out_specs=None):
    size = sum(math.prod(v.shape) * v.dtype.itemsize for v in list(args) + list(outs))
    return pl.pallas_call(
        kernel,
        out_shape=tuple(outs),
        in_specs=in_specs or [VMEM] * len(args),
        out_specs=tuple(out_specs or [VMEM] * len(outs)),
        scratch_shapes=scratch,
        cost_estimate=pl.CostEstimate(flops=flops, bytes_accessed=size, transcendentals=0),
        compiler_params=pltpu.CompilerParams(vmem_limit_bytes=VMEM_LIMIT),
    )(*args)


def in_hbm(v):
    return pltpu.with_memory_space_constraint(v, pltpu.HBM)


def shaped(*shape, dtype=F32):
    return jax.ShapeDtypeStruct(shape, dtype)


def rounded(rows):
    return -(-rows // TILE) * TILE


def shards(covariates, outcome, predictor, firm_id, dy_id, pd_owner, pd_local):
    rows, width = covariates.shape
    devices = lax.axis_size(AXIS)
    blocks = devices // 4
    share = width // devices
    total_rows = rows * devices
    dy_width, pd_width = DY // (2 * blocks), devices * PD_DEV // (2 * blocks)
    dy_high, pd_high = rounded(dy_width + 2), rounded(pd_width + 3)
    gram_high = rounded(4 * share)
    lines = rows // LANES
    groups = [
        [half * (devices // 2) + core_of + 2 * chip for chip in range(blocks)]
        for half in range(2)
        for core_of in range(2)
    ]
    partner = [(i, i ^ 1) for i in range(devices)]
    opposite = [(i, (i + devices // 2) % devices) for i in range(devices)]
    outcome, predictor, firm, dy, owner, local = (
        v.reshape(lines, LANES) for v in (outcome, predictor, firm_id, dy_id, pd_owner, pd_local)
    )
    dy_half, pd_half = blocks * dy_width, blocks * pd_width

    def to_core(v):
        return lax.ppermute(v, AXIS, partner)

    def to_half(v):
        return lax.ppermute(v, AXIS, opposite)

    def across(v):
        return lax.all_to_all(v, AXIS, 0, 0, axis_index_groups=groups)

    def total_of(v):
        return call(total_kernel, (shaped(*v.shape[1:]),), (v,))[0]

    wide = 4 * rows * LANES
    count = min(4, lines)
    x1, z1, weight, dy, pairs, send = call(
        functools.partial(firm_kernel, blocks, dy_width),
        (
            shaped(rows, width),
            shaped(lines, LANES),
            shaped(lines, LANES),
            shaped(lines, LANES, dtype=I32),
            shaped(rows, 2 * LANES, dtype=BF16),
            shaped(blocks, dy_high, LANES),
        ),
        tuple(in_hbm(v) for v in (covariates, outcome, predictor, firm, dy)),
        scratch=(
            pltpu.VMEM((rows, width), F32),
            pltpu.VMEM((lines, LANES), F32),
            pltpu.VMEM((lines, LANES), F32),
            pltpu.VMEM((lines, LANES), I32),
            pltpu.SemaphoreType.DMA((4 + count,)),
        ),
        flops=wide * (dy_half + 2 * FIRM_DEV),
        in_specs=[HBM] * 5,
    )
    got = to_core(send)
    (keep,) = call(
        functools.partial(sums_kernel, blocks, dy_width),
        (shaped(blocks, dy_high, LANES),),
        (pairs, z1, weight, dy),
        flops=wide * dy_half,
    )
    mine = total_of(across(keep + got))
    (means,) = call(
        functools.partial(means_kernel, dy_width), (shaped(blocks, dy_high, LANES),), (mine, to_half(mine))
    )
    means = across(means)
    other = to_core(means)
    x1, z1 = call(
        functools.partial(gather_kernel, blocks, dy_width),
        (shaped(rows, width), shaped(lines, LANES)),
        (x1, z1, means, dy),
        flops=wide * dy_half,
    )
    x2, z2, pairs, send = call(
        functools.partial(effect_kernel, blocks, dy_width, pd_width),
        (
            shaped(rows, width),
            shaped(lines, LANES),
            shaped(rows, 2 * LANES, dtype=BF16),
            shaped(blocks, pd_high, LANES),
        ),
        (x1, z1, other, dy, weight, owner, local),
        flops=wide * (dy_half + pd_half),
    )
    got = to_core(send)
    keep, gram = call(
        functools.partial(gram_kernel, blocks, pd_width, share),
        (shaped(blocks, pd_high, LANES), shaped(blocks, gram_high, LANES)),
        (x2, z2, pairs, weight, owner, local),
        scratch=(pltpu.VMEM((rows, 2 * LANES), BF16),),
        flops=wide * (pd_half + 2 * LANES),
    )
    mine = total_of(across(jnp.concatenate([keep + got, gram], axis=1)))
    means, gram = call(
        functools.partial(means_kernel, pd_width),
        (shaped(blocks, pd_high, LANES), shaped(gram_high + TILE, LANES)),
        (mine, to_half(mine)),
    )
    got = to_core(gram)
    means = across(means)
    other = to_core(means)
    x3, z3, less = call(
        functools.partial(own_kernel, blocks, pd_width, share),
        (shaped(rows, width), shaped(lines, LANES), shaped(rounded(share + 1), LANES)),
        (x2, z2, means, owner, local),
        flops=wide * pd_half,
    )
    x3, z3, gram, rhs = call(
        functools.partial(last_kernel, blocks, pd_width, share, total_rows),
        (shaped(rows, width), shaped(lines, LANES), shaped(share, LANES), shaped(1, share)),
        (x3, z3, other, less, gram, got, owner, local),
        scratch=(
            pltpu.VMEM((rows, width), F32),
            pltpu.VMEM((lines, LANES), F32),
            pltpu.VMEM((share, LANES), F32),
            pltpu.VMEM((1, share), F32),
            pltpu.SemaphoreType.DMA((3 + count,)),
        ),
        flops=wide * pd_half,
        out_specs=[HBM] * 4,
    )
    return x3, z3.reshape(rows), gram, rhs.reshape(share)


def solution(mesh):
    in_specs = (
        P("rows", None),
        P("rows"),
        P("rows"),
        P("rows"),
        P("rows"),
        P("rows", None),
        P("rows"),
    )
    out_specs = (P("rows", None), P("rows"), P("rows", None), P("rows"))
    return jax.shard_map(shards, mesh=mesh, in_specs=in_specs, out_specs=out_specs, check_vma=False)
```

```python
import functools
import math

import jax
import jax.numpy as jnp
from jax import lax
from jax.experimental import pallas as pl
from jax.experimental.pallas import tpu as pltpu
from jax.sharding import PartitionSpec as P

DY = 2048
FIRM_DEV = 128
PD_DEV = 16
LANES = 128
TILE = 8
AXIS = "rows"
VMEM_LIMIT = 32 * 1024 * 1024

BF16 = jnp.bfloat16
F32 = jnp.float32
I32 = jnp.int32


def core_index():
    return lax.rem(lax.axis_index(AXIS), 2)


def iota(shape, dim):
    return lax.broadcasted_iota(I32, shape, dim)


def dot(a, b):
    return jnp.dot(a, b, preferred_element_type=F32)


def dot_first(a, b):
    return lax.dot_general(a, b, (((0,), (0,)), ((), ())), preferred_element_type=F32)


def onehot(mask):
    return jnp.where(mask, 1.0, 0.0).astype(BF16)


def pieces(value, count):
    parts = []
    for _ in range(count):
        part = value.astype(BF16)
        parts.append(part)
        value = value - part.astype(F32)
    return parts


def pair(value):
    return jnp.concatenate(pieces(value, 2), axis=1)


def unpair(value):
    return value[:, :LANES] + value[:, LANES:]


def row_block(a):
    return slice(a * LANES, (a + 1) * LANES)


def weights_of(predictor, outcome):
    weight = jnp.exp(predictor)
    return weight, predictor + outcome / weight - 1.0


def scatter_half(ids, weight, working, pairs_ref, base, blocks, width, out_ref, group=16):
    lines = ids.shape[0]
    count = blocks * width
    step = math.gcd(count, 256)
    for first in range(0, count, step):
        labels = iota((step, LANES), 0) + (base + first)
        table = jnp.concatenate([onehot(labels == ids[a : a + 1, :]) for a in range(lines)], axis=1)
        sums = unpair(dot(table, pairs_ref[...]))
        out_ref[first // width : (first + step) // width, :width, :] = sums.reshape(
            step // width, width, LANES
        )
    block = lax.div(ids, I32(width))
    place = lax.rem(ids, I32(width))
    labels = iota((blocks, LANES), 0) + lax.div(base, I32(width))
    parts = [part.astype(F32) for part in pieces(weight, 3) + pieces(weight * working, 3)]
    sums = jnp.zeros((6 * blocks, width), F32)
    for a in range(0, lines, group):
        left, right = [], []
        for b in range(a, min(a + group, lines)):
            mask = labels == block[b : b + 1, :]
            left.append(jnp.concatenate([jnp.where(mask, part[b : b + 1, :], 0.0) for part in parts], axis=0))
            right.append(onehot(iota((width, LANES), 0) == place[b : b + 1, :]))
        left = jnp.concatenate(left, axis=1).astype(BF16)
        right = jnp.concatenate(right, axis=1)
        sums += lax.dot_general(left, right, (((1,), (1,)), ((), ())), preferred_element_type=F32)
    sums = [sums[i * blocks : (i + 1) * blocks, :] for i in range(6)]
    out_ref[:, width, :width] = sums[0] + sums[1] + sums[2]
    out_ref[:, width + 1, :width] = sums[3] + sums[4] + sums[5]
    spare = out_ref.shape[1] - width - 2
    if spare:
        out_ref[:, width + 2 :, :] = jnp.zeros((blocks, spare, LANES), F32)


def gather_half(ids, means_ref, base, blocks, width, z, emit):
    lines = ids.shape[0]
    count = blocks * width
    group = math.gcd(lines, 4)
    parts = jnp.concatenate([part.astype(F32) for part in pieces(means_ref[:, width + 1, :], 3)], axis=0)
    left = jnp.transpose(parts)[:width, :].astype(BF16)
    block = lax.div(ids, I32(width)) - lax.div(base, I32(width))
    place = lax.rem(ids, I32(width))
    table = pair(means_ref[:, :width, :].reshape(count, LANES))
    labels = iota((count, LANES), 0) + base
    z_new = []
    for a in range(0, lines, group):
        span = range(a, a + group)
        mask = jnp.concatenate([onehot(iota((blocks, LANES), 0) == block[b : b + 1, :]) for b in span], axis=1)
        candidates = dot(left, jnp.concatenate([mask, mask, mask], axis=0))
        for b in span:
            chosen = jnp.where(iota((width, LANES), 0) == place[b : b + 1, :], candidates[:, row_block(b - a)], 0.0)
            z_new.append(z[b : b + 1, :] - jnp.sum(chosen, axis=0, keepdims=True))
        mask = jnp.concatenate([onehot(labels == ids[b : b + 1, :]) for b in range(a, a + group)], axis=1)
        picked = unpair(dot_first(mask, table))
        for b in range(group):
            emit(a + b, picked[row_block(b), :])
    return jnp.concatenate(z_new, axis=0)


def firm_kernel(
    blocks, width, x_hbm, outcome_hbm, predictor_hbm, firm_hbm, dy_hbm,
    x1_ref, z1_ref, weight_ref, dy_ref, pairs_ref, out_ref, x_ref, outcome_ref, predictor_ref, firm_ref, sems,
):
    small = [(firm_hbm, firm_ref), (predictor_hbm, predictor_ref), (outcome_hbm, outcome_ref), (dy_hbm, dy_ref)]
    copies = [pltpu.make_async_copy(src, dst, sems.at[i]) for i, (src, dst) in enumerate(small)]
    count = firm_ref.shape[0]
    chunk = max(1, count // 4)
    starts = list(range(0, count, chunk))
    for i, a in enumerate(starts):
        span = slice(a * LANES, (a + chunk) * LANES)
        copies.append(pltpu.make_async_copy(x_hbm.at[span, :], x_ref.at[span, :], sems.at[len(small) + i]))
    for copy in copies:
        copy.start()
    for copy in copies[: len(small)]:
        copy.wait()
    firm = firm_ref[...]
    weight, working = weights_of(predictor_ref[...], outcome_ref[...])
    weight_ref[...] = weight
    weight_t = jnp.transpose(weight)
    group = math.gcd(count, 4)
    masks = [iota((FIRM_DEV, LANES), 0) == firm[a : a + 1, :] for a in range(count)]
    spread_w = jnp.zeros((FIRM_DEV, LANES), F32)
    spread_z = jnp.zeros((FIRM_DEV, LANES), F32)
    weighted = weight * working
    for a in range(count):
        spread_w += jnp.where(masks[a], weight[a : a + 1, :], 0.0)
        spread_z += jnp.where(masks[a], weighted[a : a + 1, :], 0.0)
    sum_w = jnp.sum(spread_w, axis=1, keepdims=True)
    sum_z = jnp.sum(spread_z, axis=1, keepdims=True)
    denominator = jnp.where(sum_w > 0.0, sum_w, 1.0)
    mean_z = sum_z / denominator
    table = jnp.concatenate([onehot(mask) for mask in masks], axis=1)
    for i, a in enumerate(starts):
        copies[len(small) + i].wait()
        if a == 0:
            offset = jnp.sum(x_ref[row_block(0), :], axis=0, keepdims=True) * (1.0 / LANES)
        for b in range(a, a + chunk):
            pairs_ref[row_block(b), :] = pair((x_ref[row_block(b), :] - offset) * weight_t[:, b : b + 1])
    mean_x = pair(unpair(dot(table, pairs_ref[...])) / denominator)
    z1 = []
    for a in range(count):
        if a % group == 0:
            picked = unpair(dot_first(table[:, a * LANES : (a + group) * LANES], mean_x))
        x1 = (x_ref[row_block(a), :] - offset) - picked[row_block(a % group), :]
        x1_ref[row_block(a), :] = x1
        pairs_ref[row_block(a), :] = pair(x1 * weight_t[:, a : a + 1])
        picked_z = jnp.sum(jnp.where(masks[a], mean_z, 0.0), axis=0, keepdims=True)
        z1.append(working[a : a + 1, :] - picked_z)
    z1 = jnp.concatenate(z1, axis=0)
    z1_ref[...] = z1
    dy = dy_ref[...]
    scatter_half(dy, weight, z1, pairs_ref, (1 - core_index()) * (blocks * width), blocks, width, out_ref)


def sums_kernel(blocks, width, pairs_ref, z1_ref, weight_ref, dy_ref, out_ref):
    dy = dy_ref[...]
    scatter_half(dy, weight_ref[...], z1_ref[...], pairs_ref, core_index() * (blocks * width), blocks, width, out_ref)


def total_kernel(in_ref, out_ref):
    total = in_ref[0]
    for j in range(1, in_ref.shape[0]):
        total = total + in_ref[j]
    out_ref[...] = total


def means_kernel(width, mine_ref, got_ref, out_ref, *rest_ref):
    total = mine_ref[...] + got_ref[...]
    line_w = total[width : width + 1, :]
    line_z = total[width + 1 : width + 2, :]
    diagonal = iota((width, LANES), 0) == iota((width, LANES), 1)
    sum_w = jnp.sum(jnp.where(diagonal, line_w, 0.0), axis=1, keepdims=True)
    mean_x = total[:width, :] / jnp.where(sum_w > 0.0, sum_w, 1.0)
    mean_z = line_z / jnp.where(line_w > 0.0, line_w, 1.0)
    height = out_ref.shape[1]
    rest = jnp.zeros((height - width - 2, LANES), F32)
    result = jnp.concatenate([mean_x, line_w, mean_z, rest], axis=0)
    for j in range(out_ref.shape[0]):
        out_ref[j] = result
    if rest_ref:
        gram = total[height:, :]
        rest_ref[0][: gram.shape[0], :] = gram
        rest_ref[0][gram.shape[0] :, :] = total[width + 2 : width + 2 + TILE, :]


def gather_kernel(blocks, width, x_ref, z_ref, means_ref, dy_ref, x_out, z_out):
    def emit(a, picked):
        x_out[row_block(a), :] = x_ref[row_block(a), :] - picked

    base = core_index() * (blocks * width)
    z_out[...] = gather_half(dy_ref[...], means_ref, base, blocks, width, z_ref[...], emit)


def effect_kernel(
    blocks, width, pd_width, x_ref, z_ref, means_ref, dy_ref, weight_ref, owner_ref, local_ref,
    x2_ref, z2_ref, weighted_ref, send_ref,
):
    dy = dy_ref[...]
    weight = weight_ref[...]
    weight_t = jnp.transpose(weight)

    def emit(a, picked):
        x2 = x_ref[row_block(a), :] - picked
        x2_ref[row_block(a), :] = x2
        weighted_ref[row_block(a), :] = pair(x2 * weight_t[:, a : a + 1])

    z2 = gather_half(dy, means_ref, (1 - core_index()) * (blocks * width), blocks, width, z_ref[...], emit)
    z2_ref[...] = z2
    effect = owner_ref[...] * PD_DEV + local_ref[...]
    scatter_half(
        effect, weight, z2, weighted_ref, (1 - core_index()) * (blocks * pd_width), blocks, pd_width, send_ref
    )


def gram_kernel(
    blocks, pd_width, share, x2_ref, z2_ref, weighted_ref, weight_ref, owner_ref, local_ref,
    keep_ref, gram_ref, plain_ref,
):
    weight = weight_ref[...]
    z2 = z2_ref[...]
    lines = z2.shape[0]
    effect = owner_ref[...] * PD_DEV + local_ref[...]
    scatter_half(
        effect, weight, z2, weighted_ref, core_index() * (blocks * pd_width), blocks, pd_width, keep_ref
    )
    for a in range(lines):
        plain_ref[row_block(a), :] = pair(x2_ref[row_block(a), :])
    gram = dot_first(weighted_ref[...], plain_ref[...])
    gram = unpair(gram[:LANES, :] + gram[LANES:, :])
    left = [part.astype(F32) for part in pieces(weight * z2, 3)]
    none = jnp.zeros((TILE - 3, LANES), F32)
    left = jnp.concatenate(
        [jnp.concatenate([part[a : a + 1, :] for part in left] + [none], axis=0) for a in range(lines)], axis=1
    )
    rhs = unpair(jnp.sum(dot(left.astype(BF16), plain_ref[...]), axis=0, keepdims=True))
    keep_ref[:, pd_width + 2, :] = jnp.broadcast_to(rhs, (blocks, LANES))
    half = blocks * 2 * share
    for j in range(blocks):
        low = gram[2 * j * share : 2 * (j + 1) * share, :]
        high = gram[half + 2 * j * share : half + 2 * (j + 1) * share, :]
        gram_ref[j, : 4 * share, :] = jnp.concatenate([low, high], axis=0)


def gram_less(means_ref, blocks, width, first, share):
    count = blocks * width
    diagonal = iota((blocks, width, LANES), 2) == iota((blocks, width, LANES), 1)
    sum_w = jnp.sum(jnp.where(diagonal, means_ref[:, width, :][:, None, :], 0.0), axis=2, keepdims=True)
    mean_z = jnp.sum(jnp.where(diagonal, means_ref[:, width + 1, :][:, None, :], 0.0), axis=2, keepdims=True)
    mean_x = means_ref[:, :width, :].reshape(count, LANES)
    sum_x = mean_x * sum_w.reshape(count, 1)
    lane = iota((count, LANES), 1)
    rows = []
    for i in range(share):
        column = jnp.sum(jnp.where(lane == first + i, sum_x, 0.0), axis=1, keepdims=True)
        rows.append(jnp.sum(column * mean_x, axis=0, keepdims=True))
    rows.append(jnp.sum(sum_x * mean_z.reshape(count, 1), axis=0, keepdims=True))
    return jnp.concatenate(rows, axis=0)


def own_kernel(blocks, width, share, x_ref, z_ref, means_ref, owner_ref, local_ref, x_out, z_out, less_ref):
    effect = owner_ref[...] * PD_DEV + local_ref[...]

    def emit(a, picked):
        x_out[row_block(a), :] = x_ref[row_block(a), :] - picked

    z_out[...] = gather_half(effect, means_ref, core_index() * (blocks * width), blocks, width, z_ref[...], emit)
    less_ref[: share + 1, :] = gram_less(means_ref, blocks, width, lax.axis_index(AXIS) * share, share)


def last_kernel(
    blocks, width, share, total_rows, x_ref, z_ref, means_ref, less_ref, mine_ref, got_ref, owner_ref, local_ref,
    x_hbm, z_hbm, gram_hbm, rhs_hbm, x_out, z_out, gram_out, rhs_out, sems,
):
    me = lax.axis_index(AXIS)
    core, high = core_index(), lax.div(me, 2 * blocks)
    first = me * share
    copies = []
    effect = owner_ref[...] * PD_DEV + local_ref[...]
    lines = effect.shape[0]
    chunk = max(1, lines // 4)

    def emit(a, picked):
        x_out[row_block(a), :] = x_ref[row_block(a), :] - picked
        if a % chunk == chunk - 1:
            span = slice((a + 1 - chunk) * LANES, (a + 1) * LANES)
            copies.append(pltpu.make_async_copy(x_out.at[span, :], x_hbm.at[span, :], sems.at[3 + a // chunk]))
            copies[-1].start()

    z_out[...] = gather_half(effect, means_ref, (1 - core) * (blocks * width), blocks, width, z_ref[...], emit)
    copies.append(pltpu.make_async_copy(z_out, z_hbm, sems.at[2]))
    copies[-1].start()
    less = gram_less(means_ref, blocks, width, first, share) + less_ref[: share + 1, :]
    total = mine_ref[...] + got_ref[...]
    high_rows = total.shape[0] - TILE
    gram = jnp.zeros((share, LANES), F32)
    for place in range(4):
        here = (high == place // 2) & (core == place % 2)
        gram = jnp.where(here, total[place * share : (place + 1) * share, :], gram)
    scale = 1.0 / total_rows
    gram_out[...] = (gram - less[:share, :]) * scale
    rhs = (total[high_rows : high_rows + 1, :] - less[share:, :]) * scale
    rhs_out[...] = pltpu.roll(rhs, lax.rem(LANES - first, LANES), 1)[:, :share]
    copies.append(pltpu.make_async_copy(gram_out, gram_hbm, sems.at[0]))
    copies.append(pltpu.make_async_copy(rhs_out, rhs_hbm, sems.at[1]))
    for copy in copies[-2:]:
        copy.start()
    for copy in copies:
        copy.wait()


VMEM = pl.BlockSpec(memory_space=pltpu.VMEM)
HBM = pl.BlockSpec(memory_space=pltpu.HBM)


def call(kernel, outs, args, scratch=(), flops=0, in_specs=None, out_specs=None):
    size = sum(math.prod(v.shape) * v.dtype.itemsize for v in list(args) + list(outs))
    return pl.pallas_call(
        kernel,
        out_shape=tuple(outs),
        in_specs=in_specs or [VMEM] * len(args),
        out_specs=tuple(out_specs or [VMEM] * len(outs)),
        scratch_shapes=scratch,
        cost_estimate=pl.CostEstimate(flops=flops, bytes_accessed=size, transcendentals=0),
        compiler_params=pltpu.CompilerParams(vmem_limit_bytes=VMEM_LIMIT),
    )(*args)


def in_hbm(v):
    return pltpu.with_memory_space_constraint(v, pltpu.HBM)


def shaped(*shape, dtype=F32):
    return jax.ShapeDtypeStruct(shape, dtype)


def rounded(rows):
    return -(-rows // TILE) * TILE


def shards(covariates, outcome, predictor, firm_id, dy_id, pd_owner, pd_local):
    rows, width = covariates.shape
    devices = lax.axis_size(AXIS)
    blocks = devices // 4
    share = width // devices
    total_rows = rows * devices
    dy_width, pd_width = DY // (2 * blocks), devices * PD_DEV // (2 * blocks)
    dy_high, pd_high = rounded(dy_width + 2), rounded(pd_width + 3)
    gram_high = rounded(4 * share)
    lines = rows // LANES
    groups = [
        [half * (devices // 2) + core_of + 2 * chip for chip in range(blocks)]
        for half in range(2)
        for core_of in range(2)
    ]
    partner = [(i, i ^ 1) for i in range(devices)]
    opposite = [(i, (i + devices // 2) % devices) for i in range(devices)]
    outcome, predictor, firm, dy, owner, local = (
        v.reshape(lines, LANES) for v in (outcome, predictor, firm_id, dy_id, pd_owner, pd_local)
    )
    dy_half, pd_half = blocks * dy_width, blocks * pd_width

    def to_core(v):
        return lax.ppermute(v, AXIS, partner)

    def to_half(v):
        return lax.ppermute(v, AXIS, opposite)

    def across(v):
        return lax.all_to_all(v, AXIS, 0, 0, axis_index_groups=groups)

    def total_of(v):
        return call(total_kernel, (shaped(*v.shape[1:]),), (v,))[0]

    wide = 4 * rows * LANES
    count = min(4, lines)
    x1, z1, weight, dy, pairs, send = call(
        functools.partial(firm_kernel, blocks, dy_width),
        (
            shaped(rows, width),
            shaped(lines, LANES),
            shaped(lines, LANES),
            shaped(lines, LANES, dtype=I32),
            shaped(rows, 2 * LANES, dtype=BF16),
            shaped(blocks, dy_high, LANES),
        ),
        tuple(in_hbm(v) for v in (covariates, outcome, predictor, firm, dy)),
        scratch=(
            pltpu.VMEM((rows, width), F32),
            pltpu.VMEM((lines, LANES), F32),
            pltpu.VMEM((lines, LANES), F32),
            pltpu.VMEM((lines, LANES), I32),
            pltpu.SemaphoreType.DMA((4 + count,)),
        ),
        flops=wide * (dy_half + 2 * FIRM_DEV),
        in_specs=[HBM] * 5,
    )
    got = to_core(send)
    (keep,) = call(
        functools.partial(sums_kernel, blocks, dy_width),
        (shaped(blocks, dy_high, LANES),),
        (pairs, z1, weight, dy),
        flops=wide * dy_half,
    )
    mine = total_of(across(keep + got))
    (means,) = call(
        functools.partial(means_kernel, dy_width), (shaped(blocks, dy_high, LANES),), (mine, to_half(mine))
    )
    means = across(means)
    other = to_core(means)
    x1, z1 = call(
        functools.partial(gather_kernel, blocks, dy_width),
        (shaped(rows, width), shaped(lines, LANES)),
        (x1, z1, means, dy),
        flops=wide * dy_half,
    )
    x2, z2, pairs, send = call(
        functools.partial(effect_kernel, blocks, dy_width, pd_width),
        (
            shaped(rows, width),
            shaped(lines, LANES),
            shaped(rows, 2 * LANES, dtype=BF16),
            shaped(blocks, pd_high, LANES),
        ),
        (x1, z1, other, dy, weight, owner, local),
        flops=wide * (dy_half + pd_half),
    )
    got = to_core(send)
    keep, gram = call(
        functools.partial(gram_kernel, blocks, pd_width, share),
        (shaped(blocks, pd_high, LANES), shaped(blocks, gram_high, LANES)),
        (x2, z2, pairs, weight, owner, local),
        scratch=(pltpu.VMEM((rows, 2 * LANES), BF16),),
        flops=wide * (pd_half + 2 * LANES),
    )
    mine = total_of(across(jnp.concatenate([keep + got, gram], axis=1)))
    means, gram = call(
        functools.partial(means_kernel, pd_width),
        (shaped(blocks, pd_high, LANES), shaped(gram_high + TILE, LANES)),
        (mine, to_half(mine)),
    )
    got = to_core(gram)
    means = across(means)
    other = to_core(means)
    x3, z3, less = call(
        functools.partial(own_kernel, blocks, pd_width, share),
        (shaped(rows, width), shaped(lines, LANES), shaped(rounded(share + 1), LANES)),
        (x2, z2, means, owner, local),
        flops=wide * pd_half,
    )
    x3, z3, gram, rhs = call(
        functools.partial(last_kernel, blocks, pd_width, share, total_rows),
        (shaped(rows, width), shaped(lines, LANES), shaped(share, LANES), shaped(1, share)),
        (x3, z3, other, less, gram, got, owner, local),
        scratch=(
            pltpu.VMEM((rows, width), F32),
            pltpu.VMEM((lines, LANES), F32),
            pltpu.VMEM((share, LANES), F32),
            pltpu.VMEM((1, share), F32),
            pltpu.SemaphoreType.DMA((3 + count,)),
        ),
        flops=wide * pd_half,
        out_specs=[HBM] * 4,
    )
    return x3, z3.reshape(rows), gram, rhs.reshape(share)


def solution(mesh):
    in_specs = (
        P("rows", None),
        P("rows"),
        P("rows"),
        P("rows"),
        P("rows"),
        P("rows", None),
        P("rows"),
    )
    out_specs = (P("rows", None), P("rows"), P("rows", None), P("rows"))
    return jax.shard_map(shards, mesh=mesh, in_specs=in_specs, out_specs=out_specs, check_vma=False)
```

```python
import functools
import math

import jax
import jax.numpy as jnp
from jax import lax
from jax.experimental import pallas as pl
from jax.experimental.pallas import tpu as pltpu
from jax.sharding import PartitionSpec as P

DY = 2048
FIRM_DEV = 128
PD_DEV = 16
LANES = 128
TILE = 8
AXIS = "rows"
VMEM_LIMIT = 32 * 1024 * 1024

BF16 = jnp.bfloat16
F32 = jnp.float32
I32 = jnp.int32


def core_index():
    return lax.rem(lax.axis_index(AXIS), 2)


def effect_half(blocks):
    me = lax.axis_index(AXIS)
    return lax.rem(me + lax.div(me, 2 * blocks), 2)


def iota(shape, dim):
    return lax.broadcasted_iota(I32, shape, dim)


def dot(a, b):
    return jnp.dot(a, b, preferred_element_type=F32)


def dot_first(a, b):
    return lax.dot_general(a, b, (((0,), (0,)), ((), ())), preferred_element_type=F32)


def onehot(mask):
    return jnp.where(mask, 1.0, 0.0).astype(BF16)


def pieces(value, count):
    parts = []
    for _ in range(count):
        part = value.astype(BF16)
        parts.append(part)
        value = value - part.astype(F32)
    return parts


def pair(value):
    return jnp.concatenate(pieces(value, 2), axis=1)


def unpair(value):
    return value[:, :LANES] + value[:, LANES:]


def row_block(a):
    return slice(a * LANES, (a + 1) * LANES)


def weights_of(predictor, outcome):
    weight = jnp.exp(predictor)
    return weight, predictor + outcome / weight - 1.0


def scatter_half(ids, weight, working, pairs_ref, base, blocks, width, out_ref, group=16):
    lines = ids.shape[0]
    count = blocks * width
    step = math.gcd(count, 256)
    for first in range(0, count, step):
        labels = iota((step, LANES), 0) + (base + first)
        table = jnp.concatenate([onehot(labels == ids[a : a + 1, :]) for a in range(lines)], axis=1)
        sums = unpair(dot(table, pairs_ref[...]))
        out_ref[first // width : (first + step) // width, :width, :] = sums.reshape(
            step // width, width, LANES
        )
    block = lax.div(ids, I32(width))
    place = lax.rem(ids, I32(width))
    labels = iota((blocks, LANES), 0) + lax.div(base, I32(width))
    parts = [part.astype(F32) for part in pieces(weight, 3) + pieces(weight * working, 3)]
    sums = jnp.zeros((6 * blocks, width), F32)
    for a in range(0, lines, group):
        left, right = [], []
        for b in range(a, min(a + group, lines)):
            mask = labels == block[b : b + 1, :]
            left.append(jnp.concatenate([jnp.where(mask, part[b : b + 1, :], 0.0) for part in parts], axis=0))
            right.append(onehot(iota((width, LANES), 0) == place[b : b + 1, :]))
        left = jnp.concatenate(left, axis=1).astype(BF16)
        right = jnp.concatenate(right, axis=1)
        sums += lax.dot_general(left, right, (((1,), (1,)), ((), ())), preferred_element_type=F32)
    sums = [sums[i * blocks : (i + 1) * blocks, :] for i in range(6)]
    out_ref[:, width, :width] = sums[0] + sums[1] + sums[2]
    out_ref[:, width + 1, :width] = sums[3] + sums[4] + sums[5]
    spare = out_ref.shape[1] - width - 2
    if spare:
        out_ref[:, width + 2 :, :] = jnp.zeros((blocks, spare, LANES), F32)


def gather_half(ids, means_ref, base, blocks, width, z, emit):
    lines = ids.shape[0]
    count = blocks * width
    group = math.gcd(lines, 4)
    parts = jnp.concatenate([part.astype(F32) for part in pieces(means_ref[:, width + 1, :], 3)], axis=0)
    left = jnp.transpose(parts)[:width, :].astype(BF16)
    block = lax.div(ids, I32(width)) - lax.div(base, I32(width))
    place = lax.rem(ids, I32(width))
    table = pair(means_ref[:, :width, :].reshape(count, LANES))
    labels = iota((count, LANES), 0) + base
    z_new = []
    for a in range(0, lines, group):
        span = range(a, a + group)
        mask = jnp.concatenate([onehot(iota((blocks, LANES), 0) == block[b : b + 1, :]) for b in span], axis=1)
        candidates = dot(left, jnp.concatenate([mask, mask, mask], axis=0))
        for b in span:
            chosen = jnp.where(iota((width, LANES), 0) == place[b : b + 1, :], candidates[:, row_block(b - a)], 0.0)
            z_new.append(z[b : b + 1, :] - jnp.sum(chosen, axis=0, keepdims=True))
        mask = jnp.concatenate([onehot(labels == ids[b : b + 1, :]) for b in range(a, a + group)], axis=1)
        picked = unpair(dot_first(mask, table))
        for b in range(group):
            emit(a + b, picked[row_block(b), :])
    return jnp.concatenate(z_new, axis=0)


def firm_kernel(
    blocks, width, x_hbm, outcome_hbm, predictor_hbm, firm_hbm, dy_hbm,
    x1_ref, z1_ref, weight_ref, dy_ref, pairs_ref, out_ref, x_ref, outcome_ref, predictor_ref, firm_ref, sems,
):
    small = [(firm_hbm, firm_ref), (predictor_hbm, predictor_ref), (outcome_hbm, outcome_ref), (dy_hbm, dy_ref)]
    copies = [pltpu.make_async_copy(src, dst, sems.at[i]) for i, (src, dst) in enumerate(small)]
    count = firm_ref.shape[0]
    chunk = max(1, count // 4)
    starts = list(range(0, count, chunk))
    for i, a in enumerate(starts):
        span = slice(a * LANES, (a + chunk) * LANES)
        copies.append(pltpu.make_async_copy(x_hbm.at[span, :], x_ref.at[span, :], sems.at[len(small) + i]))
    for copy in copies:
        copy.start()
    for copy in copies[: len(small)]:
        copy.wait()
    firm = firm_ref[...]
    weight, working = weights_of(predictor_ref[...], outcome_ref[...])
    weight_ref[...] = weight
    weight_t = jnp.transpose(weight)
    group = math.gcd(count, 4)
    masks = [iota((FIRM_DEV, LANES), 0) == firm[a : a + 1, :] for a in range(count)]
    spread_w = jnp.zeros((FIRM_DEV, LANES), F32)
    spread_z = jnp.zeros((FIRM_DEV, LANES), F32)
    weighted = weight * working
    for a in range(count):
        spread_w += jnp.where(masks[a], weight[a : a + 1, :], 0.0)
        spread_z += jnp.where(masks[a], weighted[a : a + 1, :], 0.0)
    sum_w = jnp.sum(spread_w, axis=1, keepdims=True)
    sum_z = jnp.sum(spread_z, axis=1, keepdims=True)
    denominator = jnp.where(sum_w > 0.0, sum_w, 1.0)
    mean_z = sum_z / denominator
    table = jnp.concatenate([onehot(mask) for mask in masks], axis=1)
    for i, a in enumerate(starts):
        copies[len(small) + i].wait()
        if a == 0:
            offset = jnp.sum(x_ref[row_block(0), :], axis=0, keepdims=True) * (1.0 / LANES)
        for b in range(a, a + chunk):
            pairs_ref[row_block(b), :] = pair((x_ref[row_block(b), :] - offset) * weight_t[:, b : b + 1])
    mean_x = pair(unpair(dot(table, pairs_ref[...])) / denominator)
    z1 = []
    for a in range(count):
        if a % group == 0:
            picked = unpair(dot_first(table[:, a * LANES : (a + group) * LANES], mean_x))
        x1 = (x_ref[row_block(a), :] - offset) - picked[row_block(a % group), :]
        x1_ref[row_block(a), :] = x1
        pairs_ref[row_block(a), :] = pair(x1 * weight_t[:, a : a + 1])
        picked_z = jnp.sum(jnp.where(masks[a], mean_z, 0.0), axis=0, keepdims=True)
        z1.append(working[a : a + 1, :] - picked_z)
    z1 = jnp.concatenate(z1, axis=0)
    z1_ref[...] = z1
    dy = dy_ref[...]
    scatter_half(dy, weight, z1, pairs_ref, (1 - core_index()) * (blocks * width), blocks, width, out_ref)


def sums_kernel(blocks, width, pairs_ref, z1_ref, weight_ref, dy_ref, out_ref):
    dy = dy_ref[...]
    scatter_half(dy, weight_ref[...], z1_ref[...], pairs_ref, core_index() * (blocks * width), blocks, width, out_ref)


def total_kernel(in_ref, out_ref):
    total = in_ref[0]
    for j in range(1, in_ref.shape[0]):
        total = total + in_ref[j]
    out_ref[...] = total


def means_kernel(width, mine_ref, got_ref, out_ref, *rest_ref):
    total = mine_ref[...] + got_ref[...]
    line_w = total[width : width + 1, :]
    line_z = total[width + 1 : width + 2, :]
    diagonal = iota((width, LANES), 0) == iota((width, LANES), 1)
    sum_w = jnp.sum(jnp.where(diagonal, line_w, 0.0), axis=1, keepdims=True)
    mean_x = total[:width, :] / jnp.where(sum_w > 0.0, sum_w, 1.0)
    mean_z = line_z / jnp.where(line_w > 0.0, line_w, 1.0)
    height = out_ref.shape[1]
    rest = jnp.zeros((height - width - 2, LANES), F32)
    result = jnp.concatenate([mean_x, line_w, mean_z, rest], axis=0)
    for j in range(out_ref.shape[0]):
        out_ref[j] = result
    if rest_ref:
        gram = total[height:, :]
        rest_ref[0][: gram.shape[0], :] = gram
        rest_ref[0][gram.shape[0] :, :] = total[width + 2 : width + 2 + TILE, :]


def gather_kernel(blocks, width, x_ref, z_ref, means_ref, dy_ref, x_out, z_out):
    def emit(a, picked):
        x_out[row_block(a), :] = x_ref[row_block(a), :] - picked

    base = core_index() * (blocks * width)
    z_out[...] = gather_half(dy_ref[...], means_ref, base, blocks, width, z_ref[...], emit)


def effect_kernel(
    blocks, width, pd_width, x_ref, z_ref, means_ref, dy_ref, weight_ref, owner_ref, local_ref,
    x2_ref, z2_ref, weighted_ref, send_ref,
):
    dy = dy_ref[...]
    weight = weight_ref[...]
    weight_t = jnp.transpose(weight)

    def emit(a, picked):
        x2 = x_ref[row_block(a), :] - picked
        x2_ref[row_block(a), :] = x2
        weighted_ref[row_block(a), :] = pair(x2 * weight_t[:, a : a + 1])

    z2 = gather_half(dy, means_ref, (1 - core_index()) * (blocks * width), blocks, width, z_ref[...], emit)
    z2_ref[...] = z2
    effect = owner_ref[...] * PD_DEV + local_ref[...]
    scatter_half(
        effect, weight, z2, weighted_ref, (1 - effect_half(blocks)) * (blocks * pd_width), blocks, pd_width, send_ref
    )


def gram_kernel(
    blocks, pd_width, share, x2_ref, z2_ref, weighted_ref, weight_ref, owner_ref, local_ref,
    keep_ref, gram_ref, plain_ref,
):
    weight = weight_ref[...]
    z2 = z2_ref[...]
    lines = z2.shape[0]
    effect = owner_ref[...] * PD_DEV + local_ref[...]
    scatter_half(
        effect, weight, z2, weighted_ref, effect_half(blocks) * (blocks * pd_width), blocks, pd_width, keep_ref
    )
    for a in range(lines):
        plain_ref[row_block(a), :] = pair(x2_ref[row_block(a), :])
    gram = dot_first(weighted_ref[...], plain_ref[...])
    gram = unpair(gram[:LANES, :] + gram[LANES:, :])
    left = [part.astype(F32) for part in pieces(weight * z2, 3)]
    none = jnp.zeros((TILE - 3, LANES), F32)
    left = jnp.concatenate(
        [jnp.concatenate([part[a : a + 1, :] for part in left] + [none], axis=0) for a in range(lines)], axis=1
    )
    rhs = unpair(jnp.sum(dot(left.astype(BF16), plain_ref[...]), axis=0, keepdims=True))
    keep_ref[:, pd_width + 2, :] = jnp.broadcast_to(rhs, (blocks, LANES))
    half = blocks * 2 * share
    for j in range(blocks):
        low = gram[2 * j * share : 2 * (j + 1) * share, :]
        high = gram[half + 2 * j * share : half + 2 * (j + 1) * share, :]
        gram_ref[j, : 4 * share, :] = jnp.concatenate([low, high], axis=0)


def gram_less(means_ref, blocks, width, first, share):
    count = blocks * width
    diagonal = iota((blocks, width, LANES), 2) == iota((blocks, width, LANES), 1)
    sum_w = jnp.sum(jnp.where(diagonal, means_ref[:, width, :][:, None, :], 0.0), axis=2, keepdims=True)
    mean_z = jnp.sum(jnp.where(diagonal, means_ref[:, width + 1, :][:, None, :], 0.0), axis=2, keepdims=True)
    mean_x = means_ref[:, :width, :].reshape(count, LANES)
    sum_x = mean_x * sum_w.reshape(count, 1)
    lane = iota((count, LANES), 1)
    rows = []
    for i in range(share):
        column = jnp.sum(jnp.where(lane == first + i, sum_x, 0.0), axis=1, keepdims=True)
        rows.append(jnp.sum(column * mean_x, axis=0, keepdims=True))
    rows.append(jnp.sum(sum_x * mean_z.reshape(count, 1), axis=0, keepdims=True))
    return jnp.concatenate(rows, axis=0)


def own_kernel(blocks, width, share, x_ref, z_ref, means_ref, owner_ref, local_ref, x_out, z_out, less_ref):
    effect = owner_ref[...] * PD_DEV + local_ref[...]

    def emit(a, picked):
        x_out[row_block(a), :] = x_ref[row_block(a), :] - picked

    z_out[...] = gather_half(effect, means_ref, effect_half(blocks) * (blocks * width), blocks, width, z_ref[...], emit)
    less_ref[: share + 1, :] = gram_less(means_ref, blocks, width, lax.axis_index(AXIS) * share, share)


def last_kernel(
    blocks, width, share, total_rows, x_ref, z_ref, means_ref, less_ref, mine_ref, got_ref, owner_ref, local_ref,
    x_hbm, z_hbm, gram_hbm, rhs_hbm, x_out, z_out, gram_out, rhs_out, sems,
):
    me = lax.axis_index(AXIS)
    core, high = core_index(), lax.div(me, 2 * blocks)
    first = me * share
    copies = []
    effect = owner_ref[...] * PD_DEV + local_ref[...]
    lines = effect.shape[0]
    chunk = max(1, lines // 4)

    def emit(a, picked):
        x_out[row_block(a), :] = x_ref[row_block(a), :] - picked
        if a % chunk == chunk - 1:
            span = slice((a + 1 - chunk) * LANES, (a + 1) * LANES)
            copies.append(pltpu.make_async_copy(x_out.at[span, :], x_hbm.at[span, :], sems.at[3 + a // chunk]))
            copies[-1].start()

    z_out[...] = gather_half(effect, means_ref, (1 - effect_half(blocks)) * (blocks * width), blocks, width, z_ref[...], emit)
    copies.append(pltpu.make_async_copy(z_out, z_hbm, sems.at[2]))
    copies[-1].start()
    less = gram_less(means_ref, blocks, width, first, share) + less_ref[: share + 1, :]
    total = mine_ref[...] + got_ref[...]
    high_rows = total.shape[0] - TILE
    gram = jnp.zeros((share, LANES), F32)
    for place in range(4):
        here = (high == place // 2) & (core == place % 2)
        gram = jnp.where(here, total[place * share : (place + 1) * share, :], gram)
    scale = 1.0 / total_rows
    gram_out[...] = (gram - less[:share, :]) * scale
    rhs = (total[high_rows : high_rows + 1, :] - less[share:, :]) * scale
    rhs_out[...] = pltpu.roll(rhs, lax.rem(LANES - first, LANES), 1)[:, :share]
    copies.append(pltpu.make_async_copy(gram_out, gram_hbm, sems.at[0]))
    copies.append(pltpu.make_async_copy(rhs_out, rhs_hbm, sems.at[1]))
    for copy in copies[-2:]:
        copy.start()
    for copy in copies:
        copy.wait()


VMEM = pl.BlockSpec(memory_space=pltpu.VMEM)
HBM = pl.BlockSpec(memory_space=pltpu.HBM)


def call(kernel, outs, args, scratch=(), flops=0, in_specs=None, out_specs=None):
    size = sum(math.prod(v.shape) * v.dtype.itemsize for v in list(args) + list(outs))
    return pl.pallas_call(
        kernel,
        out_shape=tuple(outs),
        in_specs=in_specs or [VMEM] * len(args),
        out_specs=tuple(out_specs or [VMEM] * len(outs)),
        scratch_shapes=scratch,
        cost_estimate=pl.CostEstimate(flops=flops, bytes_accessed=size, transcendentals=0),
        compiler_params=pltpu.CompilerParams(vmem_limit_bytes=VMEM_LIMIT),
    )(*args)


def in_hbm(v):
    return pltpu.with_memory_space_constraint(v, pltpu.HBM)


def shaped(*shape, dtype=F32):
    return jax.ShapeDtypeStruct(shape, dtype)


def rounded(rows):
    return -(-rows // TILE) * TILE


def shards(covariates, outcome, predictor, firm_id, dy_id, pd_owner, pd_local):
    rows, width = covariates.shape
    devices = lax.axis_size(AXIS)
    blocks = devices // 4
    share = width // devices
    total_rows = rows * devices
    dy_width, pd_width = DY // (2 * blocks), devices * PD_DEV // (2 * blocks)
    dy_high, pd_high = rounded(dy_width + 2), rounded(pd_width + 3)
    gram_high = rounded(4 * share)
    lines = rows // LANES
    groups = [
        [half * (devices // 2) + core_of + 2 * chip for chip in range(blocks)]
        for half in range(2)
        for core_of in range(2)
    ]
    partner = [(i, i ^ 1) for i in range(devices)]
    opposite = [(i, (i + devices // 2) % devices) for i in range(devices)]
    crossed = [(i, (i + devices // 2) % devices ^ 1) for i in range(devices)]
    outcome, predictor, firm, dy, owner, local = (
        v.reshape(lines, LANES) for v in (outcome, predictor, firm_id, dy_id, pd_owner, pd_local)
    )
    dy_half, pd_half = blocks * dy_width, blocks * pd_width

    def to_core(v):
        return lax.ppermute(v, AXIS, partner)

    def to_half(v, pairs):
        return lax.ppermute(v, AXIS, pairs)

    def across(v):
        return lax.all_to_all(v, AXIS, 0, 0, axis_index_groups=groups)

    def total_of(v):
        return call(total_kernel, (shaped(*v.shape[1:]),), (v,))[0]

    wide = 4 * rows * LANES
    count = min(4, lines)
    x1, z1, weight, dy, pairs, send = call(
        functools.partial(firm_kernel, blocks, dy_width),
        (
            shaped(rows, width),
            shaped(lines, LANES),
            shaped(lines, LANES),
            shaped(lines, LANES, dtype=I32),
            shaped(rows, 2 * LANES, dtype=BF16),
            shaped(blocks, dy_high, LANES),
        ),
        tuple(in_hbm(v) for v in (covariates, outcome, predictor, firm, dy)),
        scratch=(
            pltpu.VMEM((rows, width), F32),
            pltpu.VMEM((lines, LANES), F32),
            pltpu.VMEM((lines, LANES), F32),
            pltpu.VMEM((lines, LANES), I32),
            pltpu.SemaphoreType.DMA((4 + count,)),
        ),
        flops=wide * (dy_half + 2 * FIRM_DEV),
        in_specs=[HBM] * 5,
    )
    got = to_core(send)
    (keep,) = call(
        functools.partial(sums_kernel, blocks, dy_width),
        (shaped(blocks, dy_high, LANES),),
        (pairs, z1, weight, dy),
        flops=wide * dy_half,
    )
    mine = total_of(across(keep + got))
    (means,) = call(
        functools.partial(means_kernel, dy_width), (shaped(blocks, dy_high, LANES),), (mine, to_half(mine, opposite))
    )
    means = across(means)
    other = to_core(means)
    x1, z1 = call(
        functools.partial(gather_kernel, blocks, dy_width),
        (shaped(rows, width), shaped(lines, LANES)),
        (x1, z1, means, dy),
        flops=wide * dy_half,
    )
    x2, z2, pairs, send = call(
        functools.partial(effect_kernel, blocks, dy_width, pd_width),
        (
            shaped(rows, width),
            shaped(lines, LANES),
            shaped(rows, 2 * LANES, dtype=BF16),
            shaped(blocks, pd_high, LANES),
        ),
        (x1, z1, other, dy, weight, owner, local),
        flops=wide * (dy_half + pd_half),
    )
    got = to_core(send)
    keep, gram = call(
        functools.partial(gram_kernel, blocks, pd_width, share),
        (shaped(blocks, pd_high, LANES), shaped(blocks, gram_high, LANES)),
        (x2, z2, pairs, weight, owner, local),
        scratch=(pltpu.VMEM((rows, 2 * LANES), BF16),),
        flops=wide * (pd_half + 2 * LANES),
    )
    mine = total_of(across(jnp.concatenate([keep + got, gram], axis=1)))
    means, gram = call(
        functools.partial(means_kernel, pd_width),
        (shaped(blocks, pd_high, LANES), shaped(gram_high + TILE, LANES)),
        (mine, to_half(mine, crossed)),
    )
    got = to_core(gram)
    means = across(means)
    other = to_core(means)
    x3, z3, less = call(
        functools.partial(own_kernel, blocks, pd_width, share),
        (shaped(rows, width), shaped(lines, LANES), shaped(rounded(share + 1), LANES)),
        (x2, z2, means, owner, local),
        flops=wide * pd_half,
    )
    x3, z3, gram, rhs = call(
        functools.partial(last_kernel, blocks, pd_width, share, total_rows),
        (shaped(rows, width), shaped(lines, LANES), shaped(share, LANES), shaped(1, share)),
        (x3, z3, other, less, gram, got, owner, local),
        scratch=(
            pltpu.VMEM((rows, width), F32),
            pltpu.VMEM((lines, LANES), F32),
            pltpu.VMEM((share, LANES), F32),
            pltpu.VMEM((1, share), F32),
            pltpu.SemaphoreType.DMA((3 + count,)),
        ),
        flops=wide * pd_half,
        out_specs=[HBM] * 4,
    )
    return x3, z3.reshape(rows), gram, rhs.reshape(share)


def solution(mesh):
    in_specs = (
        P("rows", None),
        P("rows"),
        P("rows"),
        P("rows"),
        P("rows"),
        P("rows", None),
        P("rows"),
    )
    out_specs = (P("rows", None), P("rows"), P("rows", None), P("rows"))
    return jax.shard_map(shards, mesh=mesh, in_specs=in_specs, out_specs=out_specs, check_vma=False)
```

```python
import functools
import math

import jax
import jax.numpy as jnp
from jax import lax
from jax.experimental import pallas as pl
from jax.experimental.pallas import tpu as pltpu
from jax.sharding import PartitionSpec as P

DY = 2048
FIRM_DEV = 128
PD_DEV = 16
LANES = 128
TILE = 8
AXIS = "rows"
VMEM_LIMIT = 32 * 1024 * 1024

BF16 = jnp.bfloat16
F32 = jnp.float32
I32 = jnp.int32


def core_index():
    return lax.rem(lax.axis_index(AXIS), 2)


def effect_half(blocks):
    me = lax.axis_index(AXIS)
    return lax.rem(me + lax.div(me, 2 * blocks), 2)


def iota(shape, dim):
    return lax.broadcasted_iota(I32, shape, dim)


def dot(a, b):
    return jnp.dot(a, b, preferred_element_type=F32)


def dot_first(a, b):
    return lax.dot_general(a, b, (((0,), (0,)), ((), ())), preferred_element_type=F32)


def onehot(mask):
    return jnp.where(mask, 1.0, 0.0).astype(BF16)


def pieces(value, count):
    parts = []
    for _ in range(count):
        part = value.astype(BF16)
        parts.append(part)
        value = value - part.astype(F32)
    return parts


def pair(value):
    return jnp.concatenate(pieces(value, 2), axis=1)


def unpair(value):
    return value[:, :LANES] + value[:, LANES:]


def row_block(a):
    return slice(a * LANES, (a + 1) * LANES)


def weights_of(predictor, outcome):
    weight = jnp.exp(predictor)
    return weight, predictor + outcome / weight - 1.0


def scatter_half(ids, weight, working, pairs_ref, base, blocks, width, out_ref, group=16):
    lines = ids.shape[0]
    count = blocks * width
    step = math.gcd(count, 256)
    for first in range(0, count, step):
        labels = iota((step, LANES), 0) + (base + first)
        table = jnp.concatenate([onehot(labels == ids[a : a + 1, :]) for a in range(lines)], axis=1)
        sums = unpair(dot(table, pairs_ref[...]))
        out_ref[first // width : (first + step) // width, :width, :] = sums.reshape(
            step // width, width, LANES
        )
    block = lax.div(ids, I32(width))
    place = lax.rem(ids, I32(width))
    labels = iota((blocks, LANES), 0) + lax.div(base, I32(width))
    parts = [part.astype(F32) for part in pieces(weight, 3) + pieces(weight * working, 3)]
    sums = jnp.zeros((6 * blocks, width), F32)
    for a in range(0, lines, group):
        left, right = [], []
        for b in range(a, min(a + group, lines)):
            mask = labels == block[b : b + 1, :]
            left.append(jnp.concatenate([jnp.where(mask, part[b : b + 1, :], 0.0) for part in parts], axis=0))
            right.append(onehot(iota((width, LANES), 0) == place[b : b + 1, :]))
        left = jnp.concatenate(left, axis=1).astype(BF16)
        right = jnp.concatenate(right, axis=1)
        sums += lax.dot_general(left, right, (((1,), (1,)), ((), ())), preferred_element_type=F32)
    sums = [sums[i * blocks : (i + 1) * blocks, :] for i in range(6)]
    out_ref[:, width, :width] = sums[0] + sums[1] + sums[2]
    out_ref[:, width + 1, :width] = sums[3] + sums[4] + sums[5]
    spare = out_ref.shape[1] - width - 2
    if spare:
        out_ref[:, width + 2 :, :] = jnp.zeros((blocks, spare, LANES), F32)


def gather_half(ids, means_ref, base, blocks, width, z, emit):
    lines = ids.shape[0]
    count = blocks * width
    group = math.gcd(lines, 4)
    parts = jnp.concatenate([part.astype(F32) for part in pieces(means_ref[:, width + 1, :], 3)], axis=0)
    left = jnp.transpose(parts)[:width, :].astype(BF16)
    block = lax.div(ids, I32(width)) - lax.div(base, I32(width))
    place = lax.rem(ids, I32(width))
    table = pair(means_ref[:, :width, :].reshape(count, LANES))
    labels = iota((count, LANES), 0) + base
    z_new = []
    for a in range(0, lines, group):
        span = range(a, a + group)
        mask = jnp.concatenate([onehot(iota((blocks, LANES), 0) == block[b : b + 1, :]) for b in span], axis=1)
        candidates = dot(left, jnp.concatenate([mask, mask, mask], axis=0))
        for b in span:
            chosen = jnp.where(iota((width, LANES), 0) == place[b : b + 1, :], candidates[:, row_block(b - a)], 0.0)
            z_new.append(z[b : b + 1, :] - jnp.sum(chosen, axis=0, keepdims=True))
        mask = jnp.concatenate([onehot(labels == ids[b : b + 1, :]) for b in range(a, a + group)], axis=1)
        picked = unpair(dot_first(mask, table))
        for b in range(group):
            emit(a + b, picked[row_block(b), :])
    return jnp.concatenate(z_new, axis=0)


def firm_kernel(
    blocks, width, x_hbm, outcome_hbm, predictor_hbm, firm_hbm, dy_hbm,
    x1_ref, z1_ref, weight_ref, dy_ref, pairs_ref, out_ref, x_ref, outcome_ref, predictor_ref, firm_ref, sems,
):
    small = [(firm_hbm, firm_ref), (predictor_hbm, predictor_ref), (outcome_hbm, outcome_ref), (dy_hbm, dy_ref)]
    copies = [pltpu.make_async_copy(src, dst, sems.at[i]) for i, (src, dst) in enumerate(small)]
    count = firm_ref.shape[0]
    chunk = max(1, count // 4)
    starts = list(range(0, count, chunk))
    for i, a in enumerate(starts):
        span = slice(a * LANES, (a + chunk) * LANES)
        copies.append(pltpu.make_async_copy(x_hbm.at[span, :], x_ref.at[span, :], sems.at[len(small) + i]))
    for copy in copies:
        copy.start()
    for copy in copies[: len(small)]:
        copy.wait()
    firm = firm_ref[...]
    weight, working = weights_of(predictor_ref[...], outcome_ref[...])
    weight_ref[...] = weight
    weight_t = jnp.transpose(weight)
    group = math.gcd(count, 4)
    masks = [iota((FIRM_DEV, LANES), 0) == firm[a : a + 1, :] for a in range(count)]
    spread_w = jnp.zeros((FIRM_DEV, LANES), F32)
    spread_z = jnp.zeros((FIRM_DEV, LANES), F32)
    weighted = weight * working
    for a in range(count):
        spread_w += jnp.where(masks[a], weight[a : a + 1, :], 0.0)
        spread_z += jnp.where(masks[a], weighted[a : a + 1, :], 0.0)
    sum_w = jnp.sum(spread_w, axis=1, keepdims=True)
    sum_z = jnp.sum(spread_z, axis=1, keepdims=True)
    denominator = jnp.where(sum_w > 0.0, sum_w, 1.0)
    mean_z = sum_z / denominator
    table = jnp.concatenate([onehot(mask) for mask in masks], axis=1)
    for i, a in enumerate(starts):
        copies[len(small) + i].wait()
        if a == 0:
            offset = jnp.sum(x_ref[row_block(0), :], axis=0, keepdims=True) * (1.0 / LANES)
        for b in range(a, a + chunk):
            pairs_ref[row_block(b), :] = pair((x_ref[row_block(b), :] - offset) * weight_t[:, b : b + 1])
    mean_x = pair(unpair(dot(table, pairs_ref[...])) / denominator)
    z1 = []
    for a in range(count):
        if a % group == 0:
            picked = unpair(dot_first(table[:, a * LANES : (a + group) * LANES], mean_x))
        x1 = (x_ref[row_block(a), :] - offset) - picked[row_block(a % group), :]
        x1_ref[row_block(a), :] = x1
        pairs_ref[row_block(a), :] = pair(x1 * weight_t[:, a : a + 1])
        picked_z = jnp.sum(jnp.where(masks[a], mean_z, 0.0), axis=0, keepdims=True)
        z1.append(working[a : a + 1, :] - picked_z)
    z1 = jnp.concatenate(z1, axis=0)
    z1_ref[...] = z1
    dy = dy_ref[...]
    scatter_half(dy, weight, z1, pairs_ref, (1 - core_index()) * (blocks * width), blocks, width, out_ref)


def sums_kernel(blocks, width, pairs_ref, z1_ref, weight_ref, dy_ref, out_ref):
    dy = dy_ref[...]
    scatter_half(dy, weight_ref[...], z1_ref[...], pairs_ref, core_index() * (blocks * width), blocks, width, out_ref)


def total_kernel(in_ref, out_ref):
    total = in_ref[0]
    for j in range(1, in_ref.shape[0]):
        total = total + in_ref[j]
    out_ref[...] = total


def means_kernel(width, share, mine_ref, got_ref, out_ref, *rest_ref):
    total = mine_ref[...] + got_ref[...]
    line_w = total[width : width + 1, :]
    line_z = total[width + 1 : width + 2, :]
    diagonal = iota((width, LANES), 0) == iota((width, LANES), 1)
    sum_w = jnp.sum(jnp.where(diagonal, line_w, 0.0), axis=1, keepdims=True)
    mean_x = total[:width, :] / jnp.where(sum_w > 0.0, sum_w, 1.0)
    mean_z = line_z / jnp.where(line_w > 0.0, line_w, 1.0)
    height = out_ref.shape[1]
    rest = jnp.zeros((height - width - 2, LANES), F32)
    if rest_ref:
        core, high = core_index(), lax.div(lax.axis_index(AXIS), 2 * out_ref.shape[0])
        own = jnp.zeros((share, LANES), F32)
        other = jnp.zeros((share, LANES), F32)
        for place in range(4):
            rows = total[height + place * share : height + (place + 1) * share, :]
            own = jnp.where((high == place // 2) & (core == place % 2), rows, own)
            other = jnp.where((high == place // 2) & (core != place % 2), rows, other)
        rhs = total[width + 2 : width + 3, :]
        rest_ref[0][: share + 1, :] = jnp.concatenate([own, rhs], axis=0)
        rest = jnp.concatenate([other, rhs, rest[share + 1 :, :]], axis=0)
    result = jnp.concatenate([mean_x, line_w, mean_z, rest], axis=0)
    for j in range(out_ref.shape[0]):
        out_ref[j] = result


def gather_kernel(blocks, width, x_ref, z_ref, means_ref, dy_ref, x_out, z_out):
    def emit(a, picked):
        x_out[row_block(a), :] = x_ref[row_block(a), :] - picked

    base = core_index() * (blocks * width)
    z_out[...] = gather_half(dy_ref[...], means_ref, base, blocks, width, z_ref[...], emit)


def effect_kernel(
    blocks, width, pd_width, x_ref, z_ref, means_ref, dy_ref, weight_ref, owner_ref, local_ref,
    x2_ref, z2_ref, weighted_ref, send_ref,
):
    dy = dy_ref[...]
    weight = weight_ref[...]
    weight_t = jnp.transpose(weight)

    def emit(a, picked):
        x2 = x_ref[row_block(a), :] - picked
        x2_ref[row_block(a), :] = x2
        weighted_ref[row_block(a), :] = pair(x2 * weight_t[:, a : a + 1])

    z2 = gather_half(dy, means_ref, (1 - core_index()) * (blocks * width), blocks, width, z_ref[...], emit)
    z2_ref[...] = z2
    effect = owner_ref[...] * PD_DEV + local_ref[...]
    scatter_half(
        effect, weight, z2, weighted_ref, (1 - effect_half(blocks)) * (blocks * pd_width), blocks, pd_width, send_ref
    )


def gram_kernel(
    blocks, pd_width, share, x2_ref, z2_ref, weighted_ref, weight_ref, owner_ref, local_ref,
    keep_ref, gram_ref, plain_ref,
):
    weight = weight_ref[...]
    z2 = z2_ref[...]
    lines = z2.shape[0]
    effect = owner_ref[...] * PD_DEV + local_ref[...]
    scatter_half(
        effect, weight, z2, weighted_ref, effect_half(blocks) * (blocks * pd_width), blocks, pd_width, keep_ref
    )
    for a in range(lines):
        plain_ref[row_block(a), :] = pair(x2_ref[row_block(a), :])
    gram = dot_first(weighted_ref[...], plain_ref[...])
    gram = unpair(gram[:LANES, :] + gram[LANES:, :])
    left = [part.astype(F32) for part in pieces(weight * z2, 3)]
    none = jnp.zeros((TILE - 3, LANES), F32)
    left = jnp.concatenate(
        [jnp.concatenate([part[a : a + 1, :] for part in left] + [none], axis=0) for a in range(lines)], axis=1
    )
    rhs = unpair(jnp.sum(dot(left.astype(BF16), plain_ref[...]), axis=0, keepdims=True))
    keep_ref[:, pd_width + 2, :] = jnp.broadcast_to(rhs, (blocks, LANES))
    half = blocks * 2 * share
    for j in range(blocks):
        low = gram[2 * j * share : 2 * (j + 1) * share, :]
        high = gram[half + 2 * j * share : half + 2 * (j + 1) * share, :]
        gram_ref[j, : 4 * share, :] = jnp.concatenate([low, high], axis=0)


def gram_less(means_ref, blocks, width, first, share):
    count = blocks * width
    diagonal = iota((blocks, width, LANES), 2) == iota((blocks, width, LANES), 1)
    sum_w = jnp.sum(jnp.where(diagonal, means_ref[:, width, :][:, None, :], 0.0), axis=2, keepdims=True)
    mean_z = jnp.sum(jnp.where(diagonal, means_ref[:, width + 1, :][:, None, :], 0.0), axis=2, keepdims=True)
    mean_x = means_ref[:, :width, :].reshape(count, LANES)
    sum_x = mean_x * sum_w.reshape(count, 1)
    lane = iota((count, LANES), 1)
    rows = []
    for i in range(share):
        column = jnp.sum(jnp.where(lane == first + i, sum_x, 0.0), axis=1, keepdims=True)
        rows.append(jnp.sum(column * mean_x, axis=0, keepdims=True))
    rows.append(jnp.sum(sum_x * mean_z.reshape(count, 1), axis=0, keepdims=True))
    return jnp.concatenate(rows, axis=0)


def own_kernel(blocks, width, share, x_ref, z_ref, means_ref, owner_ref, local_ref, x_out, z_out, less_ref):
    effect = owner_ref[...] * PD_DEV + local_ref[...]

    def emit(a, picked):
        x_out[row_block(a), :] = x_ref[row_block(a), :] - picked

    z_out[...] = gather_half(effect, means_ref, effect_half(blocks) * (blocks * width), blocks, width, z_ref[...], emit)
    less_ref[: share + 1, :] = gram_less(means_ref, blocks, width, lax.axis_index(AXIS) * share, share)


def last_kernel(
    blocks, width, share, total_rows, x_ref, z_ref, means_ref, less_ref, mine_ref, owner_ref, local_ref,
    x_hbm, z_hbm, gram_hbm, rhs_hbm, x_out, z_out, gram_out, rhs_out, sems,
):
    me = lax.axis_index(AXIS)
    first = me * share
    copies = []
    effect = owner_ref[...] * PD_DEV + local_ref[...]
    lines = effect.shape[0]
    chunk = max(1, lines // 4)

    def emit(a, picked):
        x_out[row_block(a), :] = x_ref[row_block(a), :] - picked
        if a % chunk == chunk - 1:
            span = slice((a + 1 - chunk) * LANES, (a + 1) * LANES)
            copies.append(pltpu.make_async_copy(x_out.at[span, :], x_hbm.at[span, :], sems.at[3 + a // chunk]))
            copies[-1].start()

    z_out[...] = gather_half(effect, means_ref, (1 - effect_half(blocks)) * (blocks * width), blocks, width, z_ref[...], emit)
    copies.append(pltpu.make_async_copy(z_out, z_hbm, sems.at[2]))
    copies[-1].start()
    less = gram_less(means_ref, blocks, width, first, share) + less_ref[: share + 1, :]
    chip = lax.rem(lax.div(me, 2), blocks)
    got = means_ref[pl.ds(chip, 1), width + 2 : width + 3 + share, :].reshape(share + 1, LANES)
    total = mine_ref[: share + 1, :] + got
    scale = 1.0 / total_rows
    gram_out[...] = (total[:share, :] - less[:share, :]) * scale
    rhs = (total[share:, :] - less[share:, :]) * scale
    rhs_out[...] = pltpu.roll(rhs, lax.rem(LANES - first, LANES), 1)[:, :share]
    copies.append(pltpu.make_async_copy(gram_out, gram_hbm, sems.at[0]))
    copies.append(pltpu.make_async_copy(rhs_out, rhs_hbm, sems.at[1]))
    for copy in copies[-2:]:
        copy.start()
    for copy in copies:
        copy.wait()


VMEM = pl.BlockSpec(memory_space=pltpu.VMEM)
HBM = pl.BlockSpec(memory_space=pltpu.HBM)


def call(kernel, outs, args, scratch=(), flops=0, in_specs=None, out_specs=None):
    size = sum(math.prod(v.shape) * v.dtype.itemsize for v in list(args) + list(outs))
    return pl.pallas_call(
        kernel,
        out_shape=tuple(outs),
        in_specs=in_specs or [VMEM] * len(args),
        out_specs=tuple(out_specs or [VMEM] * len(outs)),
        scratch_shapes=scratch,
        cost_estimate=pl.CostEstimate(flops=flops, bytes_accessed=size, transcendentals=0),
        compiler_params=pltpu.CompilerParams(vmem_limit_bytes=VMEM_LIMIT),
    )(*args)


def in_hbm(v):
    return pltpu.with_memory_space_constraint(v, pltpu.HBM)


def shaped(*shape, dtype=F32):
    return jax.ShapeDtypeStruct(shape, dtype)


def rounded(rows):
    return -(-rows // TILE) * TILE


def shards(covariates, outcome, predictor, firm_id, dy_id, pd_owner, pd_local):
    rows, width = covariates.shape
    devices = lax.axis_size(AXIS)
    blocks = devices // 4
    share = width // devices
    total_rows = rows * devices
    dy_width, pd_width = DY // (2 * blocks), devices * PD_DEV // (2 * blocks)
    dy_high, pd_high = rounded(dy_width + 2), rounded(pd_width + 3 + share)
    gram_high = rounded(4 * share)
    lines = rows // LANES
    groups = [
        [half * (devices // 2) + core_of + 2 * chip for chip in range(blocks)]
        for half in range(2)
        for core_of in range(2)
    ]
    partner = [(i, i ^ 1) for i in range(devices)]
    opposite = [(i, (i + devices // 2) % devices) for i in range(devices)]
    crossed = [(i, (i + devices // 2) % devices ^ 1) for i in range(devices)]
    outcome, predictor, firm, dy, owner, local = (
        v.reshape(lines, LANES) for v in (outcome, predictor, firm_id, dy_id, pd_owner, pd_local)
    )
    dy_half, pd_half = blocks * dy_width, blocks * pd_width

    def to_core(v):
        return lax.ppermute(v, AXIS, partner)

    def to_half(v, pairs):
        return lax.ppermute(v, AXIS, pairs)

    def across(v):
        return lax.all_to_all(v, AXIS, 0, 0, axis_index_groups=groups)

    def total_of(v):
        return call(total_kernel, (shaped(*v.shape[1:]),), (v,))[0]

    wide = 4 * rows * LANES
    count = min(4, lines)
    x1, z1, weight, dy, pairs, send = call(
        functools.partial(firm_kernel, blocks, dy_width),
        (
            shaped(rows, width),
            shaped(lines, LANES),
            shaped(lines, LANES),
            shaped(lines, LANES, dtype=I32),
            shaped(rows, 2 * LANES, dtype=BF16),
            shaped(blocks, dy_high, LANES),
        ),
        tuple(in_hbm(v) for v in (covariates, outcome, predictor, firm, dy)),
        scratch=(
            pltpu.VMEM((rows, width), F32),
            pltpu.VMEM((lines, LANES), F32),
            pltpu.VMEM((lines, LANES), F32),
            pltpu.VMEM((lines, LANES), I32),
            pltpu.SemaphoreType.DMA((4 + count,)),
        ),
        flops=wide * (dy_half + 2 * FIRM_DEV),
        in_specs=[HBM] * 5,
    )
    got = to_core(send)
    (keep,) = call(
        functools.partial(sums_kernel, blocks, dy_width),
        (shaped(blocks, dy_high, LANES),),
        (pairs, z1, weight, dy),
        flops=wide * dy_half,
    )
    mine = total_of(across(keep + got))
    (means,) = call(
        functools.partial(means_kernel, dy_width, share), (shaped(blocks, dy_high, LANES),), (mine, to_half(mine, opposite))
    )
    means = across(means)
    other = to_core(means)
    x1, z1 = call(
        functools.partial(gather_kernel, blocks, dy_width),
        (shaped(rows, width), shaped(lines, LANES)),
        (x1, z1, means, dy),
        flops=wide * dy_half,
    )
    x2, z2, pairs, send = call(
        functools.partial(effect_kernel, blocks, dy_width, pd_width),
        (
            shaped(rows, width),
            shaped(lines, LANES),
            shaped(rows, 2 * LANES, dtype=BF16),
            shaped(blocks, pd_high, LANES),
        ),
        (x1, z1, other, dy, weight, owner, local),
        flops=wide * (dy_half + pd_half),
    )
    got = to_core(send)
    keep, gram = call(
        functools.partial(gram_kernel, blocks, pd_width, share),
        (shaped(blocks, pd_high, LANES), shaped(blocks, gram_high, LANES)),
        (x2, z2, pairs, weight, owner, local),
        scratch=(pltpu.VMEM((rows, 2 * LANES), BF16),),
        flops=wide * (pd_half + 2 * LANES),
    )
    mine = total_of(across(jnp.concatenate([keep + got, gram], axis=1)))
    means, gram = call(
        functools.partial(means_kernel, pd_width, share),
        (shaped(blocks, pd_high, LANES), shaped(rounded(share + 1), LANES)),
        (mine, to_half(mine, crossed)),
    )
    means = across(means)
    other = to_core(means)
    x3, z3, less = call(
        functools.partial(own_kernel, blocks, pd_width, share),
        (shaped(rows, width), shaped(lines, LANES), shaped(rounded(share + 1), LANES)),
        (x2, z2, means, owner, local),
        flops=wide * pd_half,
    )
    x3, z3, gram, rhs = call(
        functools.partial(last_kernel, blocks, pd_width, share, total_rows),
        (shaped(rows, width), shaped(lines, LANES), shaped(share, LANES), shaped(1, share)),
        (x3, z3, other, less, gram, owner, local),
        scratch=(
            pltpu.VMEM((rows, width), F32),
            pltpu.VMEM((lines, LANES), F32),
            pltpu.VMEM((share, LANES), F32),
            pltpu.VMEM((1, share), F32),
            pltpu.SemaphoreType.DMA((3 + count,)),
        ),
        flops=wide * pd_half,
        out_specs=[HBM] * 4,
    )
    return x3, z3.reshape(rows), gram, rhs.reshape(share)


def solution(mesh):
    in_specs = (
        P("rows", None),
        P("rows"),
        P("rows"),
        P("rows"),
        P("rows"),
        P("rows", None),
        P("rows"),
    )
    out_specs = (P("rows", None), P("rows"), P("rows", None), P("rows"))
    return jax.shard_map(shards, mesh=mesh, in_specs=in_specs, out_specs=out_specs, check_vma=False)
```

```python
import functools
import math

import jax
import jax.numpy as jnp
from jax import lax
from jax.experimental import pallas as pl
from jax.experimental.pallas import tpu as pltpu
from jax.sharding import PartitionSpec as P

DY = 2048
FIRM_DEV = 128
PD_DEV = 16
LANES = 128
TILE = 8
AXIS = "rows"
VMEM_LIMIT = 32 * 1024 * 1024

BF16 = jnp.bfloat16
F32 = jnp.float32
I32 = jnp.int32


def core_index():
    return lax.rem(lax.axis_index(AXIS), 2)


def effect_half(blocks):
    me = lax.axis_index(AXIS)
    return lax.rem(me + lax.div(me, 2 * blocks), 2)


def iota(shape, dim):
    return lax.broadcasted_iota(I32, shape, dim)


def dot(a, b):
    return jnp.dot(a, b, preferred_element_type=F32)


def dot_first(a, b):
    return lax.dot_general(a, b, (((0,), (0,)), ((), ())), preferred_element_type=F32)


def onehot(mask):
    return jnp.where(mask, 1.0, 0.0).astype(BF16)


def pieces(value, count):
    parts = []
    for _ in range(count):
        part = value.astype(BF16)
        parts.append(part)
        value = value - part.astype(F32)
    return parts


def pair(value):
    return jnp.concatenate(pieces(value, 2), axis=1)


def unpair(value):
    return value[:, :LANES] + value[:, LANES:]


def row_block(a):
    return slice(a * LANES, (a + 1) * LANES)


def weights_of(predictor, outcome):
    weight = jnp.exp(predictor)
    return weight, predictor + outcome / weight - 1.0


def scatter_half(ids, weight, working, pairs_ref, base, blocks, width, out_ref, group=16):
    lines = ids.shape[0]
    count = blocks * width
    step = math.gcd(count, 256)
    for first in range(0, count, step):
        labels = iota((step, LANES), 0) + (base + first)
        table = jnp.concatenate([onehot(labels == ids[a : a + 1, :]) for a in range(lines)], axis=1)
        sums = unpair(dot(table, pairs_ref[...]))
        out_ref[first // width : (first + step) // width, :width, :] = sums.reshape(
            step // width, width, LANES
        )
    block = lax.div(ids, I32(width))
    place = lax.rem(ids, I32(width))
    labels = iota((blocks, LANES), 0) + lax.div(base, I32(width))
    parts = [part.astype(F32) for part in pieces(weight, 3) + pieces(weight * working, 3)]
    sums = jnp.zeros((6 * blocks, width), F32)
    for a in range(0, lines, group):
        left, right = [], []
        for b in range(a, min(a + group, lines)):
            mask = labels == block[b : b + 1, :]
            left.append(jnp.concatenate([jnp.where(mask, part[b : b + 1, :], 0.0) for part in parts], axis=0))
            right.append(onehot(iota((width, LANES), 0) == place[b : b + 1, :]))
        left = jnp.concatenate(left, axis=1).astype(BF16)
        right = jnp.concatenate(right, axis=1)
        sums += lax.dot_general(left, right, (((1,), (1,)), ((), ())), preferred_element_type=F32)
    sums = [sums[i * blocks : (i + 1) * blocks, :] for i in range(6)]
    out_ref[:, width, :width] = sums[0] + sums[1] + sums[2]
    out_ref[:, width + 1, :width] = sums[3] + sums[4] + sums[5]
    spare = out_ref.shape[1] - width - 2
    if spare:
        out_ref[:, width + 2 :, :] = jnp.zeros((blocks, spare, LANES), F32)


def gather_half(ids, means_ref, base, blocks, width, z, emit):
    lines = ids.shape[0]
    count = blocks * width
    group = math.gcd(lines, 4)
    parts = jnp.concatenate([part.astype(F32) for part in pieces(means_ref[:, width + 1, :], 3)], axis=0)
    left = jnp.transpose(parts)[:width, :].astype(BF16)
    block = lax.div(ids, I32(width)) - lax.div(base, I32(width))
    place = lax.rem(ids, I32(width))
    table = pair(means_ref[:, :width, :].reshape(count, LANES))
    labels = iota((count, LANES), 0) + base
    z_new = []
    for a in range(0, lines, group):
        span = range(a, a + group)
        mask = jnp.concatenate([onehot(iota((blocks, LANES), 0) == block[b : b + 1, :]) for b in span], axis=1)
        candidates = dot(left, jnp.concatenate([mask, mask, mask], axis=0))
        for b in span:
            chosen = jnp.where(iota((width, LANES), 0) == place[b : b + 1, :], candidates[:, row_block(b - a)], 0.0)
            z_new.append(z[b : b + 1, :] - jnp.sum(chosen, axis=0, keepdims=True))
        mask = jnp.concatenate([onehot(labels == ids[b : b + 1, :]) for b in range(a, a + group)], axis=1)
        picked = unpair(dot_first(mask, table))
        for b in range(group):
            emit(a + b, picked[row_block(b), :])
    return jnp.concatenate(z_new, axis=0)


def firm_kernel(
    blocks, width, x_hbm, outcome_hbm, predictor_hbm, firm_hbm, dy_hbm,
    x1_ref, z1_ref, weight_ref, dy_ref, pairs_ref, out_ref, x_ref, outcome_ref, predictor_ref, firm_ref, sems,
):
    small = [(firm_hbm, firm_ref), (predictor_hbm, predictor_ref), (outcome_hbm, outcome_ref), (dy_hbm, dy_ref)]
    copies = [pltpu.make_async_copy(src, dst, sems.at[i]) for i, (src, dst) in enumerate(small)]
    count = firm_ref.shape[0]
    chunk = max(1, count // 2)
    starts = list(range(0, count, chunk))
    for i, a in enumerate(starts):
        span = slice(a * LANES, (a + chunk) * LANES)
        copies.append(pltpu.make_async_copy(x_hbm.at[span, :], x_ref.at[span, :], sems.at[len(small) + i]))
    for copy in copies:
        copy.start()
    for copy in copies[: len(small)]:
        copy.wait()
    firm = firm_ref[...]
    weight, working = weights_of(predictor_ref[...], outcome_ref[...])
    weight_ref[...] = weight
    weight_t = jnp.transpose(weight)
    group = math.gcd(count, 4)
    masks = [iota((FIRM_DEV, LANES), 0) == firm[a : a + 1, :] for a in range(count)]
    spread_w = jnp.zeros((FIRM_DEV, LANES), F32)
    spread_z = jnp.zeros((FIRM_DEV, LANES), F32)
    weighted = weight * working
    for a in range(count):
        spread_w += jnp.where(masks[a], weight[a : a + 1, :], 0.0)
        spread_z += jnp.where(masks[a], weighted[a : a + 1, :], 0.0)
    sum_w = jnp.sum(spread_w, axis=1, keepdims=True)
    sum_z = jnp.sum(spread_z, axis=1, keepdims=True)
    denominator = jnp.where(sum_w > 0.0, sum_w, 1.0)
    mean_z = sum_z / denominator
    table = jnp.concatenate([onehot(mask) for mask in masks], axis=1)
    for i, a in enumerate(starts):
        copies[len(small) + i].wait()
        if a == 0:
            offset = jnp.sum(x_ref[row_block(0), :], axis=0, keepdims=True) * (1.0 / LANES)
        for b in range(a, a + chunk):
            pairs_ref[row_block(b), :] = pair((x_ref[row_block(b), :] - offset) * weight_t[:, b : b + 1])
    mean_x = pair(unpair(dot(table, pairs_ref[...])) / denominator)
    z1 = []
    for a in range(count):
        if a % group == 0:
            picked = unpair(dot_first(table[:, a * LANES : (a + group) * LANES], mean_x))
        x1 = (x_ref[row_block(a), :] - offset) - picked[row_block(a % group), :]
        x1_ref[row_block(a), :] = x1
        pairs_ref[row_block(a), :] = pair(x1 * weight_t[:, a : a + 1])
        picked_z = jnp.sum(jnp.where(masks[a], mean_z, 0.0), axis=0, keepdims=True)
        z1.append(working[a : a + 1, :] - picked_z)
    z1 = jnp.concatenate(z1, axis=0)
    z1_ref[...] = z1
    dy = dy_ref[...]
    scatter_half(dy, weight, z1, pairs_ref, (1 - core_index()) * (blocks * width), blocks, width, out_ref)


def sums_kernel(blocks, width, pairs_ref, z1_ref, weight_ref, dy_ref, out_ref):
    dy = dy_ref[...]
    scatter_half(dy, weight_ref[...], z1_ref[...], pairs_ref, core_index() * (blocks * width), blocks, width, out_ref)


def total_kernel(in_ref, out_ref):
    total = in_ref[0]
    for j in range(1, in_ref.shape[0]):
        total = total + in_ref[j]
    out_ref[...] = total


def means_kernel(width, share, mine_ref, got_ref, out_ref, *rest_ref):
    total = mine_ref[...] + got_ref[...]
    line_w = total[width : width + 1, :]
    line_z = total[width + 1 : width + 2, :]
    diagonal = iota((width, LANES), 0) == iota((width, LANES), 1)
    sum_w = jnp.sum(jnp.where(diagonal, line_w, 0.0), axis=1, keepdims=True)
    mean_x = total[:width, :] / jnp.where(sum_w > 0.0, sum_w, 1.0)
    mean_z = line_z / jnp.where(line_w > 0.0, line_w, 1.0)
    height = out_ref.shape[1]
    rest = jnp.zeros((height - width - 2, LANES), F32)
    if rest_ref:
        core, high = core_index(), lax.div(lax.axis_index(AXIS), 2 * out_ref.shape[0])
        own = jnp.zeros((share, LANES), F32)
        other = jnp.zeros((share, LANES), F32)
        for place in range(4):
            rows = total[height + place * share : height + (place + 1) * share, :]
            own = jnp.where((high == place // 2) & (core == place % 2), rows, own)
            other = jnp.where((high == place // 2) & (core != place % 2), rows, other)
        rhs = total[width + 2 : width + 3, :]
        rest_ref[0][: share + 1, :] = jnp.concatenate([own, rhs], axis=0)
        rest = jnp.concatenate([other, rhs, rest[share + 1 :, :]], axis=0)
    result = jnp.concatenate([mean_x, line_w, mean_z, rest], axis=0)
    for j in range(out_ref.shape[0]):
        out_ref[j] = result


def gather_kernel(blocks, width, x_ref, z_ref, means_ref, dy_ref, x_out, z_out):
    def emit(a, picked):
        x_out[row_block(a), :] = x_ref[row_block(a), :] - picked

    base = core_index() * (blocks * width)
    z_out[...] = gather_half(dy_ref[...], means_ref, base, blocks, width, z_ref[...], emit)


def effect_kernel(
    blocks, width, pd_width, x_ref, z_ref, means_ref, dy_ref, weight_ref, owner_ref, local_ref,
    x2_ref, z2_ref, weighted_ref, send_ref,
):
    dy = dy_ref[...]
    weight = weight_ref[...]
    weight_t = jnp.transpose(weight)

    def emit(a, picked):
        x2 = x_ref[row_block(a), :] - picked
        x2_ref[row_block(a), :] = x2
        weighted_ref[row_block(a), :] = pair(x2 * weight_t[:, a : a + 1])

    z2 = gather_half(dy, means_ref, (1 - core_index()) * (blocks * width), blocks, width, z_ref[...], emit)
    z2_ref[...] = z2
    effect = owner_ref[...] * PD_DEV + local_ref[...]
    scatter_half(
        effect, weight, z2, weighted_ref, (1 - effect_half(blocks)) * (blocks * pd_width), blocks, pd_width, send_ref
    )


def gram_kernel(
    blocks, pd_width, share, x2_ref, z2_ref, weighted_ref, weight_ref, owner_ref, local_ref,
    keep_ref, gram_ref, plain_ref,
):
    weight = weight_ref[...]
    z2 = z2_ref[...]
    lines = z2.shape[0]
    effect = owner_ref[...] * PD_DEV + local_ref[...]
    scatter_half(
        effect, weight, z2, weighted_ref, effect_half(blocks) * (blocks * pd_width), blocks, pd_width, keep_ref
    )
    for a in range(lines):
        plain_ref[row_block(a), :] = pair(x2_ref[row_block(a), :])
    gram = dot_first(weighted_ref[...], plain_ref[...])
    gram = unpair(gram[:LANES, :] + gram[LANES:, :])
    left = [part.astype(F32) for part in pieces(weight * z2, 3)]
    none = jnp.zeros((TILE - 3, LANES), F32)
    left = jnp.concatenate(
        [jnp.concatenate([part[a : a + 1, :] for part in left] + [none], axis=0) for a in range(lines)], axis=1
    )
    rhs = unpair(jnp.sum(dot(left.astype(BF16), plain_ref[...]), axis=0, keepdims=True))
    keep_ref[:, pd_width + 2, :] = jnp.broadcast_to(rhs, (blocks, LANES))
    half = blocks * 2 * share
    for j in range(blocks):
        low = gram[2 * j * share : 2 * (j + 1) * share, :]
        high = gram[half + 2 * j * share : half + 2 * (j + 1) * share, :]
        gram_ref[j, : 4 * share, :] = jnp.concatenate([low, high], axis=0)


def gram_less(means_ref, blocks, width, first, share):
    count = blocks * width
    diagonal = iota((blocks, width, LANES), 2) == iota((blocks, width, LANES), 1)
    sum_w = jnp.sum(jnp.where(diagonal, means_ref[:, width, :][:, None, :], 0.0), axis=2, keepdims=True)
    mean_z = jnp.sum(jnp.where(diagonal, means_ref[:, width + 1, :][:, None, :], 0.0), axis=2, keepdims=True)
    mean_x = means_ref[:, :width, :].reshape(count, LANES)
    sum_x = mean_x * sum_w.reshape(count, 1)
    lane = iota((count, LANES), 1)
    rows = []
    for i in range(share):
        column = jnp.sum(jnp.where(lane == first + i, sum_x, 0.0), axis=1, keepdims=True)
        rows.append(jnp.sum(column * mean_x, axis=0, keepdims=True))
    rows.append(jnp.sum(sum_x * mean_z.reshape(count, 1), axis=0, keepdims=True))
    return jnp.concatenate(rows, axis=0)


def own_kernel(blocks, width, share, x_ref, z_ref, means_ref, owner_ref, local_ref, x_out, z_out, less_ref):
    effect = owner_ref[...] * PD_DEV + local_ref[...]

    def emit(a, picked):
        x_out[row_block(a), :] = x_ref[row_block(a), :] - picked

    z_out[...] = gather_half(effect, means_ref, effect_half(blocks) * (blocks * width), blocks, width, z_ref[...], emit)
    less_ref[: share + 1, :] = gram_less(means_ref, blocks, width, lax.axis_index(AXIS) * share, share)


def last_kernel(
    blocks, width, share, total_rows, x_ref, z_ref, means_ref, less_ref, mine_ref, owner_ref, local_ref,
    x_hbm, z_hbm, gram_hbm, rhs_hbm, x_out, z_out, gram_out, rhs_out, sems,
):
    me = lax.axis_index(AXIS)
    first = me * share
    copies = []
    effect = owner_ref[...] * PD_DEV + local_ref[...]
    lines = effect.shape[0]
    chunk = max(1, lines // 4)

    def emit(a, picked):
        x_out[row_block(a), :] = x_ref[row_block(a), :] - picked
        if a % chunk == chunk - 1:
            span = slice((a + 1 - chunk) * LANES, (a + 1) * LANES)
            copies.append(pltpu.make_async_copy(x_out.at[span, :], x_hbm.at[span, :], sems.at[3 + a // chunk]))
            copies[-1].start()

    z_out[...] = gather_half(effect, means_ref, (1 - effect_half(blocks)) * (blocks * width), blocks, width, z_ref[...], emit)
    copies.append(pltpu.make_async_copy(z_out, z_hbm, sems.at[2]))
    copies[-1].start()
    less = gram_less(means_ref, blocks, width, first, share) + less_ref[: share + 1, :]
    chip = lax.rem(lax.div(me, 2), blocks)
    got = means_ref[pl.ds(chip, 1), width + 2 : width + 3 + share, :].reshape(share + 1, LANES)
    total = mine_ref[: share + 1, :] + got
    scale = 1.0 / total_rows
    gram_out[...] = (total[:share, :] - less[:share, :]) * scale
    rhs = (total[share:, :] - less[share:, :]) * scale
    rhs_out[...] = pltpu.roll(rhs, lax.rem(LANES - first, LANES), 1)[:, :share]
    copies.append(pltpu.make_async_copy(gram_out, gram_hbm, sems.at[0]))
    copies.append(pltpu.make_async_copy(rhs_out, rhs_hbm, sems.at[1]))
    for copy in copies[-2:]:
        copy.start()
    for copy in copies:
        copy.wait()


VMEM = pl.BlockSpec(memory_space=pltpu.VMEM)
HBM = pl.BlockSpec(memory_space=pltpu.HBM)


def call(kernel, outs, args, scratch=(), flops=0, in_specs=None, out_specs=None):
    size = sum(math.prod(v.shape) * v.dtype.itemsize for v in list(args) + list(outs))
    return pl.pallas_call(
        kernel,
        out_shape=tuple(outs),
        in_specs=in_specs or [VMEM] * len(args),
        out_specs=tuple(out_specs or [VMEM] * len(outs)),
        scratch_shapes=scratch,
        cost_estimate=pl.CostEstimate(flops=flops, bytes_accessed=size, transcendentals=0),
        compiler_params=pltpu.CompilerParams(vmem_limit_bytes=VMEM_LIMIT),
    )(*args)


def in_hbm(v):
    return pltpu.with_memory_space_constraint(v, pltpu.HBM)


def shaped(*shape, dtype=F32):
    return jax.ShapeDtypeStruct(shape, dtype)


def rounded(rows):
    return -(-rows // TILE) * TILE


def shards(covariates, outcome, predictor, firm_id, dy_id, pd_owner, pd_local):
    rows, width = covariates.shape
    devices = lax.axis_size(AXIS)
    blocks = devices // 4
    share = width // devices
    total_rows = rows * devices
    dy_width, pd_width = DY // (2 * blocks), devices * PD_DEV // (2 * blocks)
    dy_high, pd_high = rounded(dy_width + 2), rounded(pd_width + 3 + share)
    gram_high = rounded(4 * share)
    lines = rows // LANES
    groups = [
        [half * (devices // 2) + core_of + 2 * chip for chip in range(blocks)]
        for half in range(2)
        for core_of in range(2)
    ]
    partner = [(i, i ^ 1) for i in range(devices)]
    opposite = [(i, (i + devices // 2) % devices) for i in range(devices)]
    crossed = [(i, (i + devices // 2) % devices ^ 1) for i in range(devices)]
    outcome, predictor, firm, dy, owner, local = (
        v.reshape(lines, LANES) for v in (outcome, predictor, firm_id, dy_id, pd_owner, pd_local)
    )
    dy_half, pd_half = blocks * dy_width, blocks * pd_width

    def to_core(v):
        return lax.ppermute(v, AXIS, partner)

    def to_half(v, pairs):
        return lax.ppermute(v, AXIS, pairs)

    def across(v):
        return lax.all_to_all(v, AXIS, 0, 0, axis_index_groups=groups)

    def total_of(v):
        return call(total_kernel, (shaped(*v.shape[1:]),), (v,))[0]

    wide = 4 * rows * LANES
    count = min(4, lines)
    x1, z1, weight, dy, pairs, send = call(
        functools.partial(firm_kernel, blocks, dy_width),
        (
            shaped(rows, width),
            shaped(lines, LANES),
            shaped(lines, LANES),
            shaped(lines, LANES, dtype=I32),
            shaped(rows, 2 * LANES, dtype=BF16),
            shaped(blocks, dy_high, LANES),
        ),
        tuple(in_hbm(v) for v in (covariates, outcome, predictor, firm, dy)),
        scratch=(
            pltpu.VMEM((rows, width), F32),
            pltpu.VMEM((lines, LANES), F32),
            pltpu.VMEM((lines, LANES), F32),
            pltpu.VMEM((lines, LANES), I32),
            pltpu.SemaphoreType.DMA((4 + count,)),
        ),
        flops=wide * (dy_half + 2 * FIRM_DEV),
        in_specs=[HBM] * 5,
    )
    got = to_core(send)
    (keep,) = call(
        functools.partial(sums_kernel, blocks, dy_width),
        (shaped(blocks, dy_high, LANES),),
        (pairs, z1, weight, dy),
        flops=wide * dy_half,
    )
    mine = total_of(across(keep + got))
    (means,) = call(
        functools.partial(means_kernel, dy_width, share), (shaped(blocks, dy_high, LANES),), (mine, to_half(mine, opposite))
    )
    means = across(means)
    other = to_core(means)
    x1, z1 = call(
        functools.partial(gather_kernel, blocks, dy_width),
        (shaped(rows, width), shaped(lines, LANES)),
        (x1, z1, means, dy),
        flops=wide * dy_half,
    )
    x2, z2, pairs, send = call(
        functools.partial(effect_kernel, blocks, dy_width, pd_width),
        (
            shaped(rows, width),
            shaped(lines, LANES),
            shaped(rows, 2 * LANES, dtype=BF16),
            shaped(blocks, pd_high, LANES),
        ),
        (x1, z1, other, dy, weight, owner, local),
        flops=wide * (dy_half + pd_half),
    )
    got = to_core(send)
    keep, gram = call(
        functools.partial(gram_kernel, blocks, pd_width, share),
        (shaped(blocks, pd_high, LANES), shaped(blocks, gram_high, LANES)),
        (x2, z2, pairs, weight, owner, local),
        scratch=(pltpu.VMEM((rows, 2 * LANES), BF16),),
        flops=wide * (pd_half + 2 * LANES),
    )
    mine = total_of(across(jnp.concatenate([keep + got, gram], axis=1)))
    means, gram = call(
        functools.partial(means_kernel, pd_width, share),
        (shaped(blocks, pd_high, LANES), shaped(rounded(share + 1), LANES)),
        (mine, to_half(mine, crossed)),
    )
    means = across(means)
    other = to_core(means)
    x3, z3, less = call(
        functools.partial(own_kernel, blocks, pd_width, share),
        (shaped(rows, width), shaped(lines, LANES), shaped(rounded(share + 1), LANES)),
        (x2, z2, means, owner, local),
        flops=wide * pd_half,
    )
    x3, z3, gram, rhs = call(
        functools.partial(last_kernel, blocks, pd_width, share, total_rows),
        (shaped(rows, width), shaped(lines, LANES), shaped(share, LANES), shaped(1, share)),
        (x3, z3, other, less, gram, owner, local),
        scratch=(
            pltpu.VMEM((rows, width), F32),
            pltpu.VMEM((lines, LANES), F32),
            pltpu.VMEM((share, LANES), F32),
            pltpu.VMEM((1, share), F32),
            pltpu.SemaphoreType.DMA((3 + count,)),
        ),
        flops=wide * pd_half,
        out_specs=[HBM] * 4,
    )
    return x3, z3.reshape(rows), gram, rhs.reshape(share)


def solution(mesh):
    in_specs = (
        P("rows", None),
        P("rows"),
        P("rows"),
        P("rows"),
        P("rows"),
        P("rows", None),
        P("rows"),
    )
    out_specs = (P("rows", None), P("rows"), P("rows", None), P("rows"))
    return jax.shard_map(shards, mesh=mesh, in_specs=in_specs, out_specs=out_specs, check_vma=False)
```
